32 devices in a mesh: snap: 8 (over z, y), rows: 4 (over x, core).
Axes of the slice: x: 2, y: 2, z: 4, core: 2. Of those that a mesh axis runs over, the one named last changes fastest.
Arguments:
- snapshots: bfloat16 [32, 128, 64, 128], P('snap', 'rows'), may hold values from -6 to 6
- cotangent: bfloat16 [32, 128, 64, 128], P('snap', 'rows'), may hold values from -6 to 6
- lengths: int32 [8], P('snap'), may hold values from 1 to 4, as said below
- slot_mask: int32 [32], P('snap'), may hold values from 0 to 1, as said below
- encoder_kernel: float32 [5, 5, 64, 128], replicated, may hold values from -0.15625 to 0.15625
- decoder_kernel: float32 [5, 5, 128, 64], replicated, may hold values from -0.21875 to 0.21875
- biases: float32 [192], replicated, may hold values from -1.5 to 1.5
- encoder_mom: float32 [5, 5, 64, 128], replicated, may hold values from -32 to 32
- decoder_mom: float32 [5, 5, 128, 64], replicated, may hold values from -16 to 16
- bias_mom: float32 [192], replicated, may hold values from -64 to 64
- encoder_ema: float32 [5, 5, 64, 128], replicated, may hold values from -0.15625 to 0.15625
- decoder_ema: float32 [5, 5, 128, 64], replicated, may hold values from -0.21875 to 0.21875
- bias_ema: float32 [192], replicated, may hold values from -1.5 to 1.5
Outputs:
- output: bfloat16 [32, 128, 64, 128], P('snap', 'rows')
- input_grad: bfloat16 [32, 128, 64, 128], P('snap', 'rows')
- encoder_grad: float32 [5, 5, 64, 128], replicated
- decoder_grad: float32 [5, 5, 128, 64], replicated
- bias_grad: float32 [192], replicated
- encoder_mom_new: float32 [5, 5, 64, 128], replicated
- decoder_mom_new: float32 [5, 5, 128, 64], replicated
- bias_mom_new: float32 [192], replicated
- encoder_ema_new: float32 [5, 5, 64, 128], replicated
- decoder_ema_new: float32 [5, 5, 128, 64], replicated
- bias_ema_new: float32 [192], replicated
- encoder_new: float32 [5, 5, 64, 128], replicated
- decoder_new: float32 [5, 5, 128, 64], replicated
- bias_new: float32 [192], replicated
- encoder_copy: bfloat16 [5, 5, 64, 128], replicated
- decoder_copy: bfloat16 [5, 5, 128, 64], replicated
- bias_copy: bfloat16 [192], replicated
The draws below stay inside these ranges and needn't reach their ends.
Inputs may be any that keep to these rules, and one draw needn't show every extreme that they name: `slot_mask`: the first slot of every window is valid. `lengths`: every fourth window, starting with the first, is full.
All inputs are finite; a program needn't handle non-finite values.
Results may differ from the reference program's by a relative error of at most 0.0075.
Values may be sent and summed in bfloat16 or wider, within the bound.
No kernel may reach another device: no remote copies, remote signals or barrier semaphores. Data moves between devices by JAX's collectives and lax.ppermute only.
A program may use at most 128 MiB of HBM per device.

```python
import jax
import jax.numpy as jnp
from jax import lax

H = 128
W = 128
C = 64
K = 128
WIN = 4
SLOTS = 32
WINDOWS = 8


def draw_lengths(key, part):
    key = jax.random.fold_in(key, 1)
    places = jnp.arange(WINDOWS, dtype=jnp.int32)
    drawn = jax.random.randint(key, (WINDOWS,), 1, WIN + 1)
    rising = 1 + (WIN - 1) * places // (2 * WINDOWS)
    result = jnp.maximum(drawn, rising)
    result = jnp.where(places % 4 == 0, WIN, result)
    return result.astype(jnp.int32)


def draw_slot_mask(key, part):
    key = jax.random.fold_in(key, 2)
    places = jnp.arange(SLOTS, dtype=jnp.int32)
    rolled = jax.random.randint(key, (SLOTS,), 0, 12)
    bound = 3 + 8 * places // SLOTS
    result = (rolled < bound) | (places % WIN == 0)
    return result.astype(jnp.int32)


def steps_of(key, extent, shards, least, high):
    loudness, own = 1.0, jax.random.fold_in(key, 6)
    for dim, parts in shards:
        draws = jnp.exp(jax.random.uniform(jax.random.fold_in(own, dim), (parts,), jnp.float32, least / len(shards), high / len(shards)))
        loudness = loudness * jnp.repeat(draws, extent[dim] // parts).reshape([-1 if axis == dim else 1 for axis in range(len(extent))])
    return loudness


def gaussian(own_key, extent, width, reach, cuts=(), kind=jnp.bfloat16):
    values = width * jax.random.normal(own_key, extent, jnp.float32)
    if cuts:
        values = values * steps_of(own_key, extent, cuts, -0.22, 0.18)
    return jnp.clip(values, -reach, reach).astype(kind)


def setup_inputs(seed: int = 0) -> dict:
    seeds = jax.random.split(jax.random.key(seed), 14)
    snapshots = gaussian(seeds[0], (SLOTS, H, C, W), 1.0, 6.0, ((0, 8), (1, 4)))
    cotangent = gaussian(seeds[1], (SLOTS, H, C, W), 1.0, 6.0, ((0, 8), (1, 4)))
    lengths = draw_lengths(jax.random.fold_in(seeds[13], 71), 0)
    slot_mask = draw_slot_mask(jax.random.fold_in(seeds[13], 71), 0)
    encoder_kernel = gaussian(seeds[4], (5, 5, C, K), (25 * C) ** -0.5, 0.15625, (), jnp.float32)
    decoder_kernel = gaussian(seeds[5], (5, 5, K, C), (25 * K // 4) ** -0.5, 0.21875, (), jnp.float32)
    biases = gaussian(seeds[6], (K + C,), 0.3, 1.5, (), jnp.float32)
    encoder_mom = gaussian(seeds[7], (5, 5, C, K), (20.0 / (SLOTS // 2) ** 0.5), 32.0, (), jnp.float32)
    decoder_mom = gaussian(seeds[8], (5, 5, K, C), (12.0 / (SLOTS // 2) ** 0.5), 16.0, (), jnp.float32)
    bias_mom = gaussian(seeds[9], (K + C,), (40.0 / (SLOTS // 2) ** 0.5), 64.0, (), jnp.float32)
    encoder_ema = gaussian(seeds[10], (5, 5, C, K), (25 * C) ** -0.5, 0.15625, (), jnp.float32)
    decoder_ema = gaussian(seeds[11], (5, 5, K, C), (25 * K // 4) ** -0.5, 0.21875, (), jnp.float32)
    bias_ema = gaussian(seeds[12], (K + C,), 0.3, 1.5, (), jnp.float32)
    return {"snapshots": snapshots, "cotangent": cotangent, "lengths": lengths, "slot_mask": slot_mask, "encoder_kernel": encoder_kernel, "decoder_kernel": decoder_kernel, "biases": biases, "encoder_mom": encoder_mom, "decoder_mom": decoder_mom, "bias_mom": bias_mom, "encoder_ema": encoder_ema, "decoder_ema": decoder_ema, "bias_ema": bias_ema}


MOMENTUM = 0.5
EMA_DECAY = 0.5
LEARN_RATE = 0.01
PRECISE = lax.Precision.HIGHEST
CONV_DIMS = ('NHCW', 'HWIO', 'NHCW')

@jax.custom_vjp
def low(v):
    return lax.optimization_barrier(v.astype(jnp.bfloat16)).astype(jnp.float32)

@jax.custom_vjp
def low_back(v):
    return v

def low_keep(v):
    return (low(v), None)

def low_pass(kept, grad):
    return (grad,)

def back_keep(v):
    return (v, None)

def back_low(kept, grad):
    return (low(grad),)
low.defvjp(low_keep, low_pass)
low_back.defvjp(back_keep, back_low)

def encode(images, kernel, bias_part):
    summed = lax.conv_general_dilated(images, kernel, (2, 2), ((2, 2), (2, 2)), dimension_numbers=CONV_DIMS, precision=PRECISE)
    return summed + bias_part[None, None, :, None]

def decode(latent, kernel, bias_part):
    summed = lax.conv_general_dilated(latent, kernel, (1, 1), ((2, 3), (2, 3)), lhs_dilation=(2, 2), dimension_numbers=CONV_DIMS, precision=PRECISE)
    return summed + bias_part[None, None, :, None]

def forward(images, encoder_kernel, decoder_kernel, biases):
    latent_ch = encoder_kernel.shape[3]
    pre_enc = low_back(encode(images, low(encoder_kernel), biases[:latent_ch]))
    latent = low(jax.nn.elu(pre_enc))
    pre_dec = low_back(decode(latent, low(decoder_kernel), biases[latent_ch:]))
    return jax.nn.elu(pre_dec)

def advance(grad, weight, moment, average):
    moment_new = MOMENTUM * moment + grad
    weight_new = weight - LEARN_RATE * (grad + MOMENTUM * moment_new)
    average_new = EMA_DECAY * average + (1.0 - EMA_DECAY) * weight_new
    return (moment_new, average_new, weight_new)

def reference(snapshots, cotangent, lengths, slot_mask, encoder_kernel, decoder_kernel, biases, encoder_mom, decoder_mom, bias_mom, encoder_ema, decoder_ema, bias_ema):
    window_span = slot_mask.shape[0] // lengths.shape[0]
    position = jnp.arange(slot_mask.shape[0], dtype=jnp.int32) % window_span
    valid = ((position < jnp.repeat(lengths, window_span)) & (slot_mask > 0)).astype(jnp.float32)
    live_total = jnp.sum(valid)
    slot_scale = valid / live_total
    groups = snapshots.shape[0] // WIN

    def regroup(array):
        return array.reshape((groups, WIN) + array.shape[1:])

    def accumulate(totals, group_block):
        images, back_grad, group_scale = group_block
        result, pullback = jax.vjp(forward, images.astype(jnp.float32), encoder_kernel, decoder_kernel, biases)
        seed_grad = back_grad.astype(jnp.float32) * group_scale[:, None, None, None]
        image_grad, enc_part, dec_part, bias_part = pullback(seed_grad)
        totals = (totals[0] + enc_part, totals[1] + dec_part, totals[2] + bias_part)
        return (totals, (result.astype(jnp.bfloat16), image_grad.astype(jnp.bfloat16)))
    start = (jnp.zeros(encoder_kernel.shape, jnp.float32), jnp.zeros(decoder_kernel.shape, jnp.float32), jnp.zeros(biases.shape, jnp.float32))
    sums, stacked = lax.scan(accumulate, start, (regroup(snapshots), regroup(cotangent), regroup(slot_scale)))
    encoder_grad, decoder_grad, bias_grad = sums
    output = stacked[0].reshape(snapshots.shape)
    input_grad = stacked[1].reshape(snapshots.shape)
    enc_mom, enc_ema, enc_new = advance(encoder_grad, encoder_kernel, encoder_mom, encoder_ema)
    dec_mom, dec_ema, dec_new = advance(decoder_grad, decoder_kernel, decoder_mom, decoder_ema)
    bia_mom, bia_ema, bia_new = advance(bias_grad, biases, bias_mom, bias_ema)
    return (output, input_grad, encoder_grad, decoder_grad, bias_grad, enc_mom, dec_mom, bia_mom, enc_ema, dec_ema, bia_ema, enc_new, dec_new, bia_new, enc_new.astype(jnp.bfloat16), dec_new.astype(jnp.bfloat16), bia_new.astype(jnp.bfloat16))
```

```python
import functools

import jax
import jax.numpy as jnp
from jax import lax
from jax.experimental import pallas as pl
from jax.experimental.pallas import tpu as pltpu
from jax.sharding import Mesh, PartitionSpec as P

MOMENTUM = 0.5
EMA_DECAY = 0.5
LEARN_RATE = 0.01
F32, BF16 = jnp.float32, jnp.bfloat16
XU, XD, CU, CD = 8, 7, 4, 3
NT = (((1,), (1,)), ((), ()))
KERNEL_ROWS = 1600
HALF_ROWS = 1792
BIAS_ROW, COUNT_ROW = 1600, 1601


def dot(a, b):
    return jnp.dot(a, b, preferred_element_type=F32)


def chunked(lo, hi, size, step):
    whole = (hi - lo) // size
    if whole == 1:
        step(lo, size)
    elif whole:
        pl.loop(0, whole)(lambda n: step(lo + n * size, size))
    rest = (hi - lo) % size
    if rest:
        step(hi - rest, rest)


def split_matrix():
    row = lax.broadcasted_iota(jnp.int32, (256, 256), 0)
    col = lax.broadcasted_iota(jnp.int32, (256, 256), 1)
    want = (col // 64 % 2) * 128 + (col % 64) * 2 + col // 128
    return jnp.where(row == want, 1.0, 0.0).astype(BF16)


def merge_matrix():
    row = lax.broadcasted_iota(jnp.int32, (256, 256), 0)
    col = lax.broadcasted_iota(jnp.int32, (256, 256), 1)
    want = (row // 64 % 2) * 128 + (row % 64) * 2 + row // 128
    return jnp.where(col == want, 1.0, 0.0).astype(BF16)


def column_before(v):
    return shifted(v, 1, 0)


def column_after(v):
    return shifted(v, 127, 63)


def shifted(v, by, edge):
    parts = []
    for h in range(v.shape[1] // 128):
        part = v[:, h * 128 : (h + 1) * 128]
        lane = lax.broadcasted_iota(jnp.int32, part.shape, 1) % 64
        parts.append(jnp.where(lane == edge, 0.0, pltpu.roll(part, by, axis=1)))
    return parts[0] if len(parts) == 1 else jnp.concatenate(parts, axis=1)


def split_rows(ref, rows, split):
    pieces = [
        jnp.concatenate([ref[2 * h, r], ref[2 * h + 1, r]], axis=1) for r in rows for h in range(2)
    ]
    y = dot(jnp.concatenate(pieces, axis=0), split)
    out = []
    for n in range(len(rows)):
        a, b = y[n * 128 : n * 128 + 64], y[n * 128 + 64 : n * 128 + 128]
        out.append([jnp.concatenate([a[:, p * 128 : p * 128 + 128], b[:, p * 128 : p * 128 + 128]], axis=1) for p in range(2)])
    return out


def merge_rows(v, merge):
    pieces = [
        jnp.concatenate([v[rho * 128 : rho * 128 + 64, h * 128 : h * 128 + 128], v[rho * 128 + 64 : rho * 128 + 128, h * 128 : h * 128 + 128]], axis=1)
        for rho in range(2)
        for h in range(2)
    ]
    y = dot(jnp.concatenate(pieces, axis=0), merge).astype(BF16)
    return [
        [y[(rho * 2 + n // 2) * 64 : (rho * 2 + n // 2) * 64 + 64, (n % 2) * 128 : (n % 2) * 128 + 128] for n in range(4)]
        for rho in range(2)
    ]


def up_weights(dest, taps, sign):
    for rho in range(2):
        for pi in range(2):
            for di in range(-1, 2):
                for dj in range(-1, 2):
                    a, b = 2 + sign * (2 * di - rho), 2 + sign * (2 * dj - pi)
                    inside = 0 <= a <= 4 and 0 <= b <= 4
                    block = taps[a, b].astype(BF16) if inside else jnp.zeros((64, 128), BF16)
                    r, c = (rho * 2 + pi) * 64, ((di + 1) * 3 + dj + 1) * 128
                    dest[r : r + 64, c : c + 128] = block


def lane_sums(v):
    ones = jnp.ones((8, v.shape[1]), F32)
    return lax.dot_general(ones, v, NT, precision=lax.Precision.HIGHEST, preferred_element_type=F32)[:1]


def step_kernel(
    R, U, x_hbm, c_hbm, hu, hd, we, wdt, bias, lens, mask,
    out, e_out, pay,
    xv, cv, xb, l3, slope, d5, we2, wd2, wb, dsum, esum, acc0, acc1, split_ref, merge_ref, sems,
):
    I = R // 2
    row_at = lax.axis_index("x") * 2 + lax.axis_index("core")
    row_last = lax.axis_size("x") * 2 - 1
    core = lax.axis_index("core")
    first, last = row_at == 0, row_at == row_last
    copies = [
        pltpu.make_async_copy(x_hbm, xv.at[:, XU : XU + R], sems.at[0]),
        pltpu.make_async_copy(hu.at[:, :XU], xv.at[:, :XU], sems.at[1]),
        pltpu.make_async_copy(hd.at[:, :XD], xv.at[:, XU + R : XU + R + XD], sems.at[2]),
        pltpu.make_async_copy(c_hbm, cv.at[:, CU : CU + R], sems.at[3]),
        pltpu.make_async_copy(hu.at[:, XU:], cv.at[:, :CU], sems.at[4]),
        pltpu.make_async_copy(hd.at[:, XD:], cv.at[:, CU + R : CU + R + CD], sems.at[5]),
    ]
    for c in copies:
        c.start()
    cv[:, CU + R + CD] = jnp.zeros((4, 64, 128), BF16)
    split_ref[...] = split_matrix()
    merge_ref[...] = merge_matrix()
    we2[...] = we[...].reshape(KERNEL_ROWS, 128).T.astype(BF16)
    wb[...] = jnp.concatenate([wdt[4 - q].reshape(320, 128) for q in range(5)], axis=0).T.astype(BF16)
    up_weights(wd2, wdt, 1)
    dsum[...] = jnp.zeros_like(dsum)
    esum[...] = jnp.zeros_like(esum)
    slot = lax.broadcasted_iota(jnp.int32, (1, 256), 1) // 64
    live_lane = jnp.zeros((1, 256), F32)
    count = jnp.float32(0)
    for n in range(4):
        valid = jnp.where((n < lens[0]) & (mask[n] > 0), 1.0, 0.0)
        count = count + valid
        live_lane = jnp.where(slot == n, valid, live_lane)
    for c in copies[:3]:
        c.wait()

    def columns(t, count):
        for n, (even, odd) in enumerate(split_rows(xv, [t + m for m in range(count)], split_ref[...])):
            for b, v in enumerate([column_before(even), column_before(odd), even, odd, column_after(even)]):
                xb[t + n, b * 64 : b * 64 + 64] = v.astype(BF16)

    chunked(0, XU + R + XD, 2 * U, columns)

    bias_enc = jnp.concatenate([bias[:128]] * 2, axis=1)

    def encode(u, count):
        for n in range(count):
            pre = dot(we2[...], xb[pl.ds(2 * (u + n), 5)].reshape(KERNEL_ROWS, 256)) + bias_enc
            grow = jnp.exp(jnp.minimum(pre, 0.0))
            lat = jnp.maximum(pre, 0.0) + (grow - 1.0)
            if isinstance(u, int):
                if u + n < 3:
                    lat = jnp.where(first, 0.0, lat)
                if u + n >= I + 3:
                    lat = jnp.where(last, 0.0, lat)
                if 2 <= u + n < I + 4:
                    slope[u + n - 2] = grow
            else:
                slope[u + n - 2] = grow
            l3[u + n, :128] = column_before(lat).astype(BF16)
            l3[u + n, 128:256] = lat.astype(BF16)
            l3[u + n, 256:] = column_after(lat).astype(BF16)

    chunked(0, 3, 3, encode)
    chunked(3, I + 3, U, encode)
    chunked(I + 3, I + 6, 3, encode)

    for c in copies[3:]:
        c.wait()
    bias_dec = jnp.concatenate([jnp.concatenate([bias[128:]] * 4, axis=0)] * 2, axis=1)

    def decode(w, count, own):
        for n in range(count):
            pre = dot(wd2[...], l3[pl.ds(w + n, 3)].reshape(9 * 128, 256)) + bias_dec
            grow = jnp.exp(jnp.minimum(pre, 0.0))
            if own:
                value = (jnp.maximum(pre, 0.0) + (grow - 1.0)).astype(BF16)
                for rho, slots in enumerate(merge_rows(value, merge_ref[...])):
                    for s, v in enumerate(slots):
                        out[s, 2 * (w + n - 2) + rho] = v
            total = jnp.zeros((64, 256), F32)
            for rho, halves in enumerate(split_rows(cv, [2 * (w + n), 2 * (w + n) + 1], split_ref[...])):
                even, odd = [
                    (halves[pi] * live_lane * grow[(rho * 2 + pi) * 64 : (rho * 2 + pi) * 64 + 64]).astype(BF16).astype(F32)
                    for pi in range(2)
                ]
                total = total + even + odd
                for b, v in enumerate([column_after(even), odd, even, column_before(odd), column_before(even)]):
                    d5[2 * (w + n) + rho, b * 64 : b * 64 + 64] = v.astype(BF16)
            if own:
                dsum[...] += total

    chunked(0, 2, 2, functools.partial(decode, own=False))
    chunked(2, I + 2, U, functools.partial(decode, own=True))
    chunked(I + 2, I + 4, 2, functools.partial(decode, own=False))

    def back(e, count, own):
        for n in range(count):
            v = (dot(wb[...], d5[pl.ds(2 * (e + n), 5)].reshape(KERNEL_ROWS, 256)) * slope[e + n]).astype(BF16)
            if own:
                esum[...] += v.astype(F32)
            elif e == 0:
                v = jnp.where(first, jnp.zeros_like(v), v)
            else:
                v = jnp.where(last, jnp.zeros_like(v), v)
            e_out[e + n] = v

    def kernel_grad(cols, cols_at, latent, latent_at, half, taps):
        def add(s, count):
            rows = [s + n for n in range(count)]
            lhs = jnp.concatenate([cols[cols_at + 2 * r] for r in rows], axis=1)
            rhs = jnp.concatenate([jnp.concatenate([latent(latent_at + r + d) for d in range(3)], axis=0) for r in rows], axis=1)
            even = lax.dot_general(lhs, rhs, NT, preferred_element_type=F32)
            lhs = jnp.concatenate([cols[cols_at + 2 * r + 1] for r in rows], axis=1)
            odd = lax.dot_general(lhs, rhs[128:], NT, preferred_element_type=F32)
            if isinstance(s, int) and s == 0:
                acc0[...] = even
                acc1[...] = odd
            else:
                acc0[...] += even
                acc1[...] += odd

        size = 2 * U
        add(0, size)
        chunked(size, I, size, add)
        for d in range(3):
            a = taps[0][d]
            pay[half, a * 320 : a * 320 + 320] = acc0[:, d * 128 : d * 128 + 128].astype(BF16)
        for d in range(2):
            a = taps[1][d]
            pay[half, a * 320 : a * 320 + 320] = acc1[:, d * 128 : d * 128 + 128].astype(BF16)

    enc_half, dec_half = core, 1 - core
    kernel_grad(d5, CU, lambda u: l3[u, 128:256], 2, dec_half, ((0, 2, 4), (1, 3)))
    chunked(0, 1, 1, functools.partial(back, own=False))
    chunked(1, I + 1, U, functools.partial(back, own=True))
    chunked(I + 1, I + 2, 1, functools.partial(back, own=False))
    kernel_grad(xb, XU, lambda e: e_out[e], 0, enc_half, ((4, 2, 0), (3, 1)))

    count = jnp.where(row_at == 0, count, 0.0)
    count_row = jnp.broadcast_to(count, (1, 128))
    dec_row = jnp.concatenate([lane_sums(dsum[...]), jnp.zeros((1, 64), F32)], axis=1)
    for half, row in ((enc_half, lane_sums(esum[...])), (dec_half, dec_row)):
        tail = jnp.concatenate([row, count_row, jnp.zeros((14, 128), F32)], axis=0)
        pay[half, KERNEL_ROWS : KERNEL_ROWS + 16] = tail.astype(BF16)
        pay[half, KERNEL_ROWS + 16 :] = jnp.zeros((HALF_ROWS - KERNEL_ROWS - 16, 128), BF16)


def input_grad_kernel(R, U, e_ref, we, tail, ig, e3, we3, merge_ref):
    I = R // 2
    merge_ref[...] = merge_matrix()
    up_weights(we3, we, -1)
    scale = 1.0 / tail[...].astype(F32)[1:2]
    scale = jnp.concatenate([scale] * 2, axis=1)

    def widen(e, count):
        for n in range(count):
            v = e_ref[e + n].astype(F32)
            e3[e + n, :128] = column_before(v).astype(BF16)
            e3[e + n, 128:256] = e_ref[e + n]
            e3[e + n, 256:] = column_after(v).astype(BF16)

    chunked(0, I + 2, U, widen)

    def scatter(s, count):
        for n in range(count):
            v = dot(we3[...], e3[pl.ds(s + n, 3)].reshape(9 * 128, 256)) * scale
            for rho, slots in enumerate(merge_rows(v.astype(BF16), merge_ref[...])):
                for k, piece in enumerate(slots):
                    ig[k, 2 * (s + n) + rho] = piece

    chunked(0, I, U, scatter)


def update_kernel(mine, other, tail, *refs):
    core = lax.axis_index("core")
    scale = 1.0 / tail[...].astype(F32)[1:2]
    a, b = mine[...].astype(F32), other[...].astype(F32)
    own_first = core == 0
    for n in range(2):
        grad = jnp.where(own_first, a if n == 0 else b, b if n == 0 else a) * scale
        weight, moment, average = [r[...] for r in refs[3 * n : 3 * n + 3]]
        grad_out, mom_out, ema_out, new_out, copy_out = refs[6 + 5 * n : 11 + 5 * n]
        mom = MOMENTUM * moment + grad
        new = weight - LEARN_RATE * (grad + MOMENTUM * mom)
        grad_out[...] = grad
        mom_out[...] = mom
        ema_out[...] = EMA_DECAY * average + (1.0 - EMA_DECAY) * new
        new_out[...] = new
        copy_out[...] = new.astype(BF16)


def advance(grad, weight, moment, average):
    moment_new = MOMENTUM * moment + grad
    weight_new = weight - LEARN_RATE * (grad + MOMENTUM * moment_new)
    average_new = EMA_DECAY * average + (1.0 - EMA_DECAY) * weight_new
    return (moment_new, average_new, weight_new)


def whole(shape, memory_space=pltpu.VMEM):
    return pl.BlockSpec(memory_space=memory_space)


def on_device(
    snapshots, cotangent, lengths, slot_mask, encoder_kernel, decoder_kernel, biases,
    encoder_mom, decoder_mom, bias_mom, encoder_ema, decoder_ema, bias_ema,
):
    slots, R, C, W = snapshots.shape
    I, U = R // 2, 4
    nx = lax.axis_size("x")
    peers = lax.axis_size("snap") * nx
    flat = ("x", "core")
    count = 2 * nx
    down = [(n, n + 1) for n in range(count - 1)]
    up = [(n + 1, n) for n in range(count - 1)]
    hu = lax.ppermute(jnp.concatenate([snapshots[:, R - XU :], cotangent[:, R - CU :]], axis=1), flat, down)
    hd = lax.ppermute(jnp.concatenate([snapshots[:, :XD], cotangent[:, :CD]], axis=1), flat, up)
    bias_wide = jnp.broadcast_to(biases[:, None], (192, 128))
    decoder_t = jnp.swapaxes(decoder_kernel, 2, 3)
    vmem, smem, anyspace = (pl.BlockSpec(memory_space=m) for m in (pltpu.VMEM, pltpu.SMEM, pl.ANY))
    params = pltpu.CompilerParams(vmem_limit_bytes=60 * 2**20)
    field = jax.ShapeDtypeStruct(snapshots.shape, BF16)
    output, e_rows, pay = pl.pallas_call(
        functools.partial(step_kernel, R, U),
        out_shape=[field, jax.ShapeDtypeStruct((I + 2, 128, 256), BF16), jax.ShapeDtypeStruct((2, HALF_ROWS, 128), BF16)],
        in_specs=[anyspace] * 4 + [vmem] * 3 + [smem] * 2,
        out_specs=[vmem] * 3,
        scratch_shapes=[
            pltpu.VMEM((4, XU + R + 8, 64, 128), BF16),
            pltpu.VMEM((4, CU + R + 4, 64, 128), BF16),
            pltpu.VMEM((XU + R + 8, 320, 256), BF16),
            pltpu.VMEM((I + 6, 384, 256), BF16),
            pltpu.VMEM((I + 2, 128, 256), F32),
            pltpu.VMEM((R + 8, 320, 256), BF16),
            pltpu.VMEM((128, KERNEL_ROWS), BF16),
            pltpu.VMEM((256, 1152), BF16),
            pltpu.VMEM((128, KERNEL_ROWS), BF16),
            pltpu.VMEM((64, 256), F32),
            pltpu.VMEM((128, 256), F32),
            pltpu.VMEM((320, 384), F32),
            pltpu.VMEM((320, 256), F32),
            pltpu.VMEM((256, 256), BF16),
            pltpu.VMEM((256, 256), BF16),
            pltpu.SemaphoreType.DMA((6,)),
        ],
        compiler_params=params,
        name="step",
    )(snapshots, cotangent, hu, hd, encoder_kernel, decoder_t, bias_wide, lengths, slot_mask)

    swap = [(0, 1), (1, 0)]
    recv = lax.ppermute(pay[1], "core", swap)
    part = (pay[0].astype(F32) + recv.astype(F32)).astype(BF16).reshape(peers, HALF_ROWS // peers, 128)
    parts = lax.all_to_all(part, ("snap", "x"), 0, 0, tiled=True)
    total = jnp.sum(parts.astype(F32), axis=0).astype(BF16)
    mine = lax.all_to_all(jnp.broadcast_to(total[None], part.shape), ("snap", "x"), 0, 0, tiled=True)
    mine = mine.reshape(HALF_ROWS, 128)
    other = lax.ppermute(mine, "core", swap)
    tail = mine[KERNEL_ROWS : KERNEL_ROWS + 16]
    input_grad = pl.pallas_call(
        functools.partial(input_grad_kernel, R, U),
        out_shape=field,
        in_specs=[vmem] * 3,
        out_specs=vmem,
        scratch_shapes=[
            pltpu.VMEM((I + 2, 384, 256), BF16),
            pltpu.VMEM((256, 1152), BF16),
            pltpu.VMEM((256, 256), BF16),
        ],
        compiler_params=params,
        cost_estimate=pl.CostEstimate(flops=2 * 4096 * 204800, bytes_accessed=4 << 20, transcendentals=0),
        name="input_grad",
    )(e_rows, encoder_kernel, tail)

    def rows(v):
        return v.reshape(KERNEL_ROWS, 128)

    def trows(v):
        return jnp.swapaxes(v, 2, 3).reshape(KERNEL_ROWS, 128)

    block = pl.BlockSpec((320, 128), lambda a: (a, 0))
    fixed = pl.BlockSpec((16, 128), lambda a: (0, 0))
    shape32 = jax.ShapeDtypeStruct((KERNEL_ROWS, 128), F32)
    shape16 = jax.ShapeDtypeStruct((KERNEL_ROWS, 128), BF16)
    results = pl.pallas_call(
        update_kernel,
        grid=(5,),
        out_shape=[shape32, shape32, shape32, shape32, shape16] * 2,
        in_specs=[block, block, fixed] + [block] * 6,
        out_specs=[block] * 10,
        compiler_params=params,
        name="update",
    )(
        mine, other, tail,
        rows(encoder_kernel), rows(encoder_mom), rows(encoder_ema),
        trows(decoder_kernel), trows(decoder_mom), trows(decoder_ema),
    )
    enc_grad, enc_mom, enc_ema, enc_new, enc_copy = [v.reshape(encoder_kernel.shape) for v in results[:5]]
    dec_grad, dec_mom, dec_ema, dec_new, dec_copy = [jnp.swapaxes(v.reshape(decoder_t.shape), 2, 3) for v in results[5:]]
    own_first = lax.axis_index("core") == 0
    mine_row, other_row = mine[BIAS_ROW].astype(F32), other[BIAS_ROW].astype(F32)
    enc_row, dec_row = jnp.where(own_first, mine_row, other_row), jnp.where(own_first, other_row, mine_row)
    bias_grad = jnp.concatenate([enc_row, dec_row[:C]]) / mine[COUNT_ROW, 0].astype(F32)
    bia_mom, bia_ema, bia_new = advance(bias_grad, biases, bias_mom, bias_ema)
    return (
        output, input_grad, enc_grad, dec_grad, bias_grad, enc_mom, dec_mom, bia_mom,
        enc_ema, dec_ema, bia_ema, enc_new, dec_new, bia_new, enc_copy, dec_copy, bia_new.astype(BF16),
    )


def solution(mesh):
    snap, rows = mesh.devices.shape
    split = Mesh(mesh.devices.reshape(snap, rows // 2, 2), ("snap", "x", "core"))
    field = P("snap", ("x", "core"), None, None)
    return jax.shard_map(
        on_device,
        mesh=split,
        in_specs=(field, field, P("snap"), P("snap")) + (P(),) * 9,
        out_specs=(field, field) + (P(),) * 15,
        check_vma=False,
    )
```

```python
import functools

import jax
import jax.numpy as jnp
from jax import lax
from jax.experimental import pallas as pl
from jax.experimental.pallas import tpu as pltpu
from jax.sharding import Mesh, PartitionSpec as P

MOMENTUM = 0.5
EMA_DECAY = 0.5
LEARN_RATE = 0.01
F32, BF16 = jnp.float32, jnp.bfloat16
XH, CH = 8, 4
XU, XD = 8, 7
NT = (((1,), (1,)), ((), ()))
KERNEL_ROWS = 1600
INNER_MB, OUTER_MB, FIELD_MB, UPDATE_MB = 16, 16, 12, 12


GROUPS = KERNEL_ROWS // 16


def chunk_groups(peers):
    return -(-(GROUPS + peers // 2) // peers)


def headless(peers, half):
    n = max(0, peers - (peers * chunk_groups(peers) - GROUPS))
    return peers - n * (1 + half), peers - n * half


def chunk_runs(peers, half):
    size, at, runs = chunk_groups(peers), 0, []
    lo, hi = headless(peers, half)
    for p in range(peers):
        first = 0 if lo <= p < hi else 1
        count = min(size - first, GROUPS - at)
        runs.append((first * 16, at * 16, (at + count) * 16))
        at += count
    assert at == GROUPS
    return runs


def dot(a, b):
    return jnp.dot(a, b, preferred_element_type=F32)


def chunked(lo, hi, size, step):
    whole = (hi - lo) // size
    if whole == 1:
        step(lo, size)
    elif whole:
        pl.loop(0, whole)(lambda n: step(lo + n * size, size))
    rest = (hi - lo) % size
    if rest:
        step(hi - rest, rest)


def split_matrix():
    row = lax.broadcasted_iota(jnp.int32, (256, 256), 0)
    col = lax.broadcasted_iota(jnp.int32, (256, 256), 1)
    want = (col // 64 % 2) * 128 + (col % 64) * 2 + col // 128
    return jnp.where(row == want, 1.0, 0.0).astype(BF16)


def merge_matrix():
    row = lax.broadcasted_iota(jnp.int32, (256, 256), 0)
    col = lax.broadcasted_iota(jnp.int32, (256, 256), 1)
    want = (row // 64 % 2) * 128 + (row % 64) * 2 + row // 128
    return jnp.where(col == want, 1.0, 0.0).astype(BF16)


def column_before(v):
    return shifted(v, 1, 0)


def column_after(v):
    return shifted(v, 127, 63)


def shifted(v, by, edge):
    parts = []
    for h in range(v.shape[1] // 128):
        part = v[:, h * 128 : (h + 1) * 128]
        lane = lax.broadcasted_iota(jnp.int32, part.shape, 1) % 64
        parts.append(jnp.where(lane == edge, jnp.zeros_like(part), pltpu.roll(part, by, axis=1)))
    return parts[0] if len(parts) == 1 else jnp.concatenate(parts, axis=1)


def split_rows(rows, split):
    pieces = [jnp.concatenate([row(2 * h), row(2 * h + 1)], axis=1) for row in rows for h in range(2)]
    y = dot(jnp.concatenate(pieces, axis=0), split)
    out = []
    for n in range(len(rows)):
        a, b = y[n * 128 : n * 128 + 64], y[n * 128 + 64 : n * 128 + 128]
        out.append([jnp.concatenate([a[:, p * 128 : p * 128 + 128], b[:, p * 128 : p * 128 + 128]], axis=1) for p in range(2)])
    return out


def merge_rows(v, merge):
    pieces = [
        jnp.concatenate([v[rho * 128 : rho * 128 + 64, h * 128 : h * 128 + 128], v[rho * 128 + 64 : rho * 128 + 128, h * 128 : h * 128 + 128]], axis=1)
        for rho in range(2)
        for h in range(2)
    ]
    y = dot(jnp.concatenate(pieces, axis=0), merge).astype(BF16)
    return [
        [y[(rho * 2 + n // 2) * 64 : (rho * 2 + n // 2) * 64 + 64, (n % 2) * 128 : (n % 2) * 128 + 128] for n in range(4)]
        for rho in range(2)
    ]


def up_weights(dest, taps, sign):
    for rho in range(2):
        for pi in range(2):
            for di in range(-1, 2):
                for dj in range(-1, 2):
                    a, b = 2 + sign * (2 * di - rho), 2 + sign * (2 * dj - pi)
                    inside = 0 <= a <= 4 and 0 <= b <= 4
                    block = taps[a, b].astype(BF16) if inside else jnp.zeros((64, 128), BF16)
                    r, c = (rho * 2 + pi) * 64, ((di + 1) * 3 + dj + 1) * 128
                    dest[r : r + 64, c : c + 128] = block


def lane_sums(v):
    ones = jnp.ones((8, v.shape[1]), F32)
    return lax.dot_general(ones, v, NT, precision=lax.Precision.HIGHEST, preferred_element_type=F32)[:1]


def store_columns(xb, at, halves):
    even, odd = [v.astype(BF16) for v in halves]
    for b, v in enumerate([column_before(even), column_before(odd), even, odd, column_after(even)]):
        xb[at, b * 64 : b * 64 + 64] = v


def store_split(seeds, at, pair, live_lane):
    for rho, halves in enumerate(pair):
        for pi, v in enumerate(halves):
            row = (rho * 2 + pi) * 64
            seeds[at, row : row + 64] = (v * live_lane).astype(BF16)


def up(weights, rows, at):
    even = dot(weights[:128], rows[pl.ds(at, 3)].reshape(9 * 128, 256))
    odd = dot(weights[128:, 384:], rows[pl.ds(at + 1, 2)].reshape(6 * 128, 256))
    return jnp.concatenate([even, odd], axis=0)


def encode_row(u, I, ends, we2, bias, xb, l3, slope):
    pre = dot(we2[...], xb[pl.ds(2 * u, 5)].reshape(KERNEL_ROWS, 256)) + bias
    grow = jnp.exp(jnp.minimum(pre, 0.0))
    lat = jnp.maximum(pre, grow - 1.0)
    if ends is not None:
        if u < 3:
            lat = jnp.where(ends[0], 0.0, lat)
        if u >= I + 3:
            lat = jnp.where(ends[1], 0.0, lat)
    if ends is None or 2 <= u < I + 4:
        slope[u - 2] = grow
    lat = lat.astype(BF16)
    l3[u, :128] = column_before(lat)
    l3[u, 128:256] = lat
    l3[u, 256:] = column_after(lat)


def decode_row(w, own, wd2, bias, seeds, l3, d5, value, dsum):
    pre = up(wd2, l3, w) + bias
    grow = jnp.exp(jnp.minimum(pre, 0.0))
    if own:
        value[w - 2] = jnp.maximum(pre, grow - 1.0).astype(BF16)
    full = seeds[w].astype(F32) * grow
    if own:
        dsum[...] += (full[:64] + full[64:128]) + (full[128:192] + full[192:])
    back = full.astype(BF16)
    for rho in range(2):
        even, odd = [back[(rho * 2 + pi) * 64 : (rho * 2 + pi) * 64 + 64] for pi in range(2)]
        for b, v in enumerate([column_after(even), odd, even, column_before(odd), column_before(even)]):
            d5[2 * w + rho, b * 64 : b * 64 + 64] = v


def live_lanes(lens, mask):
    slot = lax.broadcasted_iota(jnp.int32, (1, 256), 1) // 64
    lanes, count = jnp.zeros((1, 256), F32), jnp.float32(0)
    for n in range(4):
        valid = jnp.where((n < lens[0]) & (mask[n] > 0), 1.0, 0.0)
        count = count + valid
        lanes = jnp.where(slot == n, valid, lanes)
    return lanes, count


def bias_tiles(bias):
    def column(row):
        count = row.shape[1]
        at = lax.broadcasted_iota(jnp.int32, (count, count), 0)
        to = lax.broadcasted_iota(jnp.int32, (count, count), 1)
        return jnp.sum(jnp.where(at == to, jnp.broadcast_to(row, (count, count)), 0.0), axis=1, keepdims=True)

    enc = column(bias[:, :128])
    dec = column(bias[:, 128:])
    return jnp.broadcast_to(enc, (128, 256)), jnp.broadcast_to(jnp.concatenate([dec] * 4, axis=0), (256, 256))


def halo_kernel(R, x_hbm, c_hbm, near, far, sems):
    core = lax.axis_index("core")
    copies = []
    for n, (dest, low) in enumerate(((near, core == 0), (far, core == 1))):
        for m, (src, rows, at) in enumerate(((x_hbm, XH, 0), (c_hbm, CH, XH))):
            start = jnp.where(low, R - rows, 0)
            copies.append(pltpu.make_async_copy(src.at[:, pl.ds(start, rows)], dest.at[:, at : at + rows], sems.at[2 * n + m]))
    for c in copies:
        c.start()
    for c in copies:
        c.wait()


def kernel_grad(rows, cols, cols_at, latent, latent_at):
    rhs = jnp.concatenate(
        [jnp.concatenate([latent(latent_at + s + d) for d in range(3)], axis=0) for s in rows], axis=1
    )
    even, odd = [jnp.concatenate([cols[cols_at + 2 * s + rho] for s in rows], axis=1) for rho in range(2)]
    return (
        lax.dot_general(even, rhs, NT, preferred_element_type=F32),
        lax.dot_general(odd, rhs[128:], NT, preferred_element_type=F32),
    )


def inner_kernel(
    R, U, x_hbm, c_hbm, we_hbm, wdt_hbm, bias, lens, mask,
    xb, l3, slope, d5, value, seeds, dsum, acc0, acc1, we2, wd2, wb, xv, cv, we, wdt, split_ref, sems,
):
    I = R // 2
    parts = 2
    step = R // parts
    x_copies = [
        pltpu.make_async_copy(x_hbm.at[:, n * step : n * step + step], xv.at[:, n * step : n * step + step], sems.at[n])
        for n in range(parts)
    ]
    c_copy = pltpu.make_async_copy(c_hbm, cv, sems.at[parts])
    w_copies = [
        pltpu.make_async_copy(we_hbm, we, sems.at[parts + 1]),
        pltpu.make_async_copy(wdt_hbm, wdt, sems.at[parts + 2]),
    ]
    for c in w_copies[:1] + x_copies + w_copies[1:] + [c_copy]:
        c.start()
    split_ref[...] = split_matrix()
    dsum[...] = jnp.zeros_like(dsum)
    live_lane, _ = live_lanes(lens, mask)
    bias_enc, bias_dec = bias_tiles(bias[...])

    def columns(t, count):
        rows = [lambda s, r=t + m: xv[s, r] for m in range(count)]
        for n, halves in enumerate(split_rows(rows, split_ref[...])):
            store_columns(xb, XU + t + n, halves)

    def cotangent(s, count):
        rows = [lambda k, r=2 * s + m: cv[k, r] for m in range(2 * count)]
        halves = split_rows(rows, split_ref[...])
        for n in range(count):
            store_split(seeds, s + n + 2, halves[2 * n : 2 * n + 2], live_lane)

    def encode(u, count):
        for n in range(count):
            encode_row(u + n, I, None, we2, bias_enc, xb, l3, slope)

    def decode(w, count):
        for n in range(count):
            decode_row(w + n, True, wd2, bias_dec, seeds, l3, d5, value, dsum)

    w_copies[0].wait()
    we2[...] = we[...].reshape(KERNEL_ROWS, 128).T.astype(BF16)
    for n, c in enumerate(x_copies):
        c.wait()
        chunked(n * step, n * step + step, U, columns)
    chunked(4, I + 2, U, encode)
    w_copies[1].wait()
    up_weights(wd2, wdt, 1)
    c_copy.wait()
    chunked(0, I, U, cotangent)
    chunked(4, I, U, decode)
    acc0[...], acc1[...] = kernel_grad(range(2, I - 2), d5, CH, lambda u: l3[u, 128:256], 2)
    wb[...] = jnp.concatenate([wdt[4 - q].reshape(320, 128) for q in range(5)], axis=0).T.astype(BF16)


def outer_kernel(
    R, U, near, far, bias, lens, mask, we2, wd2, wb,
    xb_in, l3_in, slope_in, d5_in, value_in, seeds_in, dsum_in, acc0_in, acc1_in,
    e_out, keep, send, xb, l3, slope, d5, value, seeds, dsum, acc0, acc1,
    e_rows, esum, split_ref, sem,
):
    I = R // 2
    core = lax.axis_index("core")
    row_at = lax.axis_index("x") * 2 + core
    ends = row_at == 0, row_at == lax.axis_size("x") * 2 - 1
    split_ref[...] = split_matrix()
    esum[...] = jnp.zeros_like(esum)
    live_lane, count = live_lanes(lens, mask)
    bias_enc, bias_dec = bias_tiles(bias[...])
    upper = core == 0

    def above(r):
        return lambda s: jnp.where(upper, far[s, r], near[s, r])

    def below(r):
        return lambda s: jnp.where(upper, near[s, r], far[s, r])

    rows = [above(r) for r in range(XU)] + [below(r) for r in range(XD)]
    for n, halves in enumerate(split_rows(rows, split_ref[...])):
        store_columns(xb, n if n < XU else R + n, halves)
    halves = split_rows([above(XH + r) for r in range(CH)] + [below(XH + r) for r in range(CH)], split_ref[...])
    for n, w in enumerate((0, 1, I + 2, I + 3)):
        store_split(seeds, w, halves[2 * n : 2 * n + 2], live_lane)
    for u in list(range(4)) + list(range(I + 2, I + 6)):
        encode_row(u, I, ends, we2, bias_enc, xb, l3, slope)
    for w in list(range(4)) + list(range(I, I + 4)):
        decode_row(w, 2 <= w < I + 2, wd2, bias_dec, seeds, l3, d5, value, dsum)

    def back(e, count, own):
        for n in range(count):
            v = dot(wb[...], d5[pl.ds(2 * (e + n), 5)].reshape(KERNEL_ROWS, 256)) * slope[e + n]
            if own:
                esum[...] += v
            else:
                v = jnp.where(ends[0] if e == 0 else ends[1], 0.0, v)
            e_rows[e + n] = v.astype(BF16)

    chunks, chunk_rows = keep.shape[:2]

    def put(half, even_taps, odd_taps):
        blocks = {a: (acc0, d) for d, a in enumerate(even_taps)} | {a: (acc1, d) for d, a in enumerate(odd_taps)}

        def into(dest):
            for a, (acc, d) in blocks.items():
                block = acc[:, d * 128 : d * 128 + 128].astype(BF16)
                for p, (first, lo, hi) in enumerate(chunk_runs(chunks, half)):
                    lo, hi, start = max(lo, a * 320), min(hi, a * 320 + 320), lo
                    if lo < hi:
                        dest[p, first + lo - start : first + hi - start] = block[lo - a * 320 : hi - a * 320]

        pl.when(core == half)(lambda: into(keep))
        pl.when(core != half)(lambda: into(send))

    even, odd = kernel_grad([0, 1, I - 2, I - 1], d5, CH, lambda u: l3[u, 128:256], 2)
    acc0[...] += even
    acc1[...] += odd
    put(1, (0, 2, 4), (1, 3))
    back(0, 1, False)
    chunked(1, I + 1, U, functools.partial(back, own=True))
    back(I + 1, 1, False)
    e_copy = pltpu.make_async_copy(e_rows, e_out, sem)
    e_copy.start()
    acc0[...], acc1[...] = kernel_grad(range(I), xb, XU, lambda e: e_rows[e], 0)
    put(0, (4, 2, 0), (3, 1))

    count_row = jnp.broadcast_to(jnp.where(row_at == 0, count, 0.0), (1, 128))
    dec_row = jnp.concatenate([lane_sums(dsum[...]), jnp.zeros((1, 64), F32)], axis=1)
    head = jnp.concatenate([count_row, lane_sums(esum[...]), dec_row, jnp.zeros((13, 128), F32)], axis=0).astype(BF16)
    other_head = jnp.concatenate([count_row, jnp.zeros((15, 128), F32)], axis=0).astype(BF16)

    def finish(half, dest):
        for p, (first, lo, hi) in enumerate(chunk_runs(chunks, half)):
            if first:
                dest[p, :16] = other_head if p else head
            end = first + hi - lo
            if end < chunk_rows:
                dest[p, end:] = jnp.zeros((chunk_rows - end, 128), BF16)

    for half in range(2):
        pl.when(core == half)(functools.partial(finish, half, keep))
        pl.when(core != half)(functools.partial(finish, half, send))
    e_copy.wait()


def field_copies(R, field, out, sems):
    step = R // 4
    return [pltpu.make_async_copy(field.at[:, n * step : n * step + step], out.at[:, n * step : n * step + step], sems.at[n]) for n in range(4)]


def merge_field(R, value, merge, field, out, sems):
    I = R // 2
    copies = field_copies(R, field, out, sems)
    for n, c in enumerate(copies):
        for s in range(n * I // 4, (n + 1) * I // 4):
            for rho, slots in enumerate(merge_rows(value[s], merge)):
                for k, piece in enumerate(slots):
                    field[k, 2 * s + rho] = piece
        c.start()
    return copies


def output_kernel(R, value, out, field, merge_ref, sems):
    merge_ref[...] = merge_matrix()
    for c in merge_field(R, value, merge_ref[...], field, out, sems):
        c.wait()


def input_grad_kernel(R, U, e_hbm, we_hbm, count, count_other, ig, e_rows, we, e3, we3, grads, field, merge_ref, sems):
    I = R // 2
    fetch = [pltpu.make_async_copy(we_hbm, we, sems.at[4]), pltpu.make_async_copy(e_hbm, e_rows, sems.at[5])]
    for c in fetch:
        c.start()
    merge_ref[...] = merge_matrix()
    scale = 1.0 / jnp.maximum(count[:1], count_other[:1])
    scale = jnp.concatenate([scale] * 2, axis=1)
    fetch[0].wait()
    up_weights(we3, we, -1)
    fetch[1].wait()

    def widen(e, count):
        for n in range(count):
            v = e_rows[e + n]
            e3[e + n, :128] = column_before(v)
            e3[e + n, 128:256] = v
            e3[e + n, 256:] = column_after(v)

    def scatter(s, count):
        for n in range(count):
            grads[s + n] = (up(we3, e3, s + n) * scale).astype(BF16)

    chunked(0, I + 2, I + 2, widen)
    chunked(0, I, U, scatter)
    for c in merge_field(R, grads, merge_ref[...], field, ig, sems):
        c.wait()


def total_kernel(parts, count, wide, total, sems):
    peers = parts.shape[0]
    total[...] = sum(parts[p].astype(F32) for p in range(peers)).astype(BF16)
    copies = [pltpu.make_async_copy(total, wide.at[p], sems.at[p]) for p in range(peers)]
    for c in copies:
        c.start()
    me = lax.axis_index("snap") * lax.axis_size("x") + lax.axis_index("x")
    core = lax.axis_index("core")
    lo, hi = [jnp.where(core == 0, a, b) for a, b in zip(headless(peers, 0), headless(peers, 1), strict=True)]
    row = jnp.where((lo <= me) & (me < hi), 0.0, total[:16].astype(F32)[:1])
    count[...] = jnp.broadcast_to(row, (8, 128))
    for c in copies:
        c.wait()


PARTS = 4


def update_rows(n, totals, scale, weights, staged, results, sems, before):
    copies, sent = [], 0
    for p, (first, lo, hi) in enumerate(chunk_runs(totals.shape[0], n)):
        if lo == hi:
            break
        before(hi)
        grad = totals[p, first : first + hi - lo].astype(F32) * scale
        mom, ema, new = advance(grad, *[r[lo:hi] for r in weights])
        for ref, v in zip(staged, (grad, mom, ema, new, new.astype(BF16)), strict=True):
            ref[lo:hi] = v
        if hi == KERNEL_ROWS or hi - sent >= KERNEL_ROWS // PARTS:
            for m in range(5):
                c = pltpu.make_async_copy(staged[m].at[sent:hi], results[5 * n + m].at[sent:hi], sems.at[len(copies)])
                c.start()
                copies.append(c)
            sent = hi
    for c in copies:
        c.wait()


def own_update_kernel(totals, *refs):
    sources, small, results, bias_out = refs[:6], refs[6:9], refs[9:19], refs[19:24]
    ahead, weights, staged, sems, out_sems = refs[24:27], refs[27:30], refs[30:35], refs[35], refs[36]
    head = totals[0, 0:16].astype(F32)
    scale = 1.0 / head[0:1]
    core = lax.axis_index("core")
    step = KERNEL_ROWS // PARTS

    def half(n):
        own = [
            [
                pltpu.make_async_copy(sources[3 * n + m].at[p * step : p * step + step], weights[m].at[p * step : p * step + step], sems.at[3 * p + m])
                for m in range(3)
            ]
            for p in range(PARTS)
        ]
        later = [pltpu.make_async_copy(sources[3 * (1 - n) + m], ahead[m], sems.at[3 * PARTS + m]) for m in range(3)]
        for c in sum(own, []) + later:
            c.start()
        waited = [0]

        def before(hi):
            while waited[0] * step < hi:
                for c in own[waited[0]]:
                    c.wait()
                waited[0] += 1

        update_rows(n, totals, scale, weights, staged, results, out_sems, before)
        for c in later:
            c.wait()

    pl.when(core == 0)(lambda: half(0))
    pl.when(core != 0)(lambda: half(1))
    grad = jnp.concatenate([head[1:2], head[2:3, :64]], axis=1) * scale[:, :1]
    mom, ema, new = advance(grad, *[r[...] for r in small])
    for ref, v in zip(bias_out, (grad, mom, ema, new, new.astype(BF16)), strict=True):
        ref[...] = v


def other_update_kernel(totals, *refs):
    weights, results, staged, out_sems = refs[:3], refs[13:23], refs[23:28], refs[28]
    scale = 1.0 / totals[0, 0:16].astype(F32)[0:1]
    core = lax.axis_index("core")

    def half(n):
        update_rows(n, totals, scale, weights, staged, results, out_sems, lambda hi: None)

    pl.when(core == 0)(lambda: half(1))
    pl.when(core != 0)(lambda: half(0))


def advance(grad, weight, moment, average):
    moment_new = MOMENTUM * moment + grad
    weight_new = weight - LEARN_RATE * (grad + MOMENTUM * moment_new)
    average_new = EMA_DECAY * average + (1.0 - EMA_DECAY) * weight_new
    return (moment_new, average_new, weight_new)


def on_device(
    snapshots, cotangent, lengths, slot_mask, encoder_kernel, decoder_kernel, biases,
    encoder_mom, decoder_mom, bias_mom, encoder_ema, decoder_ema, bias_ema,
):
    slots, R, C, W = snapshots.shape
    latent_ch = encoder_kernel.shape[3]
    I, U = R // 2, 16
    nx = lax.axis_size("x")
    peers = lax.axis_size("snap") * nx
    swap = [(0, 1), (1, 0)]
    decoder_t = jnp.swapaxes(decoder_kernel, 2, 3)
    vmem, smem, hbm = (pl.BlockSpec(memory_space=m) for m in (pltpu.VMEM, pltpu.SMEM, pltpu.HBM))

    def call(kernel, name, megabytes, flops, **kw):
        return pl.pallas_call(
            kernel,
            name=name,
            compiler_params=pltpu.CompilerParams(vmem_limit_bytes=megabytes * 2**20),
            cost_estimate=pl.CostEstimate(flops=flops, bytes_accessed=4 << 20, transcendentals=0),
            **kw,
        )

    def sds(*shape, dtype=BF16):
        return jax.ShapeDtypeStruct(shape, dtype)

    def in_vmem(v):
        return pltpu.with_memory_space_constraint(v, pltpu.VMEM)

    def in_hbm(v):
        return pltpu.with_memory_space_constraint(v, pltpu.HBM)

    conv = 2 * 4096 * 204800
    halo = sds(slots, XH + CH, C, W)
    near, far = call(
        functools.partial(halo_kernel, R), "halo", 4, 0,
        out_shape=[halo, halo],
        in_specs=[hbm] * 2,
        out_specs=[vmem] * 2,
        scratch_shapes=[pltpu.SemaphoreType.DMA((4,))],
    )(in_hbm(snapshots), in_hbm(cotangent))
    far = lax.ppermute(far, ("x", "core"), [pair for n in range(nx - 1) for pair in ((2 * n + 1, 2 * n + 2), (2 * n + 2, 2 * n + 1))])
    near = lax.ppermute(near, "core", swap)
    bias_row = biases.reshape(1, -1)

    field = pltpu.HBM(snapshots.shape, BF16)
    state = [
        sds(XU + R + 8, 320, 256), sds(I + 6, 384, 256), sds(I + 2, 128, 256, dtype=F32), sds(R + 8, 320, 256),
        sds(I, 256, 256), sds(I + 4, 256, 256), sds(64, 256, dtype=F32), sds(320, 384, dtype=F32), sds(320, 256, dtype=F32),
    ]
    *mid, we2, wd2, wb = call(
        functools.partial(inner_kernel, R, U), "inner", INNER_MB, 2 * conv,
        out_shape=state + [sds(128, KERNEL_ROWS), sds(256, 1152), sds(128, KERNEL_ROWS)],
        in_specs=[hbm] * 4 + [vmem] + [smem] * 2,
        out_specs=[vmem] * 12,
        scratch_shapes=[
            pltpu.VMEM(snapshots.shape, BF16),
            pltpu.VMEM(snapshots.shape, BF16),
            pltpu.VMEM(encoder_kernel.shape, F32),
            pltpu.VMEM(encoder_kernel.shape, F32),
            pltpu.VMEM((256, 256), BF16),
            pltpu.SemaphoreType.DMA((5,)),
        ],
    )(in_hbm(snapshots), in_hbm(cotangent), in_hbm(encoder_kernel), in_hbm(decoder_t), bias_row, lengths, slot_mask)
    chunk = sds(peers, 16 * chunk_groups(peers), 128)
    e_rows, keep, send, _, _, _, _, value, *_ = call(
        functools.partial(outer_kernel, R, U), "outer", OUTER_MB, 4 * conv,
        out_shape=[pltpu.HBM((I + 2, 128, 256), BF16), chunk, chunk] + state,
        in_specs=[vmem] * 3 + [smem] * 2 + [vmem] * 12,
        out_specs=[hbm] + [vmem] * 11,
        input_output_aliases={8 + n: 3 + n for n in range(9)},
        scratch_shapes=[
            pltpu.VMEM((I + 2, 128, 256), BF16),
            pltpu.VMEM((128, 256), F32),
            pltpu.VMEM((256, 256), BF16),
            pltpu.SemaphoreType.DMA,
        ],
    )(near, far, bias_row, lengths, slot_mask, we2, wd2, wb, *mid)

    recv = lax.ppermute(send, "core", swap)
    output = call(
        functools.partial(output_kernel, R), "output", FIELD_MB, conv // 4,
        out_shape=field,
        in_specs=[vmem],
        out_specs=hbm,
        scratch_shapes=[pltpu.VMEM(snapshots.shape, BF16), pltpu.VMEM((256, 256), BF16), pltpu.SemaphoreType.DMA((4,))],
    )(value)
    part = (keep.astype(F32) + recv.astype(F32)).astype(BF16)
    part, output = lax.optimization_barrier((part, output))
    parts = lax.all_to_all(part, ("snap", "x"), 0, 0, tiled=True)
    live, wide = call(
        total_kernel, "total", 4, 0,
        out_shape=[sds(8, 128, dtype=F32), pltpu.HBM(part.shape, BF16)],
        in_specs=[vmem],
        out_specs=[vmem, hbm],
        scratch_shapes=[pltpu.VMEM(part.shape[1:], BF16), pltpu.SemaphoreType.DMA((peers,))],
    )(parts)
    live_other = lax.ppermute(live, "core", swap)
    mine = lax.all_to_all(wide, ("snap", "x"), 0, 0, tiled=True)
    input_grad = call(
        functools.partial(input_grad_kernel, R, U), "input_grad", FIELD_MB, 4 * conv,
        out_shape=field,
        in_specs=[hbm, hbm, vmem, vmem],
        out_specs=hbm,
        scratch_shapes=[
            pltpu.VMEM((I + 2, 128, 256), BF16),
            pltpu.VMEM(encoder_kernel.shape, F32),
            pltpu.VMEM((I + 2, 384, 256), BF16),
            pltpu.VMEM((256, 1152), BF16),
            pltpu.VMEM((I, 256, 256), BF16),
            pltpu.VMEM(snapshots.shape, BF16),
            pltpu.VMEM((256, 256), BF16),
            pltpu.SemaphoreType.DMA((6,)),
        ],
    )(in_hbm(e_rows), in_hbm(encoder_kernel), live, live_other)
    mine, input_grad = lax.optimization_barrier((mine, input_grad))
    other = lax.ppermute(mine, "core", swap)

    def rows(v):
        return v.reshape(KERNEL_ROWS, 128)

    def trows(v):
        return jnp.swapaxes(v, 2, 3).reshape(KERNEL_ROWS, 128)

    params = [
        rows(encoder_kernel), rows(encoder_mom), rows(encoder_ema),
        trows(decoder_kernel), trows(decoder_mom), trows(decoder_ema),
    ]
    shape = (KERNEL_ROWS, 128)
    five = [pltpu.HBM(shape, F32)] * 4 + [pltpu.HBM(shape, BF16)]
    staged = [pltpu.VMEM(v.shape, v.dtype) for v in five]
    bias_shape = [sds(1, latent_ch + C, dtype=F32)] * 4 + [sds(1, latent_ch + C)]
    begun = call(
        own_update_kernel, "update_own", UPDATE_MB, 1 << 20,
        out_shape=five * 2 + bias_shape + [pltpu.VMEM(shape, F32)] * 3,
        in_specs=[vmem] + [hbm] * 6 + [vmem] * 3,
        out_specs=[hbm] * 10 + [vmem] * 8,
        scratch_shapes=[pltpu.VMEM(shape, F32)] * 3
        + staged
        + [pltpu.SemaphoreType.DMA((3 * PARTS + 3,)), pltpu.SemaphoreType.DMA((5 * PARTS,))],
    )(mine, *[in_hbm(v) for v in params], bias_row, bias_mom.reshape(1, -1), bias_ema.reshape(1, -1))
    bias_grad, bia_mom, bia_ema, bia_new, bia_copy = [v.reshape(biases.shape) for v in begun[10:15]]
    results = call(
        other_update_kernel, "update_other", UPDATE_MB, 1 << 20,
        out_shape=five * 2,
        in_specs=[vmem] * 4 + [hbm] * 10,
        out_specs=[hbm] * 10,
        input_output_aliases={4 + n: n for n in range(10)},
        scratch_shapes=staged + [pltpu.SemaphoreType.DMA((5 * PARTS,))],
    )(other, *[in_vmem(v) for v in begun[15:]], *[in_hbm(v) for v in begun[:10]])
    enc_grad, enc_mom, enc_ema, enc_new, enc_copy = [v.reshape(encoder_kernel.shape) for v in results[:5]]
    dec_grad, dec_mom, dec_ema, dec_new, dec_copy = [jnp.swapaxes(v.reshape(decoder_t.shape), 2, 3) for v in results[5:]]
    return (
        output, input_grad, enc_grad, dec_grad, bias_grad, enc_mom, dec_mom, bia_mom,
        enc_ema, dec_ema, bia_ema, enc_new, dec_new, bia_new, enc_copy, dec_copy, bia_copy,
    )


def solution(mesh):
    snap, rows = mesh.devices.shape
    split = Mesh(mesh.devices.reshape(snap, rows // 2, 2), ("snap", "x", "core"))
    field = P("snap", ("x", "core"), None, None)
    return jax.shard_map(
        on_device,
        mesh=split,
        in_specs=(field, field, P("snap"), P("snap")) + (P(),) * 9,
        out_specs=(field, field) + (P(),) * 15,
        check_vma=False,
    )
```

```python
import functools

import jax
import jax.numpy as jnp
from jax import lax
from jax.experimental import pallas as pl
from jax.experimental.pallas import tpu as pltpu
from jax.sharding import Mesh, PartitionSpec as P

MOMENTUM = 0.5
EMA_DECAY = 0.5
LEARN_RATE = 0.01
F32, BF16 = jnp.float32, jnp.bfloat16
XH, CH = 8, 4
XU, XD = 8, 7
NT = (((1,), (1,)), ((), ()))
KERNEL_ROWS = 1600
INNER_MB, OUTER_MB, FIELD_MB, UPDATE_MB = 8, 8, 12, 12


HEAD = 8


def chunk_span(peers):
    return -(-KERNEL_ROWS // (8 * peers)) * 8


def chunk_runs(peers):
    span = chunk_span(peers)
    return [(min(KERNEL_ROWS, p * span), min(KERNEL_ROWS, (p + 1) * span)) for p in range(peers)]


def dot(a, b):
    return jnp.dot(a, b, preferred_element_type=F32)


def chunked(lo, hi, size, step):
    whole = (hi - lo) // size
    if whole == 1:
        step(lo, size)
    elif whole:
        pl.loop(0, whole)(lambda n: step(lo + n * size, size))
    rest = (hi - lo) % size
    if rest:
        step(hi - rest, rest)


def split_matrix():
    row = lax.broadcasted_iota(jnp.int32, (256, 256), 0)
    col = lax.broadcasted_iota(jnp.int32, (256, 256), 1)
    want = (col // 64 % 2) * 128 + (col % 64) * 2 + col // 128
    return jnp.where(row == want, 1.0, 0.0).astype(BF16)


def merge_matrix():
    row = lax.broadcasted_iota(jnp.int32, (256, 256), 0)
    col = lax.broadcasted_iota(jnp.int32, (256, 256), 1)
    want = (row // 64 % 2) * 128 + (row % 64) * 2 + row // 128
    return jnp.where(col == want, 1.0, 0.0).astype(BF16)


def column_before(v):
    return shifted(v, 1, 0)


def column_after(v):
    return shifted(v, 127, 63)


def shifted(v, by, edge):
    parts = []
    for h in range(v.shape[1] // 128):
        part = v[:, h * 128 : (h + 1) * 128]
        lane = lax.broadcasted_iota(jnp.int32, part.shape, 1) % 64
        parts.append(jnp.where(lane == edge, jnp.zeros_like(part), pltpu.roll(part, by, axis=1)))
    return parts[0] if len(parts) == 1 else jnp.concatenate(parts, axis=1)


def split_rows(rows, split):
    pieces = [jnp.concatenate([row(2 * h), row(2 * h + 1)], axis=1) for row in rows for h in range(2)]
    y = dot(jnp.concatenate(pieces, axis=0), split)
    out = []
    for n in range(len(rows)):
        a, b = y[n * 128 : n * 128 + 64], y[n * 128 + 64 : n * 128 + 128]
        out.append([jnp.concatenate([a[:, p * 128 : p * 128 + 128], b[:, p * 128 : p * 128 + 128]], axis=1) for p in range(2)])
    return out


def merge_rows(v, merge):
    pieces = [
        jnp.concatenate([v[rho * 128 : rho * 128 + 64, h * 128 : h * 128 + 128], v[rho * 128 + 64 : rho * 128 + 128, h * 128 : h * 128 + 128]], axis=1)
        for rho in range(2)
        for h in range(2)
    ]
    y = dot(jnp.concatenate(pieces, axis=0), merge).astype(BF16)
    return [
        [y[(rho * 2 + n // 2) * 64 : (rho * 2 + n // 2) * 64 + 64, (n % 2) * 128 : (n % 2) * 128 + 128] for n in range(4)]
        for rho in range(2)
    ]


def up_weights(dest, taps, sign):
    for rho in range(2):
        for pi in range(2):
            for di in range(-1, 2):
                for dj in range(-1, 2):
                    a, b = 2 + sign * (2 * di - rho), 2 + sign * (2 * dj - pi)
                    inside = 0 <= a <= 4 and 0 <= b <= 4
                    block = taps[a, b].astype(BF16) if inside else jnp.zeros((64, 128), BF16)
                    r, c = (rho * 2 + pi) * 64, ((di + 1) * 3 + dj + 1) * 128
                    dest[r : r + 64, c : c + 128] = block


def lane_sums(v):
    ones = jnp.ones((8, v.shape[1]), F32)
    return lax.dot_general(ones, v, NT, precision=lax.Precision.HIGHEST, preferred_element_type=F32)[:1]


def store_columns(xb, at, halves):
    even, odd = [v.astype(BF16) for v in halves]
    for b, v in enumerate([column_before(even), column_before(odd), even, odd, column_after(even)]):
        xb[at, b * 64 : b * 64 + 64] = v


def store_split(seeds, at, pair, live_lane):
    for rho, halves in enumerate(pair):
        for pi, v in enumerate(halves):
            row = (rho * 2 + pi) * 64
            seeds[at, row : row + 64] = (v * live_lane).astype(BF16)


def up(weights, rows, at):
    even = dot(weights[:128], rows[pl.ds(at, 3)].reshape(9 * 128, 256))
    odd = dot(weights[128:, 384:], rows[pl.ds(at + 1, 2)].reshape(6 * 128, 256))
    return jnp.concatenate([even, odd], axis=0)


def encode_row(u, I, ends, we2, bias, xb, l3, slope):
    pre = dot(we2[...], xb[pl.ds(2 * u, 5)].reshape(KERNEL_ROWS, 256)) + bias
    grow = jnp.exp(jnp.minimum(pre, 0.0))
    lat = jnp.maximum(pre, grow - 1.0)
    if ends is not None:
        if u < 3:
            lat = jnp.where(ends[0], 0.0, lat)
        if u >= I + 3:
            lat = jnp.where(ends[1], 0.0, lat)
    if ends is None or 2 <= u < I + 4:
        slope[u - 2] = grow
    lat = lat.astype(BF16)
    l3[u, :128] = column_before(lat)
    l3[u, 128:256] = lat
    l3[u, 256:] = column_after(lat)


def decode_row(w, own, wd2, bias, seeds, l3, d5, value, dsum):
    pre = up(wd2, l3, w) + bias
    grow = jnp.exp(jnp.minimum(pre, 0.0))
    if own:
        value[w - 2] = jnp.maximum(pre, grow - 1.0).astype(BF16)
    full = seeds[w].astype(F32) * grow
    if own:
        dsum[...] += (full[:64] + full[64:128]) + (full[128:192] + full[192:])
    back = full.astype(BF16)
    for rho in range(2):
        even, odd = [back[(rho * 2 + pi) * 64 : (rho * 2 + pi) * 64 + 64] for pi in range(2)]
        for b, v in enumerate([column_after(even), odd, even, column_before(odd), column_before(even)]):
            d5[2 * w + rho, b * 64 : b * 64 + 64] = v


def back_row(e, own, wb, d5, slope, e_rows, esum, outside=None):
    v = dot(wb[...], d5[pl.ds(2 * e, 5)].reshape(KERNEL_ROWS, 256)) * slope[e]
    if own:
        esum[...] += v
    else:
        v = jnp.where(outside, 0.0, v)
    e_rows[e] = v.astype(BF16)


def live_lanes(lens, mask):
    slot = lax.broadcasted_iota(jnp.int32, (1, 256), 1) // 64
    lanes, count = jnp.zeros((1, 256), F32), jnp.float32(0)
    for n in range(4):
        valid = jnp.where((n < lens[0]) & (mask[n] > 0), 1.0, 0.0)
        count = count + valid
        lanes = jnp.where(slot == n, valid, lanes)
    return lanes, count


def bias_tiles(bias):
    def column(row):
        count = row.shape[1]
        at = lax.broadcasted_iota(jnp.int32, (count, count), 0)
        to = lax.broadcasted_iota(jnp.int32, (count, count), 1)
        return jnp.sum(jnp.where(at == to, jnp.broadcast_to(row, (count, count)), 0.0), axis=1, keepdims=True)

    enc = column(bias[:, :128])
    dec = column(bias[:, 128:])
    return jnp.broadcast_to(enc, (128, 256)), jnp.broadcast_to(jnp.concatenate([dec] * 4, axis=0), (256, 256))


def halo_kernel(R, x_hbm, c_hbm, near, far, sems):
    core = lax.axis_index("core")
    copies = []
    for n, (dest, low) in enumerate(((near, core == 0), (far, core == 1))):
        for m, (src, rows, at) in enumerate(((x_hbm, XH, 0), (c_hbm, CH, XH))):
            start = jnp.where(low, R - rows, 0)
            copies.append(pltpu.make_async_copy(src.at[:, pl.ds(start, rows)], dest.at[:, at : at + rows], sems.at[2 * n + m]))
    for c in copies:
        c.start()
    for c in copies:
        c.wait()


def kernel_grad(rows, cols, cols_at, latent, latent_at):
    rhs = jnp.concatenate(
        [jnp.concatenate([latent(latent_at + s + d) for d in range(3)], axis=0) for s in rows], axis=1
    )
    even, odd = [jnp.concatenate([cols[cols_at + 2 * s + rho] for s in rows], axis=1) for rho in range(2)]
    return (
        lax.dot_general(even, rhs, NT, preferred_element_type=F32),
        lax.dot_general(odd, rhs[128:], NT, preferred_element_type=F32),
    )


def inner_kernel(
    R, U, xv, cv, we_hbm, wdt_hbm, bias, lens, mask,
    xb, l3, slope, d5, value, seeds, dsum, acc0, acc1, e_rows, esum, we2, wd2, wb, bias_enc, bias_dec, split_ref, we, wdt, sems,
):
    I = R // 2
    copies = [pltpu.make_async_copy(a, b, sems.at[n]) for n, (a, b) in enumerate(((we_hbm, we), (wdt_hbm, wdt)))]
    for c in copies:
        c.start()
    split_ref[...] = split_matrix()
    dsum[...] = jnp.zeros_like(dsum)
    live_lane, _ = live_lanes(lens, mask)
    bias_enc[...], bias_dec[...] = bias_tiles(bias[...])
    esum[...] = jnp.zeros_like(esum)

    def columns(t, count):
        rows = [lambda s, r=t + m: xv[s, r] for m in range(count)]
        for n, halves in enumerate(split_rows(rows, split_ref[...])):
            store_columns(xb, XU + t + n, halves)

    def cotangent(s, count):
        rows = [lambda k, r=2 * s + m: cv[k, r] for m in range(2 * count)]
        halves = split_rows(rows, split_ref[...])
        for n in range(count):
            store_split(seeds, s + n + 2, halves[2 * n : 2 * n + 2], live_lane)

    def encode(u, count):
        for n in range(count):
            encode_row(u + n, I, None, we2, bias_enc[...], xb, l3, slope)

    def decode(w, count):
        for n in range(count):
            decode_row(w + n, True, wd2, bias_dec[...], seeds, l3, d5, value, dsum)

    chunked(0, R, U, columns)
    copies[0].wait()
    we2[...] = we[...].reshape(KERNEL_ROWS, 128).T.astype(BF16)
    chunked(4, I + 2, U, encode)
    copies[1].wait()
    up_weights(wd2, wdt, 1)
    chunked(0, I, U, cotangent)
    chunked(4, I, U, decode)
    wb[...] = jnp.concatenate([wdt[4 - q].reshape(320, 128) for q in range(5)], axis=0).T.astype(BF16)
    acc0[...], acc1[...] = kernel_grad(range(2, I - 2), d5, CH, lambda u: l3[u, 128:256], 2)
    for e in range(4, I - 2):
        back_row(e, True, wb, d5, slope, e_rows, esum)


def outer_kernel(
    R, far, near, lens, mask, we2, wd2, wb, bias_enc, bias_dec, split_ref,
    xb_in, l3_in, slope_in, d5_in, value_in, seeds_in, dsum_in, dec0_in, dec1_in, e_rows_in, esum_in,
    e_out, keep, send, xb, l3, slope, d5, value, seeds, dsum, dec0, dec1, e_rows, esum,
    enc0, enc1, sem,
):
    I = R // 2
    core = lax.axis_index("core")
    row_at = lax.axis_index("x") * 2 + core
    ends = row_at == 0, row_at == lax.axis_size("x") * 2 - 1
    live_lane, count = live_lanes(lens, mask)
    upper = core == 0

    def above(r):
        return lambda s: jnp.where(upper, far[s, r], near[s, r])

    def below(r):
        return lambda s: jnp.where(upper, near[s, r], far[s, r])

    def encoder_grad(rows):
        return kernel_grad(rows, xb, XU, lambda e: e_rows[e], 0)

    rows = [above(r) for r in range(XU)] + [below(r) for r in range(XD)]
    for n, halves in enumerate(split_rows(rows, split_ref[...])):
        store_columns(xb, n if n < XU else R + n, halves)
    halves = split_rows([above(XH + r) for r in range(CH)] + [below(XH + r) for r in range(CH)], split_ref[...])
    for n, w in enumerate((0, 1, I + 2, I + 3)):
        store_split(seeds, w, halves[2 * n : 2 * n + 2], live_lane)
    for u in list(range(4)) + list(range(I + 2, I + 6)):
        encode_row(u, I, ends, we2, bias_enc[...], xb, l3, slope)
    ready = range(4, I - 4)
    if ready:
        enc0[...], enc1[...] = encoder_grad(ready)
    for w in list(range(4)) + list(range(I, I + 4)):
        decode_row(w, 2 <= w < I + 2, wd2, bias_dec[...], seeds, l3, d5, value, dsum)
    even, odd = kernel_grad([0, 1, I - 2, I - 1], d5, CH, lambda u: l3[u, 128:256], 2)
    dec0[...] += even
    dec1[...] += odd
    for e in list(range(4)) + list(range(I - 2, I + 2)):
        back_row(e, 1 <= e < I + 1, wb, d5, slope, e_rows, esum, ends[0] if e == 0 else ends[1])
    e_copy = pltpu.make_async_copy(e_rows, e_out, sem)
    e_copy.start()
    even, odd = encoder_grad([s for s in range(I) if s not in ready])
    if ready:
        enc0[...] += even
        enc1[...] += odd
    else:
        enc0[...], enc1[...] = even, odd

    count_row = jnp.broadcast_to(jnp.where(row_at == 0, count, 0.0), (1, 128))
    dec_row = jnp.concatenate([lane_sums(dsum[...]), jnp.zeros((1, 64), F32)], axis=1)
    head = jnp.concatenate([count_row, lane_sums(esum[...]), dec_row, jnp.zeros((HEAD - 3, 128), F32)], axis=0).astype(BF16)
    other_head = jnp.concatenate([count_row, jnp.zeros((HEAD - 1, 128), F32)], axis=0).astype(BF16)
    chunks, chunk_rows = keep.shape[:2]

    def fill(dest, even_acc, odd_acc, even_taps, odd_taps):
        blocks = [(a, even_acc, d) for d, a in enumerate(even_taps)] + [(a, odd_acc, d) for d, a in enumerate(odd_taps)]
        runs = chunk_runs(chunks)
        for a, acc, d in blocks:
            block = acc[:, d * 128 : d * 128 + 128]
            for p, (start, end) in enumerate(runs):
                lo, hi = max(start, a * 320), min(end, a * 320 + 320)
                if lo < hi:
                    dest[p, HEAD + lo - start : HEAD + hi - start] = block[lo - a * 320 : hi - a * 320].astype(BF16)
        for p, (start, end) in enumerate(runs):
            dest[p, :HEAD] = other_head if p else head
            if HEAD + end - start < chunk_rows:
                dest[p, HEAD + end - start :] = jnp.zeros((chunk_rows - HEAD - end + start, 128), BF16)

    def fill_both(enc_dest, dec_dest):
        fill(enc_dest, enc0, enc1, (4, 2, 0), (3, 1))
        fill(dec_dest, dec0, dec1, (0, 2, 4), (1, 3))

    pl.when(core == 0)(lambda: fill_both(keep, send))
    pl.when(core != 0)(lambda: fill_both(send, keep))
    e_copy.wait()


def field_copies(R, field, out, sems):
    step = R // 4
    return [pltpu.make_async_copy(field.at[:, n * step : n * step + step], out.at[:, n * step : n * step + step], sems.at[n]) for n in range(4)]


def merge_field(R, value, merge, field, out, sems):
    I = R // 2
    copies = field_copies(R, field, out, sems)
    for n, c in enumerate(copies):
        for s in range(n * I // 4, (n + 1) * I // 4):
            for rho, slots in enumerate(merge_rows(value[s], merge)):
                for k, piece in enumerate(slots):
                    field[k, 2 * s + rho] = piece
        c.start()
    return copies


def output_kernel(R, value, out, field, merge_ref, sems):
    merge_ref[...] = merge_matrix()
    for c in merge_field(R, value, merge_ref[...], field, out, sems):
        c.wait()


def input_grad_kernel(R, U, e_hbm, we_hbm, count, ig, e_rows, we, e3, we3, grads, field, merge_ref, sems):
    I = R // 2
    fetch = [pltpu.make_async_copy(we_hbm, we, sems.at[4]), pltpu.make_async_copy(e_hbm, e_rows, sems.at[5])]
    for c in fetch:
        c.start()
    merge_ref[...] = merge_matrix()
    scale = 1.0 / count[:1]
    scale = jnp.concatenate([scale] * 2, axis=1)
    fetch[0].wait()
    up_weights(we3, we, -1)
    fetch[1].wait()

    def widen(e, count):
        for n in range(count):
            v = e_rows[e + n]
            e3[e + n, :128] = column_before(v)
            e3[e + n, 128:256] = v
            e3[e + n, 256:] = column_after(v)

    def scatter(s, count):
        for n in range(count):
            grads[s + n] = (up(we3, e3, s + n) * scale).astype(BF16)

    chunked(0, I + 2, I + 2, widen)
    chunked(0, I, U, scatter)
    for c in merge_field(R, grads, merge_ref[...], field, ig, sems):
        c.wait()


def partial_kernel(parts, partial):
    partial[...] = sum(parts[p].astype(F32) for p in range(parts.shape[0])).astype(BF16)


def total_kernel(own, other, count, wide, total, sems):
    both = own[...].astype(F32) + other[...].astype(F32)
    total[...] = both.astype(BF16)
    copies = [pltpu.make_async_copy(total, wide.at[p], sems.at[p]) for p in range(wide.shape[0])]
    for c in copies:
        c.start()
    count[...] = jnp.broadcast_to(both[:1], (8, 128))
    for c in copies:
        c.wait()


PARTS = 4


def update_rows(n, totals, scale, weights, staged, results, sems, before):
    copies, sent = [], 0
    for p, (lo, hi) in enumerate(chunk_runs(totals.shape[0])):
        if lo == hi:
            break
        before(hi)
        grad = totals[p, HEAD : HEAD + hi - lo].astype(F32) * scale
        mom, ema, new = advance(grad, *[r[lo:hi] for r in weights])
        for ref, v in zip(staged, (grad, mom, ema, new, new.astype(BF16)), strict=True):
            ref[lo:hi] = v
        if hi == KERNEL_ROWS or (hi - sent >= KERNEL_ROWS // PARTS and hi % 16 == 0):
            for m in range(5):
                c = pltpu.make_async_copy(staged[m].at[sent:hi], results[5 * n + m].at[sent:hi], sems.at[len(copies)])
                c.start()
                copies.append(c)
            sent = hi
    for c in copies:
        c.wait()


def own_update_kernel(totals, *refs):
    sources, small, results, bias_out = refs[:6], refs[6:9], refs[9:19], refs[19:24]
    ahead, weights, staged, sems, out_sems = refs[24:27], refs[27:30], refs[30:35], refs[35], refs[36]
    core = lax.axis_index("core")
    head = totals[0, :16].astype(F32)
    scale = 1.0 / head[0:1]
    step = KERNEL_ROWS // PARTS

    def half(n):
        own = [
            [
                pltpu.make_async_copy(sources[3 * n + m].at[p * step : p * step + step], weights[m].at[p * step : p * step + step], sems.at[3 * p + m])
                for m in range(3)
            ]
            for p in range(PARTS)
        ]
        later = [pltpu.make_async_copy(sources[3 * (1 - n) + m], ahead[m], sems.at[3 * PARTS + m]) for m in range(3)]
        for c in sum(own, []) + later:
            c.start()
        waited = [0]

        def before(hi):
            while waited[0] * step < hi:
                for c in own[waited[0]]:
                    c.wait()
                waited[0] += 1

        update_rows(n, totals, scale, weights, staged, results, out_sems, before)
        for c in later:
            c.wait()

    pl.when(core == 0)(lambda: half(0))
    pl.when(core != 0)(lambda: half(1))
    grad = jnp.concatenate([head[1:2], head[2:3, :64]], axis=1) * scale[:, :1]
    mom, ema, new = advance(grad, *[r[...] for r in small])
    for ref, v in zip(bias_out, (grad, mom, ema, new, new.astype(BF16).reshape(-1)), strict=True):
        ref[...] = v


def other_update_kernel(totals, *refs):
    weights, results, staged, out_sems = refs[:3], refs[13:23], refs[23:28], refs[28]
    core = lax.axis_index("core")
    scale = 1.0 / totals[0, :16].astype(F32)[:1]

    def half(n):
        update_rows(n, totals, scale, weights, staged, results, out_sems, lambda hi: None)

    pl.when(core == 0)(lambda: half(1))
    pl.when(core != 0)(lambda: half(0))


def advance(grad, weight, moment, average):
    moment_new = MOMENTUM * moment + grad
    weight_new = weight - LEARN_RATE * (grad + MOMENTUM * moment_new)
    average_new = EMA_DECAY * average + (1.0 - EMA_DECAY) * weight_new
    return (moment_new, average_new, weight_new)


def on_device(
    snapshots, cotangent, lengths, slot_mask, encoder_kernel, decoder_kernel, biases,
    encoder_mom, decoder_mom, bias_mom, encoder_ema, decoder_ema, bias_ema,
):
    slots, R, C, W = snapshots.shape
    latent_ch = encoder_kernel.shape[3]
    I, U = R // 2, 16
    nx = lax.axis_size("x")
    peers = lax.axis_size("snap") * nx
    swap = [(0, 1), (1, 0)]
    decoder_t = jnp.swapaxes(decoder_kernel, 2, 3)
    vmem, smem, hbm = (pl.BlockSpec(memory_space=m) for m in (pltpu.VMEM, pltpu.SMEM, pltpu.HBM))

    def call(kernel, name, megabytes, flops, **kw):
        return pl.pallas_call(
            kernel,
            name=name,
            compiler_params=pltpu.CompilerParams(vmem_limit_bytes=megabytes * 2**20),
            cost_estimate=pl.CostEstimate(flops=flops, bytes_accessed=4 << 20, transcendentals=0),
            **kw,
        )

    def sds(*shape, dtype=BF16):
        return jax.ShapeDtypeStruct(shape, dtype)

    def in_vmem(v):
        return pltpu.with_memory_space_constraint(v, pltpu.VMEM)

    def in_hbm(v):
        return pltpu.with_memory_space_constraint(v, pltpu.HBM)

    conv = 2 * 4096 * 204800
    halo = sds(slots, XH + CH, C, W)
    near, far = call(
        functools.partial(halo_kernel, R), "halo", 4, 0,
        out_shape=[halo, halo],
        in_specs=[hbm] * 2,
        out_specs=[vmem] * 2,
        scratch_shapes=[pltpu.SemaphoreType.DMA((4,))],
    )(in_hbm(snapshots), in_hbm(cotangent))
    far = lax.ppermute(far, ("x", "core"), [pair for n in range(nx - 1) for pair in ((2 * n + 1, 2 * n + 2), (2 * n + 2, 2 * n + 1))])
    near = lax.ppermute(near, "core", swap)
    bias_row = biases.reshape(1, -1)

    field = pltpu.HBM(snapshots.shape, BF16)
    state = [
        sds(XU + R + 8, 320, 256), sds(I + 6, 384, 256), sds(I + 2, 128, 256, dtype=F32), sds(R + 8, 320, 256),
        sds(I, 256, 256), sds(I + 4, 256, 256), sds(64, 256, dtype=F32), sds(320, 384, dtype=F32), sds(320, 256, dtype=F32),
        sds(I + 2, 128, 256), sds(128, 256, dtype=F32),
    ]
    shared = [
        sds(128, KERNEL_ROWS), sds(256, 1152), sds(128, KERNEL_ROWS), sds(128, 256, dtype=F32), sds(256, 256, dtype=F32), sds(256, 256),
    ]
    parts = call(
        functools.partial(inner_kernel, R, U), "inner", INNER_MB, 2 * conv,
        out_shape=state + shared,
        in_specs=[vmem] * 2 + [hbm] * 2 + [vmem] + [smem] * 2,
        out_specs=[vmem] * 17,
        scratch_shapes=[
            pltpu.VMEM(encoder_kernel.shape, F32),
            pltpu.VMEM(encoder_kernel.shape, F32),
            pltpu.SemaphoreType.DMA((2,)),
        ],
    )(in_vmem(snapshots), in_vmem(cotangent), in_hbm(encoder_kernel), in_hbm(decoder_t), bias_row, lengths, slot_mask)
    chunk = sds(peers, HEAD + chunk_span(peers), 128)
    e_rows, keep, send, _, _, _, _, value, *_ = call(
        functools.partial(outer_kernel, R), "outer", OUTER_MB, 4 * conv,
        out_shape=[pltpu.HBM((I + 2, 128, 256), BF16), chunk, chunk] + state,
        in_specs=[vmem] * 2 + [smem] * 2 + [vmem] * 17,
        out_specs=[hbm] + [vmem] * 13,
        input_output_aliases={10 + n: 3 + n for n in range(11)},
        scratch_shapes=[pltpu.VMEM((320, 384), F32), pltpu.VMEM((320, 256), F32), pltpu.SemaphoreType.DMA],
    )(far, near, lengths, slot_mask, *parts[11:], *parts[:11])

    recv = lax.ppermute(send, "core", swap)
    output = call(
        functools.partial(output_kernel, R), "output", FIELD_MB, conv // 4,
        out_shape=field,
        in_specs=[vmem],
        out_specs=hbm,
        scratch_shapes=[pltpu.VMEM(snapshots.shape, BF16), pltpu.VMEM((256, 256), BF16), pltpu.SemaphoreType.DMA((4,))],
    )(value)
    part = (keep.astype(F32) + recv.astype(F32)).astype(BF16)
    part, output = lax.optimization_barrier((part, output))
    parts = lax.all_to_all(part, ("snap", "x"), 0, 0, tiled=True)
    own_side = call(partial_kernel, "partial", 4, 0, out_shape=sds(*part.shape[1:]), in_specs=[vmem], out_specs=vmem)(parts)
    other_side = lax.ppermute(own_side, "side", swap)
    live, wide = call(
        total_kernel, "total", 4, 0,
        out_shape=[sds(8, 128, dtype=F32), pltpu.HBM(part.shape, BF16)],
        in_specs=[vmem] * 2,
        out_specs=[vmem, hbm],
        scratch_shapes=[pltpu.VMEM(part.shape[1:], BF16), pltpu.SemaphoreType.DMA((peers,))],
    )(own_side, other_side)
    mine = lax.all_to_all(wide, ("snap", "x"), 0, 0, tiled=True)
    input_grad = call(
        functools.partial(input_grad_kernel, R, U), "input_grad", FIELD_MB, 4 * conv,
        out_shape=field,
        in_specs=[hbm, hbm, vmem],
        out_specs=hbm,
        scratch_shapes=[
            pltpu.VMEM((I + 2, 128, 256), BF16),
            pltpu.VMEM(encoder_kernel.shape, F32),
            pltpu.VMEM((I + 2, 384, 256), BF16),
            pltpu.VMEM((256, 1152), BF16),
            pltpu.VMEM((I, 256, 256), BF16),
            pltpu.VMEM(snapshots.shape, BF16),
            pltpu.VMEM((256, 256), BF16),
            pltpu.SemaphoreType.DMA((6,)),
        ],
    )(in_hbm(e_rows), in_hbm(encoder_kernel), live)
    mine, input_grad = lax.optimization_barrier((mine, input_grad))
    other = lax.ppermute(mine, "core", swap)

    def rows(v):
        return v.reshape(KERNEL_ROWS, 128)

    def trows(v):
        return jnp.swapaxes(v, 2, 3).reshape(KERNEL_ROWS, 128)

    params = [
        rows(encoder_kernel), rows(encoder_mom), rows(encoder_ema),
        trows(decoder_kernel), trows(decoder_mom), trows(decoder_ema),
    ]
    shape = (KERNEL_ROWS, 128)
    five = [pltpu.HBM(shape, F32)] * 4 + [pltpu.HBM(shape, BF16)]
    staged = [pltpu.VMEM(v.shape, v.dtype) for v in five]
    bias_shape = [sds(1, latent_ch + C, dtype=F32)] * 4 + [sds(latent_ch + C)]
    begun = call(
        own_update_kernel, "update_own", UPDATE_MB, 1 << 20,
        out_shape=five * 2 + bias_shape + [pltpu.VMEM(shape, F32)] * 3,
        in_specs=[vmem] + [hbm] * 6 + [vmem] * 3,
        out_specs=[hbm] * 10 + [vmem] * 8,
        scratch_shapes=[pltpu.VMEM(shape, F32)] * 3
        + staged
        + [pltpu.SemaphoreType.DMA((3 * PARTS + 3,)), pltpu.SemaphoreType.DMA((5 * PARTS,))],
    )(mine, *[in_hbm(v) for v in params], bias_row, bias_mom.reshape(1, -1), bias_ema.reshape(1, -1))
    bias_grad, bia_mom, bia_ema, bia_new, bia_copy = [v.reshape(biases.shape) for v in begun[10:15]]
    results = call(
        other_update_kernel, "update_other", UPDATE_MB, 1 << 20,
        out_shape=five * 2,
        in_specs=[vmem] * 4 + [hbm] * 10,
        out_specs=[hbm] * 10,
        input_output_aliases={4 + n: n for n in range(10)},
        scratch_shapes=staged + [pltpu.SemaphoreType.DMA((5 * PARTS,))],
    )(other, *[in_vmem(v) for v in begun[15:]], *[in_hbm(v) for v in begun[:10]])
    enc_grad, enc_mom, enc_ema, enc_new, enc_copy = [v.reshape(encoder_kernel.shape) for v in results[:5]]
    dec_grad, dec_mom, dec_ema, dec_new, dec_copy = [jnp.swapaxes(v.reshape(decoder_t.shape), 2, 3) for v in results[5:]]
    return (
        output, input_grad, enc_grad, dec_grad, bias_grad, enc_mom, dec_mom, bia_mom,
        enc_ema, dec_ema, bia_ema, enc_new, dec_new, bia_new, enc_copy, dec_copy, bia_copy,
    )


def solution(mesh):
    snap, rows = mesh.devices.shape
    split = Mesh(mesh.devices.reshape(2, snap // 2, rows // 2, 2), ("side", "snap", "x", "core"))
    slots = ("side", "snap")
    field = P(slots, ("x", "core"), None, None)
    return jax.shard_map(
        on_device,
        mesh=split,
        in_specs=(field, field, P(slots), P(slots)) + (P(),) * 9,
        out_specs=(field, field) + (P(),) * 15,
        check_vma=False,
    )
```

```python
import functools

import jax
import jax.numpy as jnp
from jax import lax
from jax.experimental import pallas as pl
from jax.experimental.pallas import tpu as pltpu
from jax.sharding import Mesh, PartitionSpec as P

MOMENTUM = 0.5
EMA_DECAY = 0.5
LEARN_RATE = 0.01
F32, BF16 = jnp.float32, jnp.bfloat16
XH, CH = 8, 4
XU, XD = 8, 7
NT = (((1,), (1,)), ((), ()))
KERNEL_ROWS = 1600
INNER_MB, OUTER_MB, FIELD_MB, UPDATE_MB = 8, 8, 12, 16


HEAD = 8


def chunk_span(peers):
    return -(-KERNEL_ROWS // (8 * peers)) * 8


def chunk_runs(peers):
    span = chunk_span(peers)
    return [(min(KERNEL_ROWS, p * span), min(KERNEL_ROWS, (p + 1) * span)) for p in range(peers)]


def dot(a, b):
    return jnp.dot(a, b, preferred_element_type=F32)


def chunked(lo, hi, size, step):
    whole = (hi - lo) // size
    if whole == 1:
        step(lo, size)
    elif whole:
        pl.loop(0, whole)(lambda n: step(lo + n * size, size))
    rest = (hi - lo) % size
    if rest:
        step(hi - rest, rest)


def split_matrix():
    row = lax.broadcasted_iota(jnp.int32, (256, 256), 0)
    col = lax.broadcasted_iota(jnp.int32, (256, 256), 1)
    want = (col // 64 % 2) * 128 + (col % 64) * 2 + col // 128
    return jnp.where(row == want, 1.0, 0.0).astype(BF16)


def merge_matrix():
    row = lax.broadcasted_iota(jnp.int32, (256, 256), 0)
    col = lax.broadcasted_iota(jnp.int32, (256, 256), 1)
    want = (row // 64 % 2) * 128 + (row % 64) * 2 + row // 128
    return jnp.where(col == want, 1.0, 0.0).astype(BF16)


def column_before(v):
    return shifted(v, 1, 0)


def column_after(v):
    return shifted(v, 127, 63)


def shifted(v, by, edge):
    parts = []
    for h in range(v.shape[1] // 128):
        part = v[:, h * 128 : (h + 1) * 128]
        lane = lax.broadcasted_iota(jnp.int32, part.shape, 1) % 64
        parts.append(jnp.where(lane == edge, jnp.zeros_like(part), pltpu.roll(part, by, axis=1)))
    return parts[0] if len(parts) == 1 else jnp.concatenate(parts, axis=1)


def split_rows(rows, split):
    pieces = [jnp.concatenate([row(2 * h), row(2 * h + 1)], axis=1) for row in rows for h in range(2)]
    y = dot(jnp.concatenate(pieces, axis=0), split)
    out = []
    for n in range(len(rows)):
        a, b = y[n * 128 : n * 128 + 64], y[n * 128 + 64 : n * 128 + 128]
        out.append([jnp.concatenate([a[:, p * 128 : p * 128 + 128], b[:, p * 128 : p * 128 + 128]], axis=1) for p in range(2)])
    return out


def merge_rows(v, merge):
    pieces = [
        jnp.concatenate([v[rho * 128 : rho * 128 + 64, h * 128 : h * 128 + 128], v[rho * 128 + 64 : rho * 128 + 128, h * 128 : h * 128 + 128]], axis=1)
        for rho in range(2)
        for h in range(2)
    ]
    y = dot(jnp.concatenate(pieces, axis=0), merge).astype(BF16)
    return [
        [y[(rho * 2 + n // 2) * 64 : (rho * 2 + n // 2) * 64 + 64, (n % 2) * 128 : (n % 2) * 128 + 128] for n in range(4)]
        for rho in range(2)
    ]


def up_weights(dest, taps, sign):
    for rho in range(2):
        for pi in range(2):
            for di in range(-1, 2):
                for dj in range(-1, 2):
                    a, b = 2 + sign * (2 * di - rho), 2 + sign * (2 * dj - pi)
                    inside = 0 <= a <= 4 and 0 <= b <= 4
                    block = taps[a, b].astype(BF16) if inside else jnp.zeros((64, 128), BF16)
                    r, c = (rho * 2 + pi) * 64, ((di + 1) * 3 + dj + 1) * 128
                    dest[r : r + 64, c : c + 128] = block


def lane_sums(v):
    ones = jnp.ones((8, v.shape[1]), F32)
    return lax.dot_general(ones, v, NT, precision=lax.Precision.HIGHEST, preferred_element_type=F32)[:1]


def store_columns(xb, at, halves):
    even, odd = [v.astype(BF16) for v in halves]
    for b, v in enumerate([column_before(even), column_before(odd), even, odd, column_after(even)]):
        xb[at, b * 64 : b * 64 + 64] = v


def store_split(seeds, at, pair, live_lane):
    for rho, halves in enumerate(pair):
        for pi, v in enumerate(halves):
            row = (rho * 2 + pi) * 64
            seeds[at, row : row + 64] = (v * live_lane).astype(BF16)


def up(weights, rows, at):
    even = dot(weights[:128], rows[pl.ds(at, 3)].reshape(9 * 128, 256))
    odd = dot(weights[128:, 384:], rows[pl.ds(at + 1, 2)].reshape(6 * 128, 256))
    return jnp.concatenate([even, odd], axis=0)


def encode_row(u, I, ends, we2, bias, xb, l3, slope):
    pre = dot(we2[...], xb[pl.ds(2 * u, 5)].reshape(KERNEL_ROWS, 256)) + bias
    grow = jnp.exp(jnp.minimum(pre, 0.0))
    lat = jnp.maximum(pre, grow - 1.0)
    if ends is not None:
        if u < 3:
            lat = jnp.where(ends[0], 0.0, lat)
        if u >= I + 3:
            lat = jnp.where(ends[1], 0.0, lat)
    if ends is None or 2 <= u < I + 4:
        slope[u - 2] = grow
    lat = lat.astype(BF16)
    l3[u, :128] = column_before(lat)
    l3[u, 128:256] = lat
    l3[u, 256:] = column_after(lat)


def decode_row(w, own, wd2, bias, seeds, l3, d5, value, dsum):
    pre = up(wd2, l3, w) + bias
    grow = jnp.exp(jnp.minimum(pre, 0.0))
    if own:
        value[w - 2] = jnp.maximum(pre, grow - 1.0).astype(BF16)
    full = seeds[w].astype(F32) * grow
    if own:
        dsum[...] += (full[:64] + full[64:128]) + (full[128:192] + full[192:])
    back = full.astype(BF16)
    for rho in range(2):
        even, odd = [back[(rho * 2 + pi) * 64 : (rho * 2 + pi) * 64 + 64] for pi in range(2)]
        for b, v in enumerate([column_after(even), odd, even, column_before(odd), column_before(even)]):
            d5[2 * w + rho, b * 64 : b * 64 + 64] = v


def back_row(e, own, wb, d5, slope, e_rows, esum, outside=None):
    v = dot(wb[...], d5[pl.ds(2 * e, 5)].reshape(KERNEL_ROWS, 256)) * slope[e]
    if own:
        esum[...] += v
    else:
        v = jnp.where(outside, 0.0, v)
    e_rows[e] = v.astype(BF16)


def live_lanes(lens, mask):
    slot = lax.broadcasted_iota(jnp.int32, (1, 256), 1) // 64
    lanes, count = jnp.zeros((1, 256), F32), jnp.float32(0)
    for n in range(4):
        valid = jnp.where((n < lens[0]) & (mask[n] > 0), 1.0, 0.0)
        count = count + valid
        lanes = jnp.where(slot == n, valid, lanes)
    return lanes, count


def bias_tiles(bias):
    def column(row):
        count = row.shape[1]
        at = lax.broadcasted_iota(jnp.int32, (count, count), 0)
        to = lax.broadcasted_iota(jnp.int32, (count, count), 1)
        return jnp.sum(jnp.where(at == to, jnp.broadcast_to(row, (count, count)), 0.0), axis=1, keepdims=True)

    enc = column(bias[:, :128])
    dec = column(bias[:, 128:])
    return jnp.broadcast_to(enc, (128, 256)), jnp.broadcast_to(jnp.concatenate([dec] * 4, axis=0), (256, 256))


def far_pairs(groups, nx):
    pairs = []
    for g in range(groups):
        base = g * 2 * nx
        for n in range(nx - 1):
            a, b = base + 2 * n + 1, base + 2 * n + 2
            pairs += [(a, b), (b, a)]
        other = g ^ 1
        if other < groups:
            pairs += [(base, other * 2 * nx), (base + 2 * nx - 1, (other + 1) * 2 * nx - 1)]
    return pairs


def halo_kernel(R, x_hbm, c_hbm, near, far, sems):
    core = lax.axis_index("core")
    copies = []
    for n, (dest, low) in enumerate(((near, core == 0), (far, core == 1))):
        for m, (src, rows, at) in enumerate(((x_hbm, XH, 0), (c_hbm, CH, XH))):
            start = jnp.where(low, R - rows, 0)
            copies.append(pltpu.make_async_copy(src.at[:, pl.ds(start, rows)], dest.at[:, at : at + rows], sems.at[2 * n + m]))
    for c in copies:
        c.start()
    for c in copies:
        c.wait()


def kernel_grad(rows, cols, cols_at, latent, latent_at):
    rhs = jnp.concatenate(
        [jnp.concatenate([latent(latent_at + s + d) for d in range(3)], axis=0) for s in rows], axis=1
    )
    even, odd = [jnp.concatenate([cols[cols_at + 2 * s + rho] for s in rows], axis=1) for rho in range(2)]
    return (
        lax.dot_general(even, rhs, NT, preferred_element_type=F32),
        lax.dot_general(odd, rhs[128:], NT, preferred_element_type=F32),
    )


def inner_kernel(
    R, U, xv, cv, we_hbm, wdt_hbm, bias, lens, mask,
    xb, l3, slope, d5, value, seeds, dsum, acc0, acc1, e_rows, esum, we2, wd2, wb, bias_enc, bias_dec, split_ref, we, wdt, sems,
):
    I = R // 2
    copies = [pltpu.make_async_copy(a, b, sems.at[n]) for n, (a, b) in enumerate(((we_hbm, we), (wdt_hbm, wdt)))]
    for c in copies:
        c.start()
    split_ref[...] = split_matrix()
    dsum[...] = jnp.zeros_like(dsum)
    live_lane, _ = live_lanes(lens, mask)
    bias_enc[...], bias_dec[...] = bias_tiles(bias[...])
    esum[...] = jnp.zeros_like(esum)

    def columns(t, count):
        rows = [lambda s, r=t + m: xv[s, r] for m in range(count)]
        for n, halves in enumerate(split_rows(rows, split_ref[...])):
            store_columns(xb, XU + t + n, halves)

    def cotangent(s, count):
        rows = [lambda k, r=2 * s + m: cv[k, r] for m in range(2 * count)]
        halves = split_rows(rows, split_ref[...])
        for n in range(count):
            store_split(seeds, s + n + 2, halves[2 * n : 2 * n + 2], live_lane)

    def encode(u, count):
        for n in range(count):
            encode_row(u + n, I, None, we2, bias_enc[...], xb, l3, slope)

    def decode(w, count):
        for n in range(count):
            decode_row(w + n, True, wd2, bias_dec[...], seeds, l3, d5, value, dsum)

    chunked(0, R, U, columns)
    copies[0].wait()
    we2[...] = we[...].reshape(KERNEL_ROWS, 128).T.astype(BF16)
    chunked(4, I + 2, U, encode)
    copies[1].wait()
    up_weights(wd2, wdt, 1)
    chunked(0, I, U, cotangent)
    chunked(4, I, U, decode)
    wb[...] = jnp.concatenate([wdt[4 - q].reshape(320, 128) for q in range(5)], axis=0).T.astype(BF16)
    acc0[...], acc1[...] = kernel_grad(range(2, I - 2), d5, CH, lambda u: l3[u, 128:256], 2)
    for e in range(4, I - 2):
        back_row(e, True, wb, d5, slope, e_rows, esum)


def outer_kernel(
    R, far, near, lens, mask, we2, wd2, wb, bias_enc, bias_dec, split_ref,
    xb_in, l3_in, slope_in, d5_in, value_in, seeds_in, dsum_in, dec0_in, dec1_in, e_rows_in, esum_in,
    keep, send, xb, l3, slope, d5, value, seeds, dsum, dec0, dec1, e_rows, esum, enc0, enc1,
):
    I = R // 2
    core = lax.axis_index("core")
    row_at = lax.axis_index("x") * 2 + core
    ends = row_at == 0, row_at == lax.axis_size("x") * 2 - 1
    live_lane, count = live_lanes(lens, mask)
    upper = core == 0

    def above(r):
        return lambda s: jnp.where(ends[0], jnp.zeros((64, 128), BF16), jnp.where(upper, far[s, r], near[s, r]))

    def below(r):
        return lambda s: jnp.where(ends[1], jnp.zeros((64, 128), BF16), jnp.where(upper, near[s, r], far[s, r]))

    def encoder_grad(rows):
        return kernel_grad(rows, xb, XU, lambda e: e_rows[e], 0)

    rows = [above(r) for r in range(XU)] + [below(r) for r in range(XD)]
    for n, halves in enumerate(split_rows(rows, split_ref[...])):
        store_columns(xb, n if n < XU else R + n, halves)
    halves = split_rows([above(XH + r) for r in range(CH)] + [below(XH + r) for r in range(CH)], split_ref[...])
    for n, w in enumerate((0, 1, I + 2, I + 3)):
        store_split(seeds, w, halves[2 * n : 2 * n + 2], live_lane)
    for u in list(range(4)) + list(range(I + 2, I + 6)):
        encode_row(u, I, ends, we2, bias_enc[...], xb, l3, slope)
    ready = range(4, I - 4)
    if ready:
        enc0[...], enc1[...] = encoder_grad(ready)
    for w in list(range(4)) + list(range(I, I + 4)):
        decode_row(w, 2 <= w < I + 2, wd2, bias_dec[...], seeds, l3, d5, value, dsum)
    even, odd = kernel_grad([0, 1, I - 2, I - 1], d5, CH, lambda u: l3[u, 128:256], 2)
    dec0[...] += even
    dec1[...] += odd
    for e in list(range(4)) + list(range(I - 2, I + 2)):
        back_row(e, 1 <= e < I + 1, wb, d5, slope, e_rows, esum, ends[0] if e == 0 else ends[1])
    even, odd = encoder_grad([s for s in range(I) if s not in ready])
    if ready:
        enc0[...] += even
        enc1[...] += odd
    else:
        enc0[...], enc1[...] = even, odd

    count_row = jnp.broadcast_to(jnp.where(row_at == 0, count, 0.0), (1, 128))
    dec_row = jnp.concatenate([lane_sums(dsum[...]), jnp.zeros((1, 64), F32)], axis=1)
    head = jnp.concatenate([count_row, lane_sums(esum[...]), dec_row, jnp.zeros((HEAD - 3, 128), F32)], axis=0).astype(BF16)
    other_head = jnp.concatenate([count_row, jnp.zeros((HEAD - 1, 128), F32)], axis=0).astype(BF16)
    chunks, chunk_rows = keep.shape[:2]

    def fill(dest, even_acc, odd_acc, even_taps, odd_taps):
        blocks = [(a, even_acc, d) for d, a in enumerate(even_taps)] + [(a, odd_acc, d) for d, a in enumerate(odd_taps)]
        runs = chunk_runs(chunks)
        for a, acc, d in blocks:
            block = acc[:, d * 128 : d * 128 + 128]
            for p, (start, end) in enumerate(runs):
                lo, hi = max(start, a * 320), min(end, a * 320 + 320)
                if lo < hi:
                    dest[p, HEAD + lo - start : HEAD + hi - start] = block[lo - a * 320 : hi - a * 320].astype(BF16)
        for p, (start, end) in enumerate(runs):
            dest[p, :HEAD] = other_head if p else head
            if HEAD + end - start < chunk_rows:
                dest[p, HEAD + end - start :] = jnp.zeros((chunk_rows - HEAD - end + start, 128), BF16)

    def fill_both(enc_dest, dec_dest):
        fill(enc_dest, enc0, enc1, (4, 2, 0), (3, 1))
        fill(dec_dest, dec0, dec1, (0, 2, 4), (1, 3))

    pl.when(core == 0)(lambda: fill_both(keep, send))
    pl.when(core != 0)(lambda: fill_both(send, keep))


def field_copies(R, field, out, sems):
    step = R // 4
    return [pltpu.make_async_copy(field.at[:, n * step : n * step + step], out.at[:, n * step : n * step + step], sems.at[n]) for n in range(4)]


def merge_field(R, value, merge, field, out, sems):
    I = R // 2
    copies = field_copies(R, field, out, sems)
    for n, c in enumerate(copies):
        for s in range(n * I // 4, (n + 1) * I // 4):
            for rho, slots in enumerate(merge_rows(value(s), merge)):
                for k, piece in enumerate(slots):
                    field[k, 2 * s + rho] = piece
        c.start()
    return copies


def output_kernel(R, value, out, field, merge_ref, sems):
    merge_ref[...] = merge_matrix()
    for c in merge_field(R, lambda s: value[s], merge_ref[...], field, out, sems):
        c.wait()


def scatter_kernel(R, U, e_rows, we_hbm, *refs):
    sources, grads, targets, (we, e3, we3, sems) = refs[:6], refs[6], refs[7:13], refs[13:]
    I = R // 2
    fetch = [pltpu.make_async_copy(we_hbm, we, sems.at[6])]
    fetch += [pltpu.make_async_copy(a, b, sems.at[n]) for n, (a, b) in enumerate(zip(sources, targets, strict=True))]
    for c in fetch:
        c.start()

    def widen(e, count):
        for n in range(count):
            v = e_rows[e + n]
            e3[e + n, :128] = column_before(v)
            e3[e + n, 128:256] = v
            e3[e + n, 256:] = column_after(v)

    def scatter(s, count):
        for n in range(count):
            grads[s + n] = up(we3, e3, s + n)

    chunked(0, I + 2, I + 2, widen)
    fetch[0].wait()
    up_weights(we3, we, -1)
    chunked(0, I, U, scatter)
    for c in fetch[1:]:
        c.wait()


def partial_kernel(parts, partial):
    partial[...] = sum(parts[p].astype(F32) for p in range(parts.shape[0])).astype(BF16)


def total_kernel(own, other, wide):
    both = own[...].astype(F32) + other[...].astype(F32)
    for p in range(wide.shape[0]):
        wide[p] = both.astype(BF16)


PARTS = 4


def update_kernel(owner, totals, *refs):
    params, results, staged, sems = refs[:6], refs[-16:-6], refs[-6:-1], refs[-1]
    head = totals[0, :16].astype(F32)
    scale = 1.0 / head[:1]

    def half(n):
        copies, sent = [], 0
        for p, (lo, hi) in enumerate(chunk_runs(totals.shape[0])):
            if lo == hi:
                break
            grad = totals[p, HEAD : HEAD + hi - lo].astype(F32) * scale
            mom, ema, new = advance(grad, *[r[lo:hi] for r in params[3 * n : 3 * n + 3]])
            for ref, v in zip(staged, (grad, mom, ema, new, new.astype(BF16)), strict=True):
                ref[lo:hi] = v
            if hi == KERNEL_ROWS or (hi - sent >= KERNEL_ROWS // PARTS and hi % 16 == 0):
                for m in range(5):
                    c = pltpu.make_async_copy(staged[m].at[sent:hi], results[5 * n + m].at[sent:hi], sems.at[len(copies)])
                    c.start()
                    copies.append(c)
                sent = hi
        for c in copies:
            c.wait()

    core = lax.axis_index("core")
    pl.when(core == owner)(lambda: half(0))
    pl.when(core != owner)(lambda: half(1))


def own_update_kernel(R, totals, *refs):
    params, small, grads, bias_out, ig, rest, (field, merge_ref, sems) = (
        refs[:6], refs[6:9], refs[9], refs[10:15], refs[15], refs[16:-3], refs[-3:],
    )
    head = totals[0, :16].astype(F32)
    scale = 1.0 / head[:1]
    wide_scale = jnp.concatenate([scale] * 2, axis=1)
    merge_ref[...] = merge_matrix()
    copies = merge_field(R, lambda s: (grads[s] * wide_scale).astype(BF16), merge_ref[...], field, ig, sems)
    grad = jnp.concatenate([head[1:2], head[2:3, :64]], axis=1) * scale[:, :1]
    mom, ema, new = advance(grad, *[r[...] for r in small])
    for ref, v in zip(bias_out, (grad, mom, ema, new, new.astype(BF16).reshape(-1)), strict=True):
        ref[...] = v
    update_kernel(0, totals, *params, *rest)
    for c in copies:
        c.wait()


def advance(grad, weight, moment, average):
    moment_new = MOMENTUM * moment + grad
    weight_new = weight - LEARN_RATE * (grad + MOMENTUM * moment_new)
    average_new = EMA_DECAY * average + (1.0 - EMA_DECAY) * weight_new
    return (moment_new, average_new, weight_new)


def on_device(
    snapshots, cotangent, lengths, slot_mask, encoder_kernel, decoder_kernel, biases,
    encoder_mom, decoder_mom, bias_mom, encoder_ema, decoder_ema, bias_ema,
):
    slots, R, C, W = snapshots.shape
    latent_ch = encoder_kernel.shape[3]
    I, U = R // 2, 16
    nx = lax.axis_size("x")
    peers = lax.axis_size("snap") * nx
    swap = [(0, 1), (1, 0)]
    decoder_t = jnp.swapaxes(decoder_kernel, 2, 3)
    vmem, smem, hbm = (pl.BlockSpec(memory_space=m) for m in (pltpu.VMEM, pltpu.SMEM, pltpu.HBM))

    def call(kernel, name, megabytes, flops, **kw):
        return pl.pallas_call(
            kernel,
            name=name,
            compiler_params=pltpu.CompilerParams(vmem_limit_bytes=megabytes * 2**20),
            cost_estimate=pl.CostEstimate(flops=flops, bytes_accessed=4 << 20, transcendentals=0),
            **kw,
        )

    def sds(*shape, dtype=BF16):
        return jax.ShapeDtypeStruct(shape, dtype)

    def in_vmem(v):
        return pltpu.with_memory_space_constraint(v, pltpu.VMEM)

    def in_hbm(v):
        return pltpu.with_memory_space_constraint(v, pltpu.HBM)

    conv = 2 * 4096 * 204800
    halo = sds(slots, XH + CH, C, W)
    near, far = call(
        functools.partial(halo_kernel, R), "halo", 4, 0,
        out_shape=[halo, halo],
        in_specs=[hbm] * 2,
        out_specs=[vmem] * 2,
        scratch_shapes=[pltpu.SemaphoreType.DMA((4,))],
    )(in_hbm(snapshots), in_hbm(cotangent))
    far = lax.ppermute(far, ("snap", "x", "core"), far_pairs(lax.axis_size("snap"), nx))
    near = lax.ppermute(near, "core", swap)
    bias_row = biases.reshape(1, -1)

    field = pltpu.HBM(snapshots.shape, BF16)
    state = [
        sds(XU + R + 8, 320, 256), sds(I + 6, 384, 256), sds(I + 2, 128, 256, dtype=F32), sds(R + 8, 320, 256),
        sds(I, 256, 256), sds(I + 4, 256, 256), sds(64, 256, dtype=F32), sds(320, 384, dtype=F32), sds(320, 256, dtype=F32),
        sds(I + 2, 128, 256), sds(128, 256, dtype=F32),
    ]
    shared = [
        sds(128, KERNEL_ROWS), sds(256, 1152), sds(128, KERNEL_ROWS), sds(128, 256, dtype=F32), sds(256, 256, dtype=F32), sds(256, 256),
    ]
    parts = call(
        functools.partial(inner_kernel, R, U), "inner", INNER_MB, 2 * conv,
        out_shape=state + shared,
        in_specs=[vmem] * 2 + [hbm] * 2 + [vmem] + [smem] * 2,
        out_specs=[vmem] * 17,
        scratch_shapes=[
            pltpu.VMEM(encoder_kernel.shape, F32),
            pltpu.VMEM(encoder_kernel.shape, F32),
            pltpu.SemaphoreType.DMA((2,)),
        ],
    )(in_vmem(snapshots), in_vmem(cotangent), in_hbm(encoder_kernel), in_hbm(decoder_t), bias_row, lengths, slot_mask)
    chunk = sds(peers, HEAD + chunk_span(peers), 128)
    keep, send, _, _, _, _, value, _, _, _, _, e_rows, _ = call(
        functools.partial(outer_kernel, R), "outer", OUTER_MB, 4 * conv,
        out_shape=[chunk, chunk] + state,
        in_specs=[vmem] * 2 + [smem] * 2 + [vmem] * 17,
        out_specs=[vmem] * 13,
        input_output_aliases={10 + n: 2 + n for n in range(11)},
        scratch_shapes=[pltpu.VMEM((320, 384), F32), pltpu.VMEM((320, 256), F32)],
    )(far, near, lengths, slot_mask, *parts[11:], *parts[:11])

    recv = lax.ppermute(send, "core", swap)
    output = call(
        functools.partial(output_kernel, R), "output", FIELD_MB, conv // 4,
        out_shape=field,
        in_specs=[vmem],
        out_specs=hbm,
        scratch_shapes=[pltpu.VMEM(snapshots.shape, BF16), pltpu.VMEM((256, 256), BF16), pltpu.SemaphoreType.DMA((4,))],
    )(value)
    part = (keep.astype(F32) + recv.astype(F32)).astype(BF16)
    part, output = lax.optimization_barrier((part, output))
    parts = lax.all_to_all(part, ("snap", "x"), 0, 0, tiled=True)
    parts, e_rows = lax.optimization_barrier((parts, e_rows))
    own_side = call(partial_kernel, "partial", 4, 0, out_shape=sds(*part.shape[1:]), in_specs=[vmem], out_specs=vmem)(parts)
    other_side = lax.ppermute(own_side, "side", swap)

    def rows(v):
        return v.reshape(KERNEL_ROWS, 128)

    def trows(v):
        return jnp.swapaxes(v, 2, 3).reshape(KERNEL_ROWS, 128)

    params = [
        rows(encoder_kernel), rows(encoder_mom), rows(encoder_ema),
        trows(decoder_kernel), trows(decoder_mom), trows(decoder_ema),
    ]
    shape = (KERNEL_ROWS, 128)
    grads, *params = call(
        functools.partial(scatter_kernel, R, U), "scatter", FIELD_MB, conv,
        out_shape=[sds(I, 256, 256, dtype=F32)] + [sds(*shape, dtype=F32)] * 6,
        in_specs=[vmem] + [hbm] * 7,
        out_specs=[vmem] * 7,
        scratch_shapes=[
            pltpu.VMEM(encoder_kernel.shape, F32),
            pltpu.VMEM((I + 2, 384, 256), BF16),
            pltpu.VMEM((256, 1152), BF16),
            pltpu.SemaphoreType.DMA((7,)),
        ],
    )(e_rows, in_hbm(encoder_kernel), *[in_hbm(v) for v in params])
    other_side, grads, params = lax.optimization_barrier((other_side, grads, params))
    wide = call(total_kernel, "total", 4, 0, out_shape=sds(*part.shape), in_specs=[vmem] * 2, out_specs=vmem)(own_side, other_side)
    mine = lax.all_to_all(wide, ("snap", "x"), 0, 0, tiled=True)
    mine, grads, params = lax.optimization_barrier((mine, grads, params))
    other = lax.ppermute(mine, "core", swap)
    five = [pltpu.HBM(shape, F32)] * 4 + [pltpu.HBM(shape, BF16)]
    staged = [pltpu.VMEM(v.shape, v.dtype) for v in five] + [pltpu.SemaphoreType.DMA((5 * PARTS,))]
    bias_shape = [sds(1, latent_ch + C, dtype=F32)] * 4 + [sds(latent_ch + C)]
    own = call(
        functools.partial(own_update_kernel, R), "update_own", UPDATE_MB, 1 << 20,
        out_shape=bias_shape + [field] + five * 2,
        in_specs=[vmem] * 11,
        out_specs=[vmem] * 5 + [hbm] * 11,
        scratch_shapes=staged + [pltpu.VMEM(snapshots.shape, BF16), pltpu.VMEM((256, 256), BF16), pltpu.SemaphoreType.DMA((4,))],
    )(mine, *params, bias_row, bias_mom.reshape(1, -1), bias_ema.reshape(1, -1), grads)
    bias_results, input_grad, begun = own[:5], own[5], own[6:]
    bias_grad, bia_mom, bia_ema, bia_new, bia_copy = [v.reshape(biases.shape) for v in bias_results]
    results = call(
        functools.partial(update_kernel, 1), "update_other", UPDATE_MB, 1 << 20,
        out_shape=five * 2,
        in_specs=[vmem] * 7 + [hbm] * 10,
        out_specs=[hbm] * 10,
        input_output_aliases={7 + n: n for n in range(10)},
        scratch_shapes=staged,
    )(other, *params, *[in_hbm(v) for v in begun])
    enc_grad, enc_mom, enc_ema, enc_new, enc_copy = [v.reshape(encoder_kernel.shape) for v in results[:5]]
    dec_grad, dec_mom, dec_ema, dec_new, dec_copy = [jnp.swapaxes(v.reshape(decoder_t.shape), 2, 3) for v in results[5:]]
    return (
        output, input_grad, enc_grad, dec_grad, bias_grad, enc_mom, dec_mom, bia_mom,
        enc_ema, dec_ema, bia_ema, enc_new, dec_new, bia_new, enc_copy, dec_copy, bia_copy,
    )


def solution(mesh):
    snap, rows = mesh.devices.shape
    split = Mesh(mesh.devices.reshape(2, snap // 2, rows // 2, 2), ("side", "snap", "x", "core"))
    slots = ("side", "snap")
    field = P(slots, ("x", "core"), None, None)
    return jax.shard_map(
        on_device,
        mesh=split,
        in_specs=(field, field, P(slots), P(slots)) + (P(),) * 9,
        out_specs=(field, field) + (P(),) * 15,
        check_vma=False,
    )
```

```python
import functools

import jax
import jax.numpy as jnp
from jax import lax
from jax.experimental import pallas as pl
from jax.experimental.pallas import tpu as pltpu
from jax.sharding import Mesh, PartitionSpec as P

MOMENTUM = 0.5
EMA_DECAY = 0.5
LEARN_RATE = 0.01
F32, BF16 = jnp.float32, jnp.bfloat16
XH, CH = 8, 4
XU, XD = 8, 7
NT = (((1,), (1,)), ((), ()))
KERNEL_ROWS = 1600
INNER_MB, OUTER_MB, FIELD_MB, UPDATE_MB = 8, 8, 12, 16


HEAD = 8


def chunk_span(peers):
    return -(-KERNEL_ROWS // (8 * peers)) * 8


def chunk_runs(peers):
    span = chunk_span(peers)
    return [(min(KERNEL_ROWS, p * span), min(KERNEL_ROWS, (p + 1) * span)) for p in range(peers)]


def dot(a, b):
    return jnp.dot(a, b, preferred_element_type=F32)


def chunked(lo, hi, size, step):
    whole = (hi - lo) // size
    if whole == 1:
        step(lo, size)
    elif whole:
        pl.loop(0, whole)(lambda n: step(lo + n * size, size))
    rest = (hi - lo) % size
    if rest:
        step(hi - rest, rest)


def split_matrix():
    row = lax.broadcasted_iota(jnp.int32, (256, 256), 0)
    col = lax.broadcasted_iota(jnp.int32, (256, 256), 1)
    want = (col // 64 % 2) * 128 + (col % 64) * 2 + col // 128
    return jnp.where(row == want, 1.0, 0.0).astype(BF16)


def merge_matrix():
    row = lax.broadcasted_iota(jnp.int32, (256, 256), 0)
    col = lax.broadcasted_iota(jnp.int32, (256, 256), 1)
    want = (row // 64 % 2) * 128 + (row % 64) * 2 + row // 128
    return jnp.where(col == want, 1.0, 0.0).astype(BF16)


def column_before(v):
    return shifted(v, 1, 0)


def column_after(v):
    return shifted(v, 127, 63)


def shifted(v, by, edge):
    parts = []
    for h in range(v.shape[1] // 128):
        part = v[:, h * 128 : (h + 1) * 128]
        lane = lax.broadcasted_iota(jnp.int32, part.shape, 1) % 64
        parts.append(jnp.where(lane == edge, jnp.zeros_like(part), pltpu.roll(part, by, axis=1)))
    return parts[0] if len(parts) == 1 else jnp.concatenate(parts, axis=1)


def split_rows(rows, split):
    pieces = [jnp.concatenate([row(2 * h), row(2 * h + 1)], axis=1) for row in rows for h in range(2)]
    y = dot(jnp.concatenate(pieces, axis=0), split)
    out = []
    for n in range(len(rows)):
        a, b = y[n * 128 : n * 128 + 64], y[n * 128 + 64 : n * 128 + 128]
        out.append([jnp.concatenate([a[:, p * 128 : p * 128 + 128], b[:, p * 128 : p * 128 + 128]], axis=1) for p in range(2)])
    return out


def merge_rows(v, merge):
    pieces = [
        jnp.concatenate([v[rho * 128 : rho * 128 + 64, h * 128 : h * 128 + 128], v[rho * 128 + 64 : rho * 128 + 128, h * 128 : h * 128 + 128]], axis=1)
        for rho in range(2)
        for h in range(2)
    ]
    y = dot(jnp.concatenate(pieces, axis=0), merge).astype(BF16)
    return [
        [y[(rho * 2 + n // 2) * 64 : (rho * 2 + n // 2) * 64 + 64, (n % 2) * 128 : (n % 2) * 128 + 128] for n in range(4)]
        for rho in range(2)
    ]


def up_weights(dest, taps, sign):
    for rho in range(2):
        for pi in range(2):
            for di in range(-1, 2):
                for dj in range(-1, 2):
                    a, b = 2 + sign * (2 * di - rho), 2 + sign * (2 * dj - pi)
                    inside = 0 <= a <= 4 and 0 <= b <= 4
                    block = taps[a, b].astype(BF16) if inside else jnp.zeros((64, 128), BF16)
                    r, c = (rho * 2 + pi) * 64, ((di + 1) * 3 + dj + 1) * 128
                    dest[r : r + 64, c : c + 128] = block


def lane_sums(v):
    ones = jnp.ones((8, v.shape[1]), F32)
    return lax.dot_general(ones, v, NT, precision=lax.Precision.HIGHEST, preferred_element_type=F32)[:1]


def store_columns(xb, at, halves):
    even, odd = [v.astype(BF16) for v in halves]
    for b, v in enumerate([column_before(even), column_before(odd), even, odd, column_after(even)]):
        xb[at, b * 64 : b * 64 + 64] = v


def store_split(seeds, at, pair, live_lane):
    for rho, halves in enumerate(pair):
        for pi, v in enumerate(halves):
            row = (rho * 2 + pi) * 64
            seeds[at, row : row + 64] = (v * live_lane).astype(BF16)


def up(weights, rows, at):
    even = dot(weights[:128], rows[pl.ds(at, 3)].reshape(9 * 128, 256))
    odd = dot(weights[128:, 384:], rows[pl.ds(at + 1, 2)].reshape(6 * 128, 256))
    return jnp.concatenate([even, odd], axis=0)


def encode_row(u, I, ends, we2, bias, xb, l3, slope):
    pre = dot(we2[...], xb[pl.ds(2 * u, 5)].reshape(KERNEL_ROWS, 256)) + bias
    grow = jnp.exp(jnp.minimum(pre, 0.0))
    lat = jnp.maximum(pre, grow - 1.0)
    if ends is not None:
        if u < 3:
            lat = jnp.where(ends[0], 0.0, lat)
        if u >= I + 3:
            lat = jnp.where(ends[1], 0.0, lat)
    if ends is None or 2 <= u < I + 4:
        slope[u - 2] = grow
    lat = lat.astype(BF16)
    l3[u, :128] = column_before(lat)
    l3[u, 128:256] = lat
    l3[u, 256:] = column_after(lat)


def decode_row(w, own, wd2, bias, seeds, l3, d5, value, dsum):
    pre = up(wd2, l3, w) + bias
    grow = jnp.exp(jnp.minimum(pre, 0.0))
    if own:
        value[w - 2] = jnp.maximum(pre, grow - 1.0).astype(BF16)
    full = seeds[w].astype(F32) * grow
    if own:
        dsum[...] += (full[:64] + full[64:128]) + (full[128:192] + full[192:])
    back = full.astype(BF16)
    for rho in range(2):
        even, odd = [back[(rho * 2 + pi) * 64 : (rho * 2 + pi) * 64 + 64] for pi in range(2)]
        for b, v in enumerate([column_after(even), odd, even, column_before(odd), column_before(even)]):
            d5[2 * w + rho, b * 64 : b * 64 + 64] = v


def back_row(e, own, wb, d5, slope, e_rows, esum, outside=None):
    v = dot(wb[...], d5[pl.ds(2 * e, 5)].reshape(KERNEL_ROWS, 256)) * slope[e]
    if own:
        esum[...] += v
    else:
        v = jnp.where(outside, 0.0, v)
    e_rows[e] = v.astype(BF16)


def live_lanes(lens, mask):
    lane = lax.broadcasted_iota(jnp.int32, (1, 256), 1)
    length, valid = jnp.broadcast_to(lens, (1, 256)), jnp.zeros((1, 256), jnp.int32)
    for n in range(4):
        valid = jnp.where(lane // 64 == n, jnp.broadcast_to(mask[:, n : n + 1], (1, 256)), valid)
    return jnp.where((lane // 64 < length) & (valid > 0), 1.0, 0.0)


def bias_tiles(bias):
    def column(row):
        count = row.shape[1]
        at = lax.broadcasted_iota(jnp.int32, (count, count), 0)
        to = lax.broadcasted_iota(jnp.int32, (count, count), 1)
        return jnp.sum(jnp.where(at == to, jnp.broadcast_to(row, (count, count)), 0.0), axis=1, keepdims=True)

    enc = column(bias[:, :128])
    dec = column(bias[:, 128:])
    return jnp.broadcast_to(enc, (128, 256)), jnp.broadcast_to(jnp.concatenate([dec] * 4, axis=0), (256, 256))


def far_pairs(groups, nx):
    pairs = []
    for g in range(groups):
        base = g * 2 * nx
        for n in range(nx - 1):
            a, b = base + 2 * n + 1, base + 2 * n + 2
            pairs += [(a, b), (b, a)]
        other = g ^ 1
        if other < groups:
            pairs += [(base, other * 2 * nx), (base + 2 * nx - 1, (other + 1) * 2 * nx - 1)]
    return pairs


def halo_kernel(R, x_hbm, c_hbm, near, far, sems):
    core = lax.axis_index("core")
    copies = []
    for n, (dest, low) in enumerate(((near, core == 0), (far, core == 1))):
        for m, (src, rows, at) in enumerate(((x_hbm, XH, 0), (c_hbm, CH, XH))):
            start = jnp.where(low, R - rows, 0)
            copies.append(pltpu.make_async_copy(src.at[:, pl.ds(start, rows)], dest.at[:, at : at + rows], sems.at[2 * n + m]))
    for c in copies:
        c.start()
    for c in copies:
        c.wait()


def kernel_grad(rows, cols, cols_at, latent, latent_at):
    rhs = jnp.concatenate(
        [jnp.concatenate([latent(latent_at + s + d) for d in range(3)], axis=0) for s in rows], axis=1
    )
    even, odd = [jnp.concatenate([cols[cols_at + 2 * s + rho] for s in rows], axis=1) for rho in range(2)]
    return (
        lax.dot_general(even, rhs, NT, preferred_element_type=F32),
        lax.dot_general(odd, rhs[128:], NT, preferred_element_type=F32),
    )


def inner_kernel(
    R, U, xv, cv, we_hbm, wdt_hbm, bias, lens, mask,
    xb, l3, slope, d5, value, seeds, dsum, acc0, acc1, e_rows, esum, we2, wd2, wb, bias_enc, bias_dec, split_ref, live, we, wdt, sems,
):
    I = R // 2
    copies = [pltpu.make_async_copy(a, b, sems.at[n]) for n, (a, b) in enumerate(((we_hbm, we), (wdt_hbm, wdt)))]
    for c in copies:
        c.start()
    split_ref[...] = split_matrix()
    dsum[...] = jnp.zeros_like(dsum)
    live_lane = live_lanes(lens[...], mask[...])
    live[...] = jnp.broadcast_to(live_lane, live.shape)
    bias_enc[...], bias_dec[...] = bias_tiles(bias[...])
    esum[...] = jnp.zeros_like(esum)

    def columns(t, count):
        rows = [lambda s, r=t + m: xv[s, r] for m in range(count)]
        for n, halves in enumerate(split_rows(rows, split_ref[...])):
            store_columns(xb, XU + t + n, halves)

    def cotangent(s, count):
        rows = [lambda k, r=2 * s + m: cv[k, r] for m in range(2 * count)]
        halves = split_rows(rows, split_ref[...])
        for n in range(count):
            store_split(seeds, s + n + 2, halves[2 * n : 2 * n + 2], live_lane)

    def encode(u, count):
        for n in range(count):
            encode_row(u + n, I, None, we2, bias_enc[...], xb, l3, slope)

    def decode(w, count):
        for n in range(count):
            decode_row(w + n, True, wd2, bias_dec[...], seeds, l3, d5, value, dsum)

    chunked(0, R, U, columns)
    copies[0].wait()
    we2[...] = we[...].reshape(KERNEL_ROWS, 128).T.astype(BF16)
    chunked(4, I + 2, U, encode)
    copies[1].wait()
    up_weights(wd2, wdt, 1)
    chunked(0, I, U, cotangent)
    chunked(4, I, U, decode)
    wb[...] = jnp.concatenate([wdt[4 - q].reshape(320, 128) for q in range(5)], axis=0).T.astype(BF16)
    acc0[...], acc1[...] = kernel_grad(range(2, I - 2), d5, CH, lambda u: l3[u, 128:256], 2)
    for e in range(4, I - 2):
        back_row(e, True, wb, d5, slope, e_rows, esum)


def outer_kernel(
    R, far, near, we2, wd2, wb, bias_enc, bias_dec, split_ref, live,
    xb_in, l3_in, slope_in, d5_in, value_in, seeds_in, dsum_in, dec0_in, dec1_in, e_rows_in, esum_in,
    keep, send, xb, l3, slope, d5, value, seeds, dsum, dec0, dec1, e_rows, esum, enc0, enc1,
):
    I = R // 2
    core = lax.axis_index("core")
    row_at = lax.axis_index("x") * 2 + core
    ends = row_at == 0, row_at == lax.axis_size("x") * 2 - 1
    live_lane = live[:1]
    count = sum(live_lane[:, n * 64 : n * 64 + 1] for n in range(4))
    upper = core == 0

    def above(r):
        return lambda s: jnp.where(ends[0], jnp.zeros((64, 128), BF16), jnp.where(upper, far[s, r], near[s, r]))

    def below(r):
        return lambda s: jnp.where(ends[1], jnp.zeros((64, 128), BF16), jnp.where(upper, near[s, r], far[s, r]))

    def encoder_grad(rows):
        return kernel_grad(rows, xb, XU, lambda e: e_rows[e], 0)

    rows = [above(r) for r in range(XU)] + [below(r) for r in range(XD)]
    for n, halves in enumerate(split_rows(rows, split_ref[...])):
        store_columns(xb, n if n < XU else R + n, halves)
    halves = split_rows([above(XH + r) for r in range(CH)] + [below(XH + r) for r in range(CH)], split_ref[...])
    for n, w in enumerate((0, 1, I + 2, I + 3)):
        store_split(seeds, w, halves[2 * n : 2 * n + 2], live_lane)
    for u in list(range(4)) + list(range(I + 2, I + 6)):
        encode_row(u, I, ends, we2, bias_enc[...], xb, l3, slope)
    ready = range(4, I - 4)
    if ready:
        enc0[...], enc1[...] = encoder_grad(ready)
    for w in list(range(4)) + list(range(I, I + 4)):
        decode_row(w, 2 <= w < I + 2, wd2, bias_dec[...], seeds, l3, d5, value, dsum)
    even, odd = kernel_grad([0, 1, I - 2, I - 1], d5, CH, lambda u: l3[u, 128:256], 2)
    dec0[...] += even
    dec1[...] += odd
    for e in list(range(4)) + list(range(I - 2, I + 2)):
        back_row(e, 1 <= e < I + 1, wb, d5, slope, e_rows, esum, ends[0] if e == 0 else ends[1])
    even, odd = encoder_grad([s for s in range(I) if s not in ready])
    if ready:
        enc0[...] += even
        enc1[...] += odd
    else:
        enc0[...], enc1[...] = even, odd

    count_row = jnp.broadcast_to(jnp.where(row_at == 0, count, 0.0), (1, 128))
    dec_row = jnp.concatenate([lane_sums(dsum[...]), jnp.zeros((1, 64), F32)], axis=1)
    head = jnp.concatenate([count_row, lane_sums(esum[...]), dec_row, jnp.zeros((HEAD - 3, 128), F32)], axis=0).astype(BF16)
    other_head = jnp.concatenate([count_row, jnp.zeros((HEAD - 1, 128), F32)], axis=0).astype(BF16)
    chunks, chunk_rows = keep.shape[:2]

    def fill(dest, even_acc, odd_acc, even_taps, odd_taps):
        blocks = [(a, even_acc, d) for d, a in enumerate(even_taps)] + [(a, odd_acc, d) for d, a in enumerate(odd_taps)]
        runs = chunk_runs(chunks)
        for a, acc, d in blocks:
            block = acc[:, d * 128 : d * 128 + 128]
            for p, (start, end) in enumerate(runs):
                lo, hi = max(start, a * 320), min(end, a * 320 + 320)
                if lo < hi:
                    dest[p, HEAD + lo - start : HEAD + hi - start] = block[lo - a * 320 : hi - a * 320].astype(BF16)
        for p, (start, end) in enumerate(runs):
            dest[p, :HEAD] = other_head if p else head
            if HEAD + end - start < chunk_rows:
                dest[p, HEAD + end - start :] = jnp.zeros((chunk_rows - HEAD - end + start, 128), BF16)

    def fill_both(enc_dest, dec_dest):
        fill(enc_dest, enc0, enc1, (4, 2, 0), (3, 1))
        fill(dec_dest, dec0, dec1, (0, 2, 4), (1, 3))

    pl.when(core == 0)(lambda: fill_both(keep, send))
    pl.when(core != 0)(lambda: fill_both(send, keep))


def field_copies(R, field, out, sems):
    step = R // 4
    return [pltpu.make_async_copy(field.at[:, n * step : n * step + step], out.at[:, n * step : n * step + step], sems.at[n]) for n in range(4)]


def merge_field(R, value, merge, field, out, sems):
    I = R // 2
    copies = field_copies(R, field, out, sems)
    for n, c in enumerate(copies):
        for s in range(n * I // 4, (n + 1) * I // 4):
            for rho, slots in enumerate(merge_rows(value(s), merge)):
                for k, piece in enumerate(slots):
                    field[k, 2 * s + rho] = piece
        c.start()
    return copies


def output_kernel(R, value, out, field, merge_ref, sems):
    merge_ref[...] = merge_matrix()
    for c in merge_field(R, lambda s: value[s], merge_ref[...], field, out, sems):
        c.wait()


def scatter_kernel(R, U, e_rows, we_hbm, *refs):
    sources, grads, targets, (we, e3, we3, sems) = refs[:6], refs[6], refs[7:13], refs[13:]
    I = R // 2
    fetch = [pltpu.make_async_copy(we_hbm, we, sems.at[6])]
    fetch += [pltpu.make_async_copy(a, b, sems.at[n]) for n, (a, b) in enumerate(zip(sources, targets, strict=True))]
    for c in fetch:
        c.start()

    def widen(e, count):
        for n in range(count):
            v = e_rows[e + n]
            e3[e + n, :128] = column_before(v)
            e3[e + n, 128:256] = v
            e3[e + n, 256:] = column_after(v)

    def scatter(s, count):
        for n in range(count):
            grads[s + n] = up(we3, e3, s + n)

    chunked(0, I + 2, I + 2, widen)
    fetch[0].wait()
    up_weights(we3, we, -1)
    chunked(0, I, U, scatter)
    for c in fetch[1:]:
        c.wait()


def partial_kernel(parts, partial):
    partial[...] = sum(parts[p].astype(F32) for p in range(parts.shape[0])).astype(BF16)


def total_kernel(own, other, wide):
    both = own[...].astype(F32) + other[...].astype(F32)
    for p in range(wide.shape[0]):
        wide[p] = both.astype(BF16)


PARTS = 4


def update_kernel(owner, totals, *refs):
    params, results, staged, sems = refs[:6], refs[-16:-6], refs[-6:-1], refs[-1]
    head = totals[0, :16].astype(F32)
    scale = 1.0 / head[:1]

    def half(n):
        copies, sent = [], 0
        for p, (lo, hi) in enumerate(chunk_runs(totals.shape[0])):
            if lo == hi:
                break
            grad = totals[p, HEAD : HEAD + hi - lo].astype(F32) * scale
            mom, ema, new = advance(grad, *[r[lo:hi] for r in params[3 * n : 3 * n + 3]])
            for ref, v in zip(staged, (grad, mom, ema, new, new.astype(BF16)), strict=True):
                ref[lo:hi] = v
            if hi == KERNEL_ROWS or (hi - sent >= KERNEL_ROWS // PARTS and hi % 16 == 0):
                for m in range(5):
                    c = pltpu.make_async_copy(staged[m].at[sent:hi], results[5 * n + m].at[sent:hi], sems.at[len(copies)])
                    c.start()
                    copies.append(c)
                sent = hi
        for c in copies:
            c.wait()

    core = lax.axis_index("core")
    pl.when(core == owner)(lambda: half(0))
    pl.when(core != owner)(lambda: half(1))


def own_update_kernel(R, totals, *refs):
    params, small, grads, bias_out, ig, rest, (field, merge_ref, sems) = (
        refs[:6], refs[6:9], refs[9], refs[10:15], refs[15], refs[16:-3], refs[-3:],
    )
    head = totals[0, :16].astype(F32)
    scale = 1.0 / head[:1]
    wide_scale = jnp.concatenate([scale] * 2, axis=1)
    merge_ref[...] = merge_matrix()
    copies = merge_field(R, lambda s: (grads[s] * wide_scale).astype(BF16), merge_ref[...], field, ig, sems)
    grad = jnp.concatenate([head[1:2], head[2:3, :64]], axis=1) * scale[:, :1]
    mom, ema, new = advance(grad, *[r[...] for r in small])
    for ref, v in zip(bias_out, (grad, mom, ema, new, new.astype(BF16).reshape(-1)), strict=True):
        ref[...] = v
    update_kernel(0, totals, *params, *rest)
    for c in copies:
        c.wait()


def advance(grad, weight, moment, average):
    moment_new = MOMENTUM * moment + grad
    weight_new = weight - LEARN_RATE * (grad + MOMENTUM * moment_new)
    average_new = EMA_DECAY * average + (1.0 - EMA_DECAY) * weight_new
    return (moment_new, average_new, weight_new)


def on_device(
    snapshots, cotangent, lengths, slot_mask, encoder_kernel, decoder_kernel, biases,
    encoder_mom, decoder_mom, bias_mom, encoder_ema, decoder_ema, bias_ema,
):
    slots, R, C, W = snapshots.shape
    latent_ch = encoder_kernel.shape[3]
    I, U = R // 2, 16
    nx = lax.axis_size("x")
    peers = lax.axis_size("snap") * nx
    swap = [(0, 1), (1, 0)]
    decoder_t = jnp.swapaxes(decoder_kernel, 2, 3)
    vmem, hbm = (pl.BlockSpec(memory_space=m) for m in (pltpu.VMEM, pltpu.HBM))

    def call(kernel, name, megabytes, flops, **kw):
        return pl.pallas_call(
            kernel,
            name=name,
            compiler_params=pltpu.CompilerParams(vmem_limit_bytes=megabytes * 2**20),
            cost_estimate=pl.CostEstimate(flops=flops, bytes_accessed=4 << 20, transcendentals=0),
            **kw,
        )

    def sds(*shape, dtype=BF16):
        return jax.ShapeDtypeStruct(shape, dtype)

    def in_vmem(v):
        return pltpu.with_memory_space_constraint(v, pltpu.VMEM)

    def in_hbm(v):
        return pltpu.with_memory_space_constraint(v, pltpu.HBM)

    conv = 2 * 4096 * 204800
    halo = sds(slots, XH + CH, C, W)
    near, far = call(
        functools.partial(halo_kernel, R), "halo", 4, 0,
        out_shape=[halo, halo],
        in_specs=[hbm] * 2,
        out_specs=[vmem] * 2,
        scratch_shapes=[pltpu.SemaphoreType.DMA((4,))],
    )(in_hbm(snapshots), in_hbm(cotangent))
    far = lax.ppermute(far, ("snap", "x", "core"), far_pairs(lax.axis_size("snap"), nx))
    near = lax.ppermute(near, "core", swap)
    bias_row = biases.reshape(1, -1)

    field = pltpu.HBM(snapshots.shape, BF16)
    state = [
        sds(XU + R + 8, 320, 256), sds(I + 6, 384, 256), sds(I + 2, 128, 256, dtype=F32), sds(R + 8, 320, 256),
        sds(I, 256, 256), sds(I + 4, 256, 256), sds(64, 256, dtype=F32), sds(320, 384, dtype=F32), sds(320, 256, dtype=F32),
        sds(I + 2, 128, 256), sds(128, 256, dtype=F32),
    ]
    shared = [
        sds(128, KERNEL_ROWS), sds(256, 1152), sds(128, KERNEL_ROWS), sds(128, 256, dtype=F32), sds(256, 256, dtype=F32), sds(256, 256),
        sds(8, 256, dtype=F32),
    ]
    parts = call(
        functools.partial(inner_kernel, R, U), "inner", INNER_MB, 2 * conv,
        out_shape=state + shared,
        in_specs=[vmem] * 2 + [hbm] * 2 + [vmem] * 3,
        out_specs=[vmem] * 18,
        scratch_shapes=[
            pltpu.VMEM(encoder_kernel.shape, F32),
            pltpu.VMEM(encoder_kernel.shape, F32),
            pltpu.SemaphoreType.DMA((2,)),
        ],
    )(in_vmem(snapshots), in_vmem(cotangent), in_hbm(encoder_kernel), in_hbm(decoder_t), bias_row, lengths.reshape(1, 1), slot_mask.reshape(1, slots))
    chunk = sds(peers, HEAD + chunk_span(peers), 128)
    keep, send, _, _, _, _, value, _, _, _, _, e_rows, _ = call(
        functools.partial(outer_kernel, R), "outer", OUTER_MB, 4 * conv,
        out_shape=[chunk, chunk] + state,
        in_specs=[vmem] * 20,
        out_specs=[vmem] * 13,
        input_output_aliases={9 + n: 2 + n for n in range(11)},
        scratch_shapes=[pltpu.VMEM((320, 384), F32), pltpu.VMEM((320, 256), F32)],
    )(far, near, *parts[11:], *parts[:11])

    recv = lax.ppermute(send, "core", swap)
    output = call(
        functools.partial(output_kernel, R), "output", FIELD_MB, conv // 4,
        out_shape=field,
        in_specs=[vmem],
        out_specs=hbm,
        scratch_shapes=[pltpu.VMEM(snapshots.shape, BF16), pltpu.VMEM((256, 256), BF16), pltpu.SemaphoreType.DMA((4,))],
    )(value)
    part = (keep.astype(F32) + recv.astype(F32)).astype(BF16)
    part, output = lax.optimization_barrier((part, output))
    parts = lax.all_to_all(part, ("snap", "x"), 0, 0, tiled=True)
    parts, e_rows = lax.optimization_barrier((parts, e_rows))
    own_side = call(partial_kernel, "partial", 4, 0, out_shape=sds(*part.shape[1:]), in_specs=[vmem], out_specs=vmem)(parts)
    other_side = lax.ppermute(own_side, "side", swap)

    def rows(v):
        return v.reshape(KERNEL_ROWS, 128)

    def trows(v):
        return jnp.swapaxes(v, 2, 3).reshape(KERNEL_ROWS, 128)

    params = [
        rows(encoder_kernel), rows(encoder_mom), rows(encoder_ema),
        trows(decoder_kernel), trows(decoder_mom), trows(decoder_ema),
    ]
    shape = (KERNEL_ROWS, 128)
    grads, *params = call(
        functools.partial(scatter_kernel, R, U), "scatter", FIELD_MB, conv,
        out_shape=[sds(I, 256, 256, dtype=F32)] + [sds(*shape, dtype=F32)] * 6,
        in_specs=[vmem] + [hbm] * 7,
        out_specs=[vmem] * 7,
        scratch_shapes=[
            pltpu.VMEM(encoder_kernel.shape, F32),
            pltpu.VMEM((I + 2, 384, 256), BF16),
            pltpu.VMEM((256, 1152), BF16),
            pltpu.SemaphoreType.DMA((7,)),
        ],
    )(e_rows, in_hbm(encoder_kernel), *[in_hbm(v) for v in params])
    other_side, grads, params = lax.optimization_barrier((other_side, grads, params))
    wide = call(total_kernel, "total", 4, 0, out_shape=sds(*part.shape), in_specs=[vmem] * 2, out_specs=vmem)(own_side, other_side)
    mine = lax.all_to_all(wide, ("snap", "x"), 0, 0, tiled=True)
    mine, grads, params = lax.optimization_barrier((mine, grads, params))
    other = lax.ppermute(mine, "core", swap)
    five = [pltpu.HBM(shape, F32)] * 4 + [pltpu.HBM(shape, BF16)]
    staged = [pltpu.VMEM(v.shape, v.dtype) for v in five] + [pltpu.SemaphoreType.DMA((5 * PARTS,))]
    bias_shape = [sds(1, latent_ch + C, dtype=F32)] * 4 + [sds(latent_ch + C)]
    own = call(
        functools.partial(own_update_kernel, R), "update_own", UPDATE_MB, 1 << 20,
        out_shape=bias_shape + [field] + five * 2,
        in_specs=[vmem] * 11,
        out_specs=[vmem] * 5 + [hbm] * 11,
        scratch_shapes=staged + [pltpu.VMEM(snapshots.shape, BF16), pltpu.VMEM((256, 256), BF16), pltpu.SemaphoreType.DMA((4,))],
    )(mine, *params, bias_row, bias_mom.reshape(1, -1), bias_ema.reshape(1, -1), grads)
    bias_results, input_grad, begun = own[:5], own[5], own[6:]
    bias_grad, bia_mom, bia_ema, bia_new, bia_copy = [v.reshape(biases.shape) for v in bias_results]
    results = call(
        functools.partial(update_kernel, 1), "update_other", UPDATE_MB, 1 << 20,
        out_shape=five * 2,
        in_specs=[vmem] * 7 + [hbm] * 10,
        out_specs=[hbm] * 10,
        input_output_aliases={7 + n: n for n in range(10)},
        scratch_shapes=staged,
    )(other, *params, *[in_hbm(v) for v in begun])
    enc_grad, enc_mom, enc_ema, enc_new, enc_copy = [v.reshape(encoder_kernel.shape) for v in results[:5]]
    dec_grad, dec_mom, dec_ema, dec_new, dec_copy = [jnp.swapaxes(v.reshape(decoder_t.shape), 2, 3) for v in results[5:]]
    return (
        output, input_grad, enc_grad, dec_grad, bias_grad, enc_mom, dec_mom, bia_mom,
        enc_ema, dec_ema, bia_ema, enc_new, dec_new, bia_new, enc_copy, dec_copy, bia_copy,
    )


def solution(mesh):
    snap, rows = mesh.devices.shape
    split = Mesh(mesh.devices.reshape(2, snap // 2, rows // 2, 2), ("side", "snap", "x", "core"))
    slots = ("side", "snap")
    field = P(slots, ("x", "core"), None, None)
    return jax.shard_map(
        on_device,
        mesh=split,
        in_specs=(field, field, P(slots), P(slots)) + (P(),) * 9,
        out_specs=(field, field) + (P(),) * 15,
        check_vma=False,
    )
```

```python
import functools

import jax
import jax.numpy as jnp
from jax import lax
from jax.experimental import pallas as pl
from jax.experimental.pallas import tpu as pltpu
from jax.sharding import Mesh, PartitionSpec as P

MOMENTUM = 0.5
EMA_DECAY = 0.5
LEARN_RATE = 0.01
F32, BF16 = jnp.float32, jnp.bfloat16
XH, CH = 8, 4
XU, XD = 8, 7
NT = (((1,), (1,)), ((), ()))
KERNEL_ROWS = 1600
INNER_MB, OUTER_MB, FIELD_MB, UPDATE_MB = 8, 8, 12, 16


HEAD = 8


def chunk_span(peers):
    return -(-KERNEL_ROWS // (8 * peers)) * 8


def chunk_runs(peers):
    span = chunk_span(peers)
    return [(min(KERNEL_ROWS, p * span), min(KERNEL_ROWS, (p + 1) * span)) for p in range(peers)]


def dot(a, b):
    return jnp.dot(a, b, preferred_element_type=F32)


def chunked(lo, hi, size, step):
    whole = (hi - lo) // size
    if whole == 1:
        step(lo, size)
    elif whole:
        pl.loop(0, whole)(lambda n: step(lo + n * size, size))
    rest = (hi - lo) % size
    if rest:
        step(hi - rest, rest)


def split_matrix():
    row = lax.broadcasted_iota(jnp.int32, (256, 256), 0)
    col = lax.broadcasted_iota(jnp.int32, (256, 256), 1)
    want = (col // 64 % 2) * 128 + (col % 64) * 2 + col // 128
    return jnp.where(row == want, 1.0, 0.0).astype(BF16)


def merge_matrix():
    row = lax.broadcasted_iota(jnp.int32, (256, 256), 0)
    col = lax.broadcasted_iota(jnp.int32, (256, 256), 1)
    want = (row // 64 % 2) * 128 + (row % 64) * 2 + row // 128
    return jnp.where(col == want, 1.0, 0.0).astype(BF16)


def column_before(v):
    return shifted(v, 1, 0)


def column_after(v):
    return shifted(v, 127, 63)


def shifted(v, by, edge):
    parts = []
    for h in range(v.shape[1] // 128):
        part = v[:, h * 128 : (h + 1) * 128]
        lane = lax.broadcasted_iota(jnp.int32, part.shape, 1) % 64
        parts.append(jnp.where(lane == edge, jnp.zeros_like(part), pltpu.roll(part, by, axis=1)))
    return parts[0] if len(parts) == 1 else jnp.concatenate(parts, axis=1)


def split_rows(rows, split):
    pieces = [jnp.concatenate([row(2 * h), row(2 * h + 1)], axis=1) for row in rows for h in range(2)]
    y = dot(jnp.concatenate(pieces, axis=0), split)
    out = []
    for n in range(len(rows)):
        a, b = y[n * 128 : n * 128 + 64], y[n * 128 + 64 : n * 128 + 128]
        out.append([jnp.concatenate([a[:, p * 128 : p * 128 + 128], b[:, p * 128 : p * 128 + 128]], axis=1) for p in range(2)])
    return out


def merge_rows(v, merge):
    pieces = [
        jnp.concatenate([v[rho * 128 : rho * 128 + 64, h * 128 : h * 128 + 128], v[rho * 128 + 64 : rho * 128 + 128, h * 128 : h * 128 + 128]], axis=1)
        for rho in range(2)
        for h in range(2)
    ]
    y = dot(jnp.concatenate(pieces, axis=0), merge).astype(BF16)
    return [
        [y[(rho * 2 + n // 2) * 64 : (rho * 2 + n // 2) * 64 + 64, (n % 2) * 128 : (n % 2) * 128 + 128] for n in range(4)]
        for rho in range(2)
    ]


def up_weights(dest, taps, sign):
    for rho in range(2):
        for pi in range(2):
            for di in range(-1, 2):
                for dj in range(-1, 2):
                    a, b = 2 + sign * (2 * di - rho), 2 + sign * (2 * dj - pi)
                    inside = 0 <= a <= 4 and 0 <= b <= 4
                    block = taps[a, b].astype(BF16) if inside else jnp.zeros((64, 128), BF16)
                    r, c = (rho * 2 + pi) * 64, ((di + 1) * 3 + dj + 1) * 128
                    dest[r : r + 64, c : c + 128] = block


def lane_sums(v):
    ones = jnp.ones((8, v.shape[1]), F32)
    return lax.dot_general(ones, v, NT, precision=lax.Precision.HIGHEST, preferred_element_type=F32)[:1]


def store_columns(xb, at, halves):
    even, odd = [v.astype(BF16) for v in halves]
    for b, v in enumerate([column_before(even), column_before(odd), even, odd, column_after(even)]):
        xb[at, b * 64 : b * 64 + 64] = v


def store_split(seeds, at, pair, live_lane):
    for rho, halves in enumerate(pair):
        for pi, v in enumerate(halves):
            row = (rho * 2 + pi) * 64
            seeds[at, row : row + 64] = (v * live_lane).astype(BF16)


def up(weights, rows, at):
    even = dot(weights[:128], rows[pl.ds(at, 3)].reshape(9 * 128, 256))
    odd = dot(weights[128:, 384:], rows[pl.ds(at + 1, 2)].reshape(6 * 128, 256))
    return jnp.concatenate([even, odd], axis=0)


def encode_row(u, I, ends, we2, bias, xb, l3, slope):
    pre = dot(we2[...], xb[pl.ds(2 * u, 5)].reshape(KERNEL_ROWS, 256)) + bias
    grow = jnp.exp(jnp.minimum(pre, 0.0))
    lat = jnp.maximum(pre, grow - 1.0)
    if ends is not None:
        if u < 3:
            lat = jnp.where(ends[0], 0.0, lat)
        if u >= I + 3:
            lat = jnp.where(ends[1], 0.0, lat)
    if ends is None or 2 <= u < I + 4:
        slope[u - 2] = grow
    lat = lat.astype(BF16)
    l3[u, :128] = column_before(lat)
    l3[u, 128:256] = lat
    l3[u, 256:] = column_after(lat)


def decode_row(w, own, wd2, bias, seeds, l3, d5, value, dsum):
    pre = up(wd2, l3, w) + bias
    grow = jnp.exp(jnp.minimum(pre, 0.0))
    if own:
        value[w - 2] = jnp.maximum(pre, grow - 1.0).astype(BF16)
    full = seeds[w].astype(F32) * grow
    if own:
        dsum[...] += (full[:64] + full[64:128]) + (full[128:192] + full[192:])
    back = full.astype(BF16)
    for rho in range(2):
        even, odd = [back[(rho * 2 + pi) * 64 : (rho * 2 + pi) * 64 + 64] for pi in range(2)]
        for b, v in enumerate([column_after(even), odd, even, column_before(odd), column_before(even)]):
            d5[2 * w + rho, b * 64 : b * 64 + 64] = v


def back_row(e, own, wb, d5, slope, e_rows, esum, outside=None):
    v = dot(wb[...], d5[pl.ds(2 * e, 5)].reshape(KERNEL_ROWS, 256)) * slope[e]
    if own:
        esum[...] += v
    else:
        v = jnp.where(outside, 0.0, v)
    e_rows[e] = v.astype(BF16)


def live_lanes(lens, mask):
    lane = lax.broadcasted_iota(jnp.int32, (1, 256), 1)
    length, valid = jnp.broadcast_to(lens, (1, 256)), jnp.zeros((1, 256), jnp.int32)
    for n in range(4):
        valid = jnp.where(lane // 64 == n, jnp.broadcast_to(mask[:, n : n + 1], (1, 256)), valid)
    return jnp.where((lane // 64 < length) & (valid > 0), 1.0, 0.0)


def bias_tiles(bias):
    def column(row):
        count = row.shape[1]
        at = lax.broadcasted_iota(jnp.int32, (count, count), 0)
        to = lax.broadcasted_iota(jnp.int32, (count, count), 1)
        return jnp.sum(jnp.where(at == to, jnp.broadcast_to(row, (count, count)), 0.0), axis=1, keepdims=True)

    enc = column(bias[:, :128])
    dec = column(bias[:, 128:])
    return jnp.broadcast_to(enc, (128, 256)), jnp.broadcast_to(jnp.concatenate([dec] * 4, axis=0), (256, 256))


def far_pairs(groups, nx):
    pairs = []
    for g in range(groups):
        base = g * 2 * nx
        for n in range(nx - 1):
            a, b = base + 2 * n + 1, base + 2 * n + 2
            pairs += [(a, b), (b, a)]
        other = g ^ 1
        if other < groups:
            pairs += [(base, other * 2 * nx), (base + 2 * nx - 1, (other + 1) * 2 * nx - 1)]
    return pairs


def halo_kernel(R, x_hbm, c_hbm, near, far, sems):
    core = lax.axis_index("core")
    copies = []
    for n, (dest, low) in enumerate(((near, core == 0), (far, core == 1))):
        for m, (src, rows, at) in enumerate(((x_hbm, XH, 0), (c_hbm, CH, XH))):
            start = jnp.where(low, R - rows, 0)
            copies.append(pltpu.make_async_copy(src.at[:, pl.ds(start, rows)], dest.at[:, at : at + rows], sems.at[2 * n + m]))
    for c in copies:
        c.start()
    for c in copies:
        c.wait()


def kernel_grad(rows, cols, cols_at, latent, latent_at):
    rhs = jnp.concatenate(
        [jnp.concatenate([latent(latent_at + s + d) for d in range(3)], axis=0) for s in rows], axis=1
    )
    even, odd = [jnp.concatenate([cols[cols_at + 2 * s + rho] for s in rows], axis=1) for rho in range(2)]
    return (
        lax.dot_general(even, rhs, NT, preferred_element_type=F32),
        lax.dot_general(odd, rhs[128:], NT, preferred_element_type=F32),
    )


def inner_kernel(
    R, U, xv, cv, we_hbm, wdt_hbm, bias, lens, mask,
    xb, l3, slope, d5, value, seeds, dsum, acc0, acc1, e_rows, esum, we2, wd2, wb, bias_enc, bias_dec, split_ref, live, we, wdt, sems,
):
    I = R // 2
    copies = [pltpu.make_async_copy(a, b, sems.at[n]) for n, (a, b) in enumerate(((we_hbm, we), (wdt_hbm, wdt)))]
    for c in copies:
        c.start()
    split_ref[...] = split_matrix()
    dsum[...] = jnp.zeros_like(dsum)
    live_lane = live_lanes(lens[...], mask[...])
    live[...] = jnp.broadcast_to(live_lane, live.shape)
    bias_enc[...], bias_dec[...] = bias_tiles(bias[...])
    esum[...] = jnp.zeros_like(esum)

    def columns(t, count):
        rows = [lambda s, r=t + m: xv[s, r] for m in range(count)]
        for n, halves in enumerate(split_rows(rows, split_ref[...])):
            store_columns(xb, XU + t + n, halves)

    def cotangent(s, count):
        rows = [lambda k, r=2 * s + m: cv[k, r] for m in range(2 * count)]
        halves = split_rows(rows, split_ref[...])
        for n in range(count):
            store_split(seeds, s + n + 2, halves[2 * n : 2 * n + 2], live_lane)

    def encode(u, count):
        for n in range(count):
            encode_row(u + n, I, None, we2, bias_enc[...], xb, l3, slope)

    def decode(w, count):
        for n in range(count):
            decode_row(w + n, True, wd2, bias_dec[...], seeds, l3, d5, value, dsum)

    chunked(0, R, U, columns)
    copies[0].wait()
    we2[...] = we[...].reshape(KERNEL_ROWS, 128).T.astype(BF16)
    chunked(4, I + 2, U, encode)
    copies[1].wait()
    up_weights(wd2, wdt, 1)
    chunked(0, I, U, cotangent)
    chunked(4, I, U, decode)
    wb[...] = jnp.concatenate([wdt[4 - q].reshape(320, 128) for q in range(5)], axis=0).T.astype(BF16)
    acc0[...], acc1[...] = kernel_grad(range(2, I - 2), d5, CH, lambda u: l3[u, 128:256], 2)
    for e in range(4, I - 2):
        back_row(e, True, wb, d5, slope, e_rows, esum)


def outer_kernel(
    R, far, near, we2, wd2, wb, bias_enc, bias_dec, split_ref, live,
    xb_in, l3_in, slope_in, d5_in, value_in, seeds_in, dsum_in, dec0_in, dec1_in, e_rows_in, esum_in,
    keep, send, xb, l3, slope, d5, value, seeds, dsum, dec0, dec1, e_rows, esum, enc0, enc1,
):
    I = R // 2
    core = lax.axis_index("core")
    row_at = lax.axis_index("x") * 2 + core
    ends = row_at == 0, row_at == lax.axis_size("x") * 2 - 1
    live_lane = live[:1]
    count = sum(live_lane[:, n * 64 : n * 64 + 1] for n in range(4))
    upper = core == 0

    def above(r):
        return lambda s: jnp.where(ends[0], jnp.zeros((64, 128), BF16), jnp.where(upper, far[s, r], near[s, r]))

    def below(r):
        return lambda s: jnp.where(ends[1], jnp.zeros((64, 128), BF16), jnp.where(upper, near[s, r], far[s, r]))

    def encoder_grad(rows):
        return kernel_grad(rows, xb, XU, lambda e: e_rows[e], 0)

    rows = [above(r) for r in range(XU)] + [below(r) for r in range(XD)]
    for n, halves in enumerate(split_rows(rows, split_ref[...])):
        store_columns(xb, n if n < XU else R + n, halves)
    halves = split_rows([above(XH + r) for r in range(CH)] + [below(XH + r) for r in range(CH)], split_ref[...])
    for n, w in enumerate((0, 1, I + 2, I + 3)):
        store_split(seeds, w, halves[2 * n : 2 * n + 2], live_lane)
    for u in list(range(4)) + list(range(I + 2, I + 6)):
        encode_row(u, I, ends, we2, bias_enc[...], xb, l3, slope)
    ready = range(4, I - 4)
    if ready:
        enc0[...], enc1[...] = encoder_grad(ready)
    for w in list(range(4)) + list(range(I, I + 4)):
        decode_row(w, 2 <= w < I + 2, wd2, bias_dec[...], seeds, l3, d5, value, dsum)
    even, odd = kernel_grad([0, 1, I - 2, I - 1], d5, CH, lambda u: l3[u, 128:256], 2)
    dec0[...] += even
    dec1[...] += odd
    for e in list(range(4)) + list(range(I - 2, I + 2)):
        back_row(e, 1 <= e < I + 1, wb, d5, slope, e_rows, esum, ends[0] if e == 0 else ends[1])
    even, odd = encoder_grad([s for s in range(I) if s not in ready])
    if ready:
        enc0[...] += even
        enc1[...] += odd
    else:
        enc0[...], enc1[...] = even, odd

    count_row = jnp.broadcast_to(jnp.where(row_at == 0, count, 0.0), (1, 128))
    dec_row = jnp.concatenate([lane_sums(dsum[...]), jnp.zeros((1, 64), F32)], axis=1)
    head = jnp.concatenate([count_row, lane_sums(esum[...]), dec_row, jnp.zeros((HEAD - 3, 128), F32)], axis=0).astype(BF16)
    other_head = jnp.concatenate([count_row, jnp.zeros((HEAD - 1, 128), F32)], axis=0).astype(BF16)
    chunks, chunk_rows = keep.shape[:2]

    def fill(dest, even_acc, odd_acc, even_taps, odd_taps):
        blocks = [(a, even_acc, d) for d, a in enumerate(even_taps)] + [(a, odd_acc, d) for d, a in enumerate(odd_taps)]
        runs = chunk_runs(chunks)
        for a, acc, d in blocks:
            block = acc[:, d * 128 : d * 128 + 128]
            for p, (start, end) in enumerate(runs):
                lo, hi = max(start, a * 320), min(end, a * 320 + 320)
                if lo < hi:
                    dest[p, HEAD + lo - start : HEAD + hi - start] = block[lo - a * 320 : hi - a * 320].astype(BF16)
        for p, (start, end) in enumerate(runs):
            dest[p, :HEAD] = other_head if p else head
            if HEAD + end - start < chunk_rows:
                dest[p, HEAD + end - start :] = jnp.zeros((chunk_rows - HEAD - end + start, 128), BF16)

    def fill_both(enc_dest, dec_dest):
        fill(enc_dest, enc0, enc1, (4, 2, 0), (3, 1))
        fill(dec_dest, dec0, dec1, (0, 2, 4), (1, 3))

    pl.when(core == 0)(lambda: fill_both(keep, send))
    pl.when(core != 0)(lambda: fill_both(send, keep))


def field_copies(R, field, out, sems):
    step = R // 4
    return [pltpu.make_async_copy(field.at[:, n * step : n * step + step], out.at[:, n * step : n * step + step], sems.at[n]) for n in range(4)]


def merge_field(R, value, merge, field, out, sems):
    I = R // 2
    copies = field_copies(R, field, out, sems)
    for n, c in enumerate(copies):
        for s in range(n * I // 4, (n + 1) * I // 4):
            for rho, slots in enumerate(merge_rows(value(s), merge)):
                for k, piece in enumerate(slots):
                    field[k, 2 * s + rho] = piece
        c.start()
    return copies


def output_kernel(R, value, out, field, merge_ref, sems):
    merge_ref[...] = merge_matrix()
    for c in merge_field(R, lambda s: value[s], merge_ref[...], field, out, sems):
        c.wait()


def scatter_kernel(R, U, e_rows, we_hbm, *refs):
    sources, grads, targets, (we, e3, we3, sems) = refs[:6], refs[6], refs[7:13], refs[13:]
    I = R // 2
    fetch = [pltpu.make_async_copy(we_hbm, we, sems.at[6])]
    fetch += [pltpu.make_async_copy(a, b, sems.at[n]) for n, (a, b) in enumerate(zip(sources, targets, strict=True))]
    for c in fetch:
        c.start()

    def widen(e, count):
        for n in range(count):
            v = e_rows[e + n]
            e3[e + n, :128] = column_before(v)
            e3[e + n, 128:256] = v
            e3[e + n, 256:] = column_after(v)

    def scatter(s, count):
        for n in range(count):
            grads[s + n] = up(we3, e3, s + n)

    chunked(0, I + 2, I + 2, widen)
    fetch[0].wait()
    up_weights(we3, we, -1)
    chunked(0, I, U, scatter)
    for c in fetch[1:]:
        c.wait()


def partial_kernel(parts, partial):
    partial[...] = sum(parts[p].astype(F32) for p in range(parts.shape[0])).astype(BF16)


def total_kernel(own, other, wide):
    both = own[...].astype(F32) + other[...].astype(F32)
    for p in range(wide.shape[0]):
        wide[p] = both.astype(BF16)


PARTS = 4


def update_kernel(owner, totals, *refs):
    params, results, staged, sems = refs[:6], refs[-16:-6], refs[-6:-1], refs[-1]
    head = totals[0, :16].astype(F32)
    scale = 1.0 / head[:1]

    def half(n):
        copies, sent = [], 0
        for p, (lo, hi) in enumerate(chunk_runs(totals.shape[0])):
            if lo == hi:
                break
            grad = totals[p, HEAD : HEAD + hi - lo].astype(F32) * scale
            mom, ema, new = advance(grad, *[r[lo:hi] for r in params[3 * n : 3 * n + 3]])
            for ref, v in zip(staged, (grad, mom, ema, new, new.astype(BF16)), strict=True):
                ref[lo:hi] = v
            if hi == KERNEL_ROWS or (hi - sent >= KERNEL_ROWS // PARTS and hi % 16 == 0):
                for m in range(5):
                    c = pltpu.make_async_copy(staged[m].at[sent:hi], results[5 * n + m].at[sent:hi], sems.at[len(copies)])
                    c.start()
                    copies.append(c)
                sent = hi
        for c in copies:
            c.wait()

    core = lax.axis_index("core")
    pl.when(core == owner)(lambda: half(0))
    pl.when(core != owner)(lambda: half(1))


def own_update_kernel(R, totals, *refs):
    params, small, grads, bias_out, ig, rest, (field, merge_ref, sems), bias_ref, bias_sems = (
        refs[:6], refs[6:9], refs[9], refs[10:15], refs[15], refs[16:32], refs[32:35], refs[35:40], refs[40],
    )
    head = totals[0, :16].astype(F32)
    scale = 1.0 / head[:1]
    wide_scale = jnp.concatenate([scale] * 2, axis=1)
    merge_ref[...] = merge_matrix()
    grad = jnp.concatenate([head[1:2], head[2:3, :64]], axis=1) * scale[:, :1]
    mom, ema, new = advance(grad, *[r[...] for r in small])
    copies = []
    for n, v in enumerate((grad, mom, ema, new, new.astype(BF16).reshape(-1))):
        bias_ref[n][...] = v
        copies.append(pltpu.make_async_copy(bias_ref[n], bias_out[n], bias_sems.at[n]))
        copies[-1].start()
    copies += merge_field(R, lambda s: (grads[s] * wide_scale).astype(BF16), merge_ref[...], field, ig, sems)
    update_kernel(0, totals, *params, *rest)
    for c in copies:
        c.wait()


def advance(grad, weight, moment, average):
    moment_new = MOMENTUM * moment + grad
    weight_new = weight - LEARN_RATE * (grad + MOMENTUM * moment_new)
    average_new = EMA_DECAY * average + (1.0 - EMA_DECAY) * weight_new
    return (moment_new, average_new, weight_new)


def on_device(
    snapshots, cotangent, lengths, slot_mask, encoder_kernel, decoder_kernel, biases,
    encoder_mom, decoder_mom, bias_mom, encoder_ema, decoder_ema, bias_ema,
):
    slots, R, C, W = snapshots.shape
    latent_ch = encoder_kernel.shape[3]
    I, U = R // 2, 16
    nx = lax.axis_size("x")
    peers = lax.axis_size("snap") * nx
    swap = [(0, 1), (1, 0)]
    decoder_t = jnp.swapaxes(decoder_kernel, 2, 3)
    vmem, hbm = (pl.BlockSpec(memory_space=m) for m in (pltpu.VMEM, pltpu.HBM))

    def call(kernel, name, megabytes, flops, **kw):
        return pl.pallas_call(
            kernel,
            name=name,
            compiler_params=pltpu.CompilerParams(vmem_limit_bytes=megabytes * 2**20),
            cost_estimate=pl.CostEstimate(flops=flops, bytes_accessed=4 << 20, transcendentals=0),
            **kw,
        )

    def sds(*shape, dtype=BF16):
        return jax.ShapeDtypeStruct(shape, dtype)

    def in_vmem(v):
        return pltpu.with_memory_space_constraint(v, pltpu.VMEM)

    def in_hbm(v):
        return pltpu.with_memory_space_constraint(v, pltpu.HBM)

    conv = 2 * 4096 * 204800
    halo = sds(slots, XH + CH, C, W)
    near, far = call(
        functools.partial(halo_kernel, R), "halo", 4, 0,
        out_shape=[halo, halo],
        in_specs=[hbm] * 2,
        out_specs=[vmem] * 2,
        scratch_shapes=[pltpu.SemaphoreType.DMA((4,))],
    )(in_hbm(snapshots), in_hbm(cotangent))
    far = lax.ppermute(far, ("snap", "x", "core"), far_pairs(lax.axis_size("snap"), nx))
    near = lax.ppermute(near, "core", swap)
    bias_row = biases.reshape(1, -1)

    field = pltpu.HBM(snapshots.shape, BF16)
    state = [
        sds(XU + R + 8, 320, 256), sds(I + 6, 384, 256), sds(I + 2, 128, 256, dtype=F32), sds(R + 8, 320, 256),
        sds(I, 256, 256), sds(I + 4, 256, 256), sds(64, 256, dtype=F32), sds(320, 384, dtype=F32), sds(320, 256, dtype=F32),
        sds(I + 2, 128, 256), sds(128, 256, dtype=F32),
    ]
    shared = [
        sds(128, KERNEL_ROWS), sds(256, 1152), sds(128, KERNEL_ROWS), sds(128, 256, dtype=F32), sds(256, 256, dtype=F32), sds(256, 256),
        sds(8, 256, dtype=F32),
    ]
    parts = call(
        functools.partial(inner_kernel, R, U), "inner", INNER_MB, 2 * conv,
        out_shape=state + shared,
        in_specs=[vmem] * 2 + [hbm] * 2 + [vmem] * 3,
        out_specs=[vmem] * 18,
        scratch_shapes=[
            pltpu.VMEM(encoder_kernel.shape, F32),
            pltpu.VMEM(encoder_kernel.shape, F32),
            pltpu.SemaphoreType.DMA((2,)),
        ],
    )(in_vmem(snapshots), in_vmem(cotangent), in_hbm(encoder_kernel), in_hbm(decoder_t), bias_row, lengths.reshape(1, 1), slot_mask.reshape(1, slots))
    chunk = sds(peers, HEAD + chunk_span(peers), 128)
    keep, send, _, _, _, _, value, _, _, _, _, e_rows, _ = call(
        functools.partial(outer_kernel, R), "outer", OUTER_MB, 4 * conv,
        out_shape=[chunk, chunk] + state,
        in_specs=[vmem] * 20,
        out_specs=[vmem] * 13,
        input_output_aliases={9 + n: 2 + n for n in range(11)},
        scratch_shapes=[pltpu.VMEM((320, 384), F32), pltpu.VMEM((320, 256), F32)],
    )(far, near, *parts[11:], *parts[:11])

    recv = lax.ppermute(send, "core", swap)
    output = call(
        functools.partial(output_kernel, R), "output", FIELD_MB, conv // 4,
        out_shape=field,
        in_specs=[vmem],
        out_specs=hbm,
        scratch_shapes=[pltpu.VMEM(snapshots.shape, BF16), pltpu.VMEM((256, 256), BF16), pltpu.SemaphoreType.DMA((4,))],
    )(value)
    part = (keep.astype(F32) + recv.astype(F32)).astype(BF16)
    part, output = lax.optimization_barrier((part, output))
    parts = lax.all_to_all(part, ("snap", "x"), 0, 0, tiled=True)
    parts, e_rows = lax.optimization_barrier((parts, e_rows))
    own_side = call(partial_kernel, "partial", 4, 0, out_shape=sds(*part.shape[1:]), in_specs=[vmem], out_specs=vmem)(parts)
    other_side = lax.ppermute(own_side, "side", swap)

    def rows(v):
        return v.reshape(KERNEL_ROWS, 128)

    def trows(v):
        return jnp.swapaxes(v, 2, 3).reshape(KERNEL_ROWS, 128)

    params = [
        rows(encoder_kernel), rows(encoder_mom), rows(encoder_ema),
        trows(decoder_kernel), trows(decoder_mom), trows(decoder_ema),
    ]
    shape = (KERNEL_ROWS, 128)
    grads, *params = call(
        functools.partial(scatter_kernel, R, U), "scatter", FIELD_MB, conv,
        out_shape=[sds(I, 256, 256, dtype=F32)] + [sds(*shape, dtype=F32)] * 6,
        in_specs=[vmem] + [hbm] * 7,
        out_specs=[vmem] * 7,
        scratch_shapes=[
            pltpu.VMEM(encoder_kernel.shape, F32),
            pltpu.VMEM((I + 2, 384, 256), BF16),
            pltpu.VMEM((256, 1152), BF16),
            pltpu.SemaphoreType.DMA((7,)),
        ],
    )(e_rows, in_hbm(encoder_kernel), *[in_hbm(v) for v in params])
    other_side, grads, params = lax.optimization_barrier((other_side, grads, params))
    wide = call(total_kernel, "total", 4, 0, out_shape=sds(*part.shape), in_specs=[vmem] * 2, out_specs=vmem)(own_side, other_side)
    mine = lax.all_to_all(wide, ("snap", "x"), 0, 0, tiled=True)
    mine, grads, params = lax.optimization_barrier((mine, grads, params))
    other = lax.ppermute(mine, "core", swap)
    five = [pltpu.HBM(shape, F32)] * 4 + [pltpu.HBM(shape, BF16)]
    staged = [pltpu.VMEM(v.shape, v.dtype) for v in five] + [pltpu.SemaphoreType.DMA((5 * PARTS,))]
    bias_shape = [pltpu.HBM((1, latent_ch + C), F32)] * 4 + [pltpu.HBM((latent_ch + C,), BF16)]
    own = call(
        functools.partial(own_update_kernel, R), "update_own", UPDATE_MB, 1 << 20,
        out_shape=bias_shape + [field] + five * 2,
        in_specs=[vmem] * 11,
        out_specs=[hbm] * 16,
        scratch_shapes=staged
        + [pltpu.VMEM(snapshots.shape, BF16), pltpu.VMEM((256, 256), BF16), pltpu.SemaphoreType.DMA((4,))]
        + [pltpu.VMEM(v.shape, v.dtype) for v in bias_shape]
        + [pltpu.SemaphoreType.DMA((5,))],
    )(mine, *params, bias_row, bias_mom.reshape(1, -1), bias_ema.reshape(1, -1), grads)
    bias_results, input_grad, begun = own[:5], own[5], own[6:]
    bias_grad, bia_mom, bia_ema, bia_new, bia_copy = [v.reshape(biases.shape) for v in bias_results]
    results = call(
        functools.partial(update_kernel, 1), "update_other", UPDATE_MB, 1 << 20,
        out_shape=five * 2,
        in_specs=[vmem] * 7 + [hbm] * 10,
        out_specs=[hbm] * 10,
        input_output_aliases={7 + n: n for n in range(10)},
        scratch_shapes=staged,
    )(other, *params, *[in_hbm(v) for v in begun])
    enc_grad, enc_mom, enc_ema, enc_new, enc_copy = [v.reshape(encoder_kernel.shape) for v in results[:5]]
    dec_grad, dec_mom, dec_ema, dec_new, dec_copy = [jnp.swapaxes(v.reshape(decoder_t.shape), 2, 3) for v in results[5:]]
    return (
        output, input_grad, enc_grad, dec_grad, bias_grad, enc_mom, dec_mom, bia_mom,
        enc_ema, dec_ema, bia_ema, enc_new, dec_new, bia_new, enc_copy, dec_copy, bia_copy,
    )


def solution(mesh):
    snap, rows = mesh.devices.shape
    split = Mesh(mesh.devices.reshape(2, snap // 2, rows // 2, 2), ("side", "snap", "x", "core"))
    slots = ("side", "snap")
    field = P(slots, ("x", "core"), None, None)
    return jax.shard_map(
        on_device,
        mesh=split,
        in_specs=(field, field, P(slots), P(slots)) + (P(),) * 9,
        out_specs=(field, field) + (P(),) * 15,
        check_vma=False,
    )
```

```python
import functools

import jax
import jax.numpy as jnp
from jax import lax
from jax.experimental import pallas as pl
from jax.experimental.pallas import tpu as pltpu
from jax.sharding import Mesh, PartitionSpec as P

MOMENTUM = 0.5
EMA_DECAY = 0.5
LEARN_RATE = 0.01
F32, BF16 = jnp.float32, jnp.bfloat16
XH, CH = 8, 4
XU, XD = 8, 7
NT = (((1,), (1,)), ((), ()))
KERNEL_ROWS = 1600
INNER_MB, OUTER_MB, FIELD_MB, UPDATE_MB = 8, 8, 12, 16


HEAD = 8


def chunk_span(peers):
    return -(-KERNEL_ROWS // (8 * peers)) * 8


def chunk_runs(peers):
    span = chunk_span(peers)
    return [(min(KERNEL_ROWS, p * span), min(KERNEL_ROWS, (p + 1) * span)) for p in range(peers)]


def dot(a, b):
    return jnp.dot(a, b, preferred_element_type=F32)


def chunked(lo, hi, size, step):
    whole = (hi - lo) // size
    if whole == 1:
        step(lo, size)
    elif whole:
        pl.loop(0, whole)(lambda n: step(lo + n * size, size))
    rest = (hi - lo) % size
    if rest:
        step(hi - rest, rest)


def split_matrix():
    row = lax.broadcasted_iota(jnp.int32, (256, 256), 0)
    col = lax.broadcasted_iota(jnp.int32, (256, 256), 1)
    want = (col // 64 % 2) * 128 + (col % 64) * 2 + col // 128
    return jnp.where(row == want, 1.0, 0.0).astype(BF16)


def merge_matrix():
    row = lax.broadcasted_iota(jnp.int32, (256, 256), 0)
    col = lax.broadcasted_iota(jnp.int32, (256, 256), 1)
    want = (row // 64 % 2) * 128 + (row % 64) * 2 + row // 128
    return jnp.where(col == want, 1.0, 0.0).astype(BF16)


def column_before(v):
    return shifted(v, 1, 0)


def column_after(v):
    return shifted(v, 127, 63)


def shifted(v, by, edge):
    parts = []
    for h in range(v.shape[1] // 128):
        part = v[:, h * 128 : (h + 1) * 128]
        lane = lax.broadcasted_iota(jnp.int32, part.shape, 1) % 64
        parts.append(jnp.where(lane == edge, jnp.zeros_like(part), pltpu.roll(part, by, axis=1)))
    return parts[0] if len(parts) == 1 else jnp.concatenate(parts, axis=1)


def split_rows(rows, split):
    pieces = [jnp.concatenate([row(2 * h), row(2 * h + 1)], axis=1) for row in rows for h in range(2)]
    y = dot(jnp.concatenate(pieces, axis=0), split)
    out = []
    for n in range(len(rows)):
        a, b = y[n * 128 : n * 128 + 64], y[n * 128 + 64 : n * 128 + 128]
        out.append([jnp.concatenate([a[:, p * 128 : p * 128 + 128], b[:, p * 128 : p * 128 + 128]], axis=1) for p in range(2)])
    return out


def merge_rows(v, merge):
    pieces = [
        jnp.concatenate([v[rho * 128 : rho * 128 + 64, h * 128 : h * 128 + 128], v[rho * 128 + 64 : rho * 128 + 128, h * 128 : h * 128 + 128]], axis=1)
        for rho in range(2)
        for h in range(2)
    ]
    y = dot(jnp.concatenate(pieces, axis=0), merge).astype(BF16)
    return [
        [y[(rho * 2 + n // 2) * 64 : (rho * 2 + n // 2) * 64 + 64, (n % 2) * 128 : (n % 2) * 128 + 128] for n in range(4)]
        for rho in range(2)
    ]


def up_weights(dest, taps, sign):
    for rho in range(2):
        for pi in range(2):
            for di in range(-1, 2):
                for dj in range(-1, 2):
                    a, b = 2 + sign * (2 * di - rho), 2 + sign * (2 * dj - pi)
                    inside = 0 <= a <= 4 and 0 <= b <= 4
                    block = taps[a, b].astype(BF16) if inside else jnp.zeros((64, 128), BF16)
                    r, c = (rho * 2 + pi) * 64, ((di + 1) * 3 + dj + 1) * 128
                    dest[r : r + 64, c : c + 128] = block


def lane_sums(v):
    ones = jnp.ones((8, v.shape[1]), F32)
    return lax.dot_general(ones, v, NT, precision=lax.Precision.HIGHEST, preferred_element_type=F32)[:1]


def store_columns(xb, at, halves):
    even, odd = [v.astype(BF16) for v in halves]
    for b, v in enumerate([column_before(even), column_before(odd), even, odd, column_after(even)]):
        xb[at, b * 64 : b * 64 + 64] = v


def store_split(seeds, at, pair, live_lane):
    for rho, halves in enumerate(pair):
        for pi, v in enumerate(halves):
            row = (rho * 2 + pi) * 64
            seeds[at, row : row + 64] = (v * live_lane).astype(BF16)


def up(weights, rows, at):
    even = dot(weights[:128], rows[pl.ds(at, 3)].reshape(9 * 128, 256))
    odd = dot(weights[128:, 384:], rows[pl.ds(at + 1, 2)].reshape(6 * 128, 256))
    return jnp.concatenate([even, odd], axis=0)


def encode_row(u, I, ends, we2, bias, xb, l3, slope):
    pre = dot(we2[...], xb[pl.ds(2 * u, 5)].reshape(KERNEL_ROWS, 256)) + bias
    grow = jnp.exp(jnp.minimum(pre, 0.0))
    lat = jnp.maximum(pre, grow - 1.0)
    if ends is not None:
        if u < 3:
            lat = jnp.where(ends[0], 0.0, lat)
        if u >= I + 3:
            lat = jnp.where(ends[1], 0.0, lat)
    if ends is None or 2 <= u < I + 4:
        slope[u - 2] = grow
    lat = lat.astype(BF16)
    l3[u, :128] = column_before(lat)
    l3[u, 128:256] = lat
    l3[u, 256:] = column_after(lat)


def decode_row(w, own, wd2, bias, seeds, l3, d5, value, dsum):
    pre = up(wd2, l3, w) + bias
    grow = jnp.exp(jnp.minimum(pre, 0.0))
    if own:
        value[w - 2] = jnp.maximum(pre, grow - 1.0).astype(BF16)
    full = seeds[w].astype(F32) * grow
    if own:
        dsum[...] += (full[:64] + full[64:128]) + (full[128:192] + full[192:])
    back = full.astype(BF16)
    for rho in range(2):
        even, odd = [back[(rho * 2 + pi) * 64 : (rho * 2 + pi) * 64 + 64] for pi in range(2)]
        for b, v in enumerate([column_after(even), odd, even, column_before(odd), column_before(even)]):
            d5[2 * w + rho, b * 64 : b * 64 + 64] = v


def back_row(e, own, wb, d5, slope, e_rows, esum, outside=None):
    v = dot(wb[...], d5[pl.ds(2 * e, 5)].reshape(KERNEL_ROWS, 256)) * slope[e]
    if own:
        esum[...] += v
    else:
        v = jnp.where(outside, 0.0, v)
    e_rows[e] = v.astype(BF16)


def live_lanes(lens, mask):
    lane = lax.broadcasted_iota(jnp.int32, (1, 256), 1)
    length, valid = jnp.broadcast_to(lens, (1, 256)), jnp.zeros((1, 256), jnp.int32)
    for n in range(4):
        valid = jnp.where(lane // 64 == n, jnp.broadcast_to(mask[:, n : n + 1], (1, 256)), valid)
    return jnp.where((lane // 64 < length) & (valid > 0), 1.0, 0.0)


def bias_tiles(bias):
    def column(row):
        count = row.shape[1]
        at = lax.broadcasted_iota(jnp.int32, (count, count), 0)
        to = lax.broadcasted_iota(jnp.int32, (count, count), 1)
        return jnp.sum(jnp.where(at == to, jnp.broadcast_to(row, (count, count)), 0.0), axis=1, keepdims=True)

    enc = column(bias[:, :128])
    dec = column(bias[:, 128:])
    return jnp.broadcast_to(enc, (128, 256)), jnp.broadcast_to(jnp.concatenate([dec] * 4, axis=0), (256, 256))


def far_pairs(groups, nx):
    pairs = []
    for g in range(groups):
        base = g * 2 * nx
        for n in range(nx - 1):
            a, b = base + 2 * n + 1, base + 2 * n + 2
            pairs += [(a, b), (b, a)]
        other = g ^ 1
        if other < groups:
            pairs += [(base, other * 2 * nx), (base + 2 * nx - 1, (other + 1) * 2 * nx - 1)]
    return pairs


def halo_kernel(R, x_hbm, c_hbm, near, far, sems):
    core = lax.axis_index("core")
    copies = []
    for n, (dest, low) in enumerate(((near, core == 0), (far, core == 1))):
        for m, (src, rows, at) in enumerate(((x_hbm, XH, 0), (c_hbm, CH, XH))):
            start = jnp.where(low, R - rows, 0)
            copies.append(pltpu.make_async_copy(src.at[:, pl.ds(start, rows)], dest.at[:, at : at + rows], sems.at[2 * n + m]))
    for c in copies:
        c.start()
    for c in copies:
        c.wait()


def kernel_grad(rows, cols, cols_at, latent, latent_at):
    rhs = jnp.concatenate(
        [jnp.concatenate([latent(latent_at + s + d) for d in range(3)], axis=0) for s in rows], axis=1
    )
    even, odd = [jnp.concatenate([cols[cols_at + 2 * s + rho] for s in rows], axis=1) for rho in range(2)]
    return (
        lax.dot_general(even, rhs, NT, preferred_element_type=F32),
        lax.dot_general(odd, rhs[128:], NT, preferred_element_type=F32),
    )


def inner_kernel(
    R, U, xv, cv, we_hbm, wdt_hbm, bias, lens, mask,
    xb, l3, slope, d5, value, seeds, dsum, acc0, acc1, e_rows, esum, we2, wd2, wb, bias_enc, bias_dec, split_ref, live, we, wdt, sems,
):
    I = R // 2
    copies = [pltpu.make_async_copy(a, b, sems.at[n]) for n, (a, b) in enumerate(((we_hbm, we), (wdt_hbm, wdt)))]
    for c in copies:
        c.start()
    split_ref[...] = split_matrix()
    dsum[...] = jnp.zeros_like(dsum)
    live_lane = live_lanes(lens[...], mask[...])
    live[...] = jnp.broadcast_to(live_lane, live.shape)
    bias_enc[...], bias_dec[...] = bias_tiles(bias[...])
    esum[...] = jnp.zeros_like(esum)

    def columns(t, count):
        rows = [lambda s, r=t + m: xv[s, r] for m in range(count)]
        for n, halves in enumerate(split_rows(rows, split_ref[...])):
            store_columns(xb, XU + t + n, halves)

    def cotangent(s, count):
        rows = [lambda k, r=2 * s + m: cv[k, r] for m in range(2 * count)]
        halves = split_rows(rows, split_ref[...])
        for n in range(count):
            store_split(seeds, s + n + 2, halves[2 * n : 2 * n + 2], live_lane)

    def encode(u, count):
        for n in range(count):
            encode_row(u + n, I, None, we2, bias_enc[...], xb, l3, slope)

    def decode(w, count):
        for n in range(count):
            decode_row(w + n, True, wd2, bias_dec[...], seeds, l3, d5, value, dsum)

    chunked(0, R, U, columns)
    copies[0].wait()
    we2[...] = we[...].reshape(KERNEL_ROWS, 128).T.astype(BF16)
    chunked(4, I + 2, U, encode)
    copies[1].wait()
    up_weights(wd2, wdt, 1)
    chunked(0, I, U, cotangent)
    chunked(4, I, U, decode)
    wb[...] = jnp.concatenate([wdt[4 - q].reshape(320, 128) for q in range(5)], axis=0).T.astype(BF16)
    acc0[...], acc1[...] = kernel_grad(range(2, I - 2), d5, CH, lambda u: l3[u, 128:256], 2)
    for e in range(4, I - 2):
        back_row(e, True, wb, d5, slope, e_rows, esum)


def outer_kernel(
    R, far, near, we2, wd2, wb, bias_enc, bias_dec, split_ref, live,
    xb_in, l3_in, slope_in, d5_in, value_in, seeds_in, dsum_in, dec0_in, dec1_in, e_rows_in, esum_in,
    keep, send, xb, l3, slope, d5, value, seeds, dsum, dec0, dec1, e_rows, esum, enc0, enc1,
):
    I = R // 2
    core = lax.axis_index("core")
    row_at = lax.axis_index("x") * 2 + core
    ends = row_at == 0, row_at == lax.axis_size("x") * 2 - 1
    live_lane = live[:1]
    count = sum(live_lane[:, n * 64 : n * 64 + 1] for n in range(4))
    upper = core == 0

    def above(r):
        return lambda s: jnp.where(ends[0], jnp.zeros((64, 128), BF16), jnp.where(upper, far[s, r], near[s, r]))

    def below(r):
        return lambda s: jnp.where(ends[1], jnp.zeros((64, 128), BF16), jnp.where(upper, near[s, r], far[s, r]))

    def encoder_grad(rows):
        return kernel_grad(rows, xb, XU, lambda e: e_rows[e], 0)

    rows = [above(r) for r in range(XU)] + [below(r) for r in range(XD)]
    for n, halves in enumerate(split_rows(rows, split_ref[...])):
        store_columns(xb, n if n < XU else R + n, halves)
    halves = split_rows([above(XH + r) for r in range(CH)] + [below(XH + r) for r in range(CH)], split_ref[...])
    for n, w in enumerate((0, 1, I + 2, I + 3)):
        store_split(seeds, w, halves[2 * n : 2 * n + 2], live_lane)
    for u in list(range(4)) + list(range(I + 2, I + 6)):
        encode_row(u, I, ends, we2, bias_enc[...], xb, l3, slope)
    ready = range(4, I - 4)
    if ready:
        enc0[...], enc1[...] = encoder_grad(ready)
    for w in list(range(4)) + list(range(I, I + 4)):
        decode_row(w, 2 <= w < I + 2, wd2, bias_dec[...], seeds, l3, d5, value, dsum)
    even, odd = kernel_grad([0, 1, I - 2, I - 1], d5, CH, lambda u: l3[u, 128:256], 2)
    dec0[...] += even
    dec1[...] += odd
    for e in list(range(4)) + list(range(I - 2, I + 2)):
        back_row(e, 1 <= e < I + 1, wb, d5, slope, e_rows, esum, ends[0] if e == 0 else ends[1])
    even, odd = encoder_grad([s for s in range(I) if s not in ready])
    if ready:
        enc0[...] += even
        enc1[...] += odd
    else:
        enc0[...], enc1[...] = even, odd

    count_row = jnp.broadcast_to(jnp.where(row_at == 0, count, 0.0), (1, 128))
    dec_row = jnp.concatenate([lane_sums(dsum[...]), jnp.zeros((1, 64), F32)], axis=1)
    head = jnp.concatenate([count_row, lane_sums(esum[...]), dec_row, jnp.zeros((HEAD - 3, 128), F32)], axis=0).astype(BF16)
    other_head = jnp.concatenate([count_row, jnp.zeros((HEAD - 1, 128), F32)], axis=0).astype(BF16)
    chunks, chunk_rows = keep.shape[:2]

    def fill(dest, even_acc, odd_acc, even_taps, odd_taps):
        blocks = [(a, even_acc, d) for d, a in enumerate(even_taps)] + [(a, odd_acc, d) for d, a in enumerate(odd_taps)]
        runs = chunk_runs(chunks)
        for a, acc, d in blocks:
            block = acc[:, d * 128 : d * 128 + 128]
            for p, (start, end) in enumerate(runs):
                lo, hi = max(start, a * 320), min(end, a * 320 + 320)
                if lo < hi:
                    dest[p, HEAD + lo - start : HEAD + hi - start] = block[lo - a * 320 : hi - a * 320].astype(BF16)
        for p, (start, end) in enumerate(runs):
            dest[p, :HEAD] = other_head if p else head
            if HEAD + end - start < chunk_rows:
                dest[p, HEAD + end - start :] = jnp.zeros((chunk_rows - HEAD - end + start, 128), BF16)

    def fill_both(enc_dest, dec_dest):
        fill(enc_dest, enc0, enc1, (4, 2, 0), (3, 1))
        fill(dec_dest, dec0, dec1, (0, 2, 4), (1, 3))

    pl.when(core == 0)(lambda: fill_both(keep, send))
    pl.when(core != 0)(lambda: fill_both(send, keep))


def field_copies(R, field, out, sems):
    step = R // 4
    return [pltpu.make_async_copy(field.at[:, n * step : n * step + step], out.at[:, n * step : n * step + step], sems.at[n]) for n in range(4)]


def merge_field(R, value, merge, field, out, sems):
    I = R // 2
    copies = field_copies(R, field, out, sems)
    for n, c in enumerate(copies):
        for s in range(n * I // 4, (n + 1) * I // 4):
            for rho, slots in enumerate(merge_rows(value(s), merge)):
                for k, piece in enumerate(slots):
                    field[k, 2 * s + rho] = piece
        c.start()
    return copies


def output_kernel(R, value, out, field, merge_ref, sems):
    merge_ref[...] = merge_matrix()
    for c in merge_field(R, lambda s: value[s], merge_ref[...], field, out, sems):
        c.wait()


def scatter_kernel(R, U, e_rows, we_hbm, *refs):
    sources, grads, targets, (we, e3, we3, sems) = refs[:6], refs[6], refs[7:13], refs[13:]
    I = R // 2
    fetch = [pltpu.make_async_copy(we_hbm, we, sems.at[6])]
    fetch += [pltpu.make_async_copy(a, b, sems.at[n]) for n, (a, b) in enumerate(zip(sources, targets, strict=True))]
    for c in fetch:
        c.start()

    def widen(e, count):
        for n in range(count):
            v = e_rows[e + n]
            e3[e + n, :128] = column_before(v)
            e3[e + n, 128:256] = v
            e3[e + n, 256:] = column_after(v)

    def scatter(s, count):
        for n in range(count):
            grads[s + n] = up(we3, e3, s + n)

    chunked(0, I + 2, I + 2, widen)
    fetch[0].wait()
    up_weights(we3, we, -1)
    chunked(0, I, U, scatter)
    for c in fetch[1:]:
        c.wait()


def partial_kernel(parts, partial):
    partial[...] = sum(parts[p].astype(F32) for p in range(parts.shape[0])).astype(BF16)


def total_kernel(own, other, wide):
    both = own[...].astype(F32) + other[...].astype(F32)
    for p in range(wide.shape[0]):
        wide[p] = both.astype(BF16)


PARTS = 2


def update_kernel(owner, totals, *refs):
    params, results, staged, sems = refs[:6], refs[-16:-6], refs[-6:-1], refs[-1]
    head = totals[0, :16].astype(F32)
    scale = 1.0 / head[:1]

    def half(n):
        copies, sent = [], 0
        for p, (lo, hi) in enumerate(chunk_runs(totals.shape[0])):
            if lo == hi:
                break
            grad = totals[p, HEAD : HEAD + hi - lo].astype(F32) * scale
            mom, ema, new = advance(grad, *[r[lo:hi] for r in params[3 * n : 3 * n + 3]])
            for ref, v in zip(staged, (grad, mom, ema, new, new.astype(BF16)), strict=True):
                ref[lo:hi] = v
            if hi == KERNEL_ROWS or (hi - sent >= KERNEL_ROWS // PARTS and hi % 16 == 0):
                for m in range(5):
                    c = pltpu.make_async_copy(staged[m].at[sent:hi], results[5 * n + m].at[sent:hi], sems.at[len(copies)])
                    c.start()
                    copies.append(c)
                sent = hi
        for c in copies:
            c.wait()

    core = lax.axis_index("core")
    pl.when(core == owner)(lambda: half(0))
    pl.when(core != owner)(lambda: half(1))


def own_update_kernel(R, totals, *refs):
    params, small, grads, bias_out, ig, rest, (field, merge_ref, sems), bias_ref, bias_sems = (
        refs[:6], refs[6:9], refs[9], refs[10:15], refs[15], refs[16:32], refs[32:35], refs[35:40], refs[40],
    )
    head = totals[0, :16].astype(F32)
    scale = 1.0 / head[:1]
    wide_scale = jnp.concatenate([scale] * 2, axis=1)
    merge_ref[...] = merge_matrix()
    grad = jnp.concatenate([head[1:2], head[2:3, :64]], axis=1) * scale[:, :1]
    mom, ema, new = advance(grad, *[r[...] for r in small])
    copies = []
    for n, v in enumerate((grad, mom, ema, new, new.astype(BF16).reshape(-1))):
        bias_ref[n][...] = v
        copies.append(pltpu.make_async_copy(bias_ref[n], bias_out[n], bias_sems.at[n]))
        copies[-1].start()
    copies += merge_field(R, lambda s: (grads[s] * wide_scale).astype(BF16), merge_ref[...], field, ig, sems)
    update_kernel(0, totals, *params, *rest)
    for c in copies:
        c.wait()


def advance(grad, weight, moment, average):
    moment_new = MOMENTUM * moment + grad
    weight_new = weight - LEARN_RATE * (grad + MOMENTUM * moment_new)
    average_new = EMA_DECAY * average + (1.0 - EMA_DECAY) * weight_new
    return (moment_new, average_new, weight_new)


def on_device(
    snapshots, cotangent, lengths, slot_mask, encoder_kernel, decoder_kernel, biases,
    encoder_mom, decoder_mom, bias_mom, encoder_ema, decoder_ema, bias_ema,
):
    slots, R, C, W = snapshots.shape
    latent_ch = encoder_kernel.shape[3]
    I, U = R // 2, 16
    nx = lax.axis_size("x")
    peers = lax.axis_size("snap") * nx
    swap = [(0, 1), (1, 0)]
    decoder_t = jnp.swapaxes(decoder_kernel, 2, 3)
    vmem, hbm = (pl.BlockSpec(memory_space=m) for m in (pltpu.VMEM, pltpu.HBM))

    def call(kernel, name, megabytes, flops, **kw):
        return pl.pallas_call(
            kernel,
            name=name,
            compiler_params=pltpu.CompilerParams(vmem_limit_bytes=megabytes * 2**20),
            cost_estimate=pl.CostEstimate(flops=flops, bytes_accessed=4 << 20, transcendentals=0),
            **kw,
        )

    def sds(*shape, dtype=BF16):
        return jax.ShapeDtypeStruct(shape, dtype)

    def in_vmem(v):
        return pltpu.with_memory_space_constraint(v, pltpu.VMEM)

    def in_hbm(v):
        return pltpu.with_memory_space_constraint(v, pltpu.HBM)

    conv = 2 * 4096 * 204800
    halo = sds(slots, XH + CH, C, W)
    near, far = call(
        functools.partial(halo_kernel, R), "halo", 4, 0,
        out_shape=[halo, halo],
        in_specs=[hbm] * 2,
        out_specs=[vmem] * 2,
        scratch_shapes=[pltpu.SemaphoreType.DMA((4,))],
    )(in_hbm(snapshots), in_hbm(cotangent))
    far = lax.ppermute(far, ("snap", "x", "core"), far_pairs(lax.axis_size("snap"), nx))
    near = lax.ppermute(near, "core", swap)
    bias_row = biases.reshape(1, -1)

    field = pltpu.HBM(snapshots.shape, BF16)
    state = [
        sds(XU + R + 8, 320, 256), sds(I + 6, 384, 256), sds(I + 2, 128, 256, dtype=F32), sds(R + 8, 320, 256),
        sds(I, 256, 256), sds(I + 4, 256, 256), sds(64, 256, dtype=F32), sds(320, 384, dtype=F32), sds(320, 256, dtype=F32),
        sds(I + 2, 128, 256), sds(128, 256, dtype=F32),
    ]
    shared = [
        sds(128, KERNEL_ROWS), sds(256, 1152), sds(128, KERNEL_ROWS), sds(128, 256, dtype=F32), sds(256, 256, dtype=F32), sds(256, 256),
        sds(8, 256, dtype=F32),
    ]
    parts = call(
        functools.partial(inner_kernel, R, U), "inner", INNER_MB, 2 * conv,
        out_shape=state + shared,
        in_specs=[vmem] * 2 + [hbm] * 2 + [vmem] * 3,
        out_specs=[vmem] * 18,
        scratch_shapes=[
            pltpu.VMEM(encoder_kernel.shape, F32),
            pltpu.VMEM(encoder_kernel.shape, F32),
            pltpu.SemaphoreType.DMA((2,)),
        ],
    )(in_vmem(snapshots), in_vmem(cotangent), in_hbm(encoder_kernel), in_hbm(decoder_t), bias_row, lengths.reshape(1, 1), slot_mask.reshape(1, slots))
    chunk = sds(peers, HEAD + chunk_span(peers), 128)
    keep, send, _, _, _, _, value, _, _, _, _, e_rows, _ = call(
        functools.partial(outer_kernel, R), "outer", OUTER_MB, 4 * conv,
        out_shape=[chunk, chunk] + state,
        in_specs=[vmem] * 20,
        out_specs=[vmem] * 13,
        input_output_aliases={9 + n: 2 + n for n in range(11)},
        scratch_shapes=[pltpu.VMEM((320, 384), F32), pltpu.VMEM((320, 256), F32)],
    )(far, near, *parts[11:], *parts[:11])

    recv = lax.ppermute(send, "core", swap)
    output = call(
        functools.partial(output_kernel, R), "output", FIELD_MB, conv // 4,
        out_shape=field,
        in_specs=[vmem],
        out_specs=hbm,
        scratch_shapes=[pltpu.VMEM(snapshots.shape, BF16), pltpu.VMEM((256, 256), BF16), pltpu.SemaphoreType.DMA((4,))],
    )(value)
    part = (keep.astype(F32) + recv.astype(F32)).astype(BF16)
    part, output = lax.optimization_barrier((part, output))
    parts = lax.all_to_all(part, ("snap", "x"), 0, 0, tiled=True)
    parts, e_rows = lax.optimization_barrier((parts, e_rows))
    own_side = call(partial_kernel, "partial", 4, 0, out_shape=sds(*part.shape[1:]), in_specs=[vmem], out_specs=vmem)(parts)
    other_side = lax.ppermute(own_side, "side", swap)

    def rows(v):
        return v.reshape(KERNEL_ROWS, 128)

    def trows(v):
        return jnp.swapaxes(v, 2, 3).reshape(KERNEL_ROWS, 128)

    params = [
        rows(encoder_kernel), rows(encoder_mom), rows(encoder_ema),
        trows(decoder_kernel), trows(decoder_mom), trows(decoder_ema),
    ]
    shape = (KERNEL_ROWS, 128)
    grads, *params = call(
        functools.partial(scatter_kernel, R, U), "scatter", FIELD_MB, conv,
        out_shape=[sds(I, 256, 256, dtype=F32)] + [sds(*shape, dtype=F32)] * 6,
        in_specs=[vmem] + [hbm] * 7,
        out_specs=[vmem] * 7,
        scratch_shapes=[
            pltpu.VMEM(encoder_kernel.shape, F32),
            pltpu.VMEM((I + 2, 384, 256), BF16),
            pltpu.VMEM((256, 1152), BF16),
            pltpu.SemaphoreType.DMA((7,)),
        ],
    )(e_rows, in_hbm(encoder_kernel), *[in_hbm(v) for v in params])
    other_side, grads, params = lax.optimization_barrier((other_side, grads, params))
    wide = call(total_kernel, "total", 4, 0, out_shape=sds(*part.shape), in_specs=[vmem] * 2, out_specs=vmem)(own_side, other_side)
    mine = lax.all_to_all(wide, ("snap", "x"), 0, 0, tiled=True)
    mine, grads, params = lax.optimization_barrier((mine, grads, params))
    other = lax.ppermute(mine, "core", swap)
    five = [pltpu.HBM(shape, F32)] * 4 + [pltpu.HBM(shape, BF16)]
    staged = [pltpu.VMEM(v.shape, v.dtype) for v in five] + [pltpu.SemaphoreType.DMA((5 * PARTS,))]
    bias_shape = [pltpu.HBM((1, latent_ch + C), F32)] * 4 + [pltpu.HBM((latent_ch + C,), BF16)]
    own = call(
        functools.partial(own_update_kernel, R), "update_own", UPDATE_MB, 1 << 20,
        out_shape=bias_shape + [field] + five * 2,
        in_specs=[vmem] * 11,
        out_specs=[hbm] * 16,
        scratch_shapes=staged
        + [pltpu.VMEM(snapshots.shape, BF16), pltpu.VMEM((256, 256), BF16), pltpu.SemaphoreType.DMA((4,))]
        + [pltpu.VMEM(v.shape, v.dtype) for v in bias_shape]
        + [pltpu.SemaphoreType.DMA((5,))],
    )(mine, *params, bias_row, bias_mom.reshape(1, -1), bias_ema.reshape(1, -1), grads)
    bias_results, input_grad, begun = own[:5], own[5], own[6:]
    bias_grad, bia_mom, bia_ema, bia_new, bia_copy = [v.reshape(biases.shape) for v in bias_results]
    results = call(
        functools.partial(update_kernel, 1), "update_other", UPDATE_MB, 1 << 20,
        out_shape=five * 2,
        in_specs=[vmem] * 7 + [hbm] * 10,
        out_specs=[hbm] * 10,
        input_output_aliases={7 + n: n for n in range(10)},
        scratch_shapes=staged,
    )(other, *params, *[in_hbm(v) for v in begun])
    enc_grad, enc_mom, enc_ema, enc_new, enc_copy = [v.reshape(encoder_kernel.shape) for v in results[:5]]
    dec_grad, dec_mom, dec_ema, dec_new, dec_copy = [jnp.swapaxes(v.reshape(decoder_t.shape), 2, 3) for v in results[5:]]
    return (
        output, input_grad, enc_grad, dec_grad, bias_grad, enc_mom, dec_mom, bia_mom,
        enc_ema, dec_ema, bia_ema, enc_new, dec_new, bia_new, enc_copy, dec_copy, bia_copy,
    )


def solution(mesh):
    snap, rows = mesh.devices.shape
    split = Mesh(mesh.devices.reshape(2, snap // 2, rows // 2, 2), ("side", "snap", "x", "core"))
    slots = ("side", "snap")
    field = P(slots, ("x", "core"), None, None)
    return jax.shard_map(
        on_device,
        mesh=split,
        in_specs=(field, field, P(slots), P(slots)) + (P(),) * 9,
        out_specs=(field, field) + (P(),) * 15,
        check_vma=False,
    )
```

```python
import functools

import jax
import jax.numpy as jnp
from jax import lax
from jax.experimental import pallas as pl
from jax.experimental.pallas import tpu as pltpu
from jax.sharding import Mesh, PartitionSpec as P

MOMENTUM = 0.5
EMA_DECAY = 0.5
LEARN_RATE = 0.01
F32, BF16 = jnp.float32, jnp.bfloat16
XH, CH = 8, 4
XU, XD = 8, 7
NT = (((1,), (1,)), ((), ()))
KERNEL_ROWS = 1600
INNER_MB, OUTER_MB, FIELD_MB, UPDATE_MB = 8, 8, 12, 16


HEAD = 8


def chunk_span(peers):
    return -(-KERNEL_ROWS // (8 * peers)) * 8


def chunk_runs(peers):
    span = chunk_span(peers)
    return [(min(KERNEL_ROWS, p * span), min(KERNEL_ROWS, (p + 1) * span)) for p in range(peers)]


def dot(a, b):
    return jnp.dot(a, b, preferred_element_type=F32)


def chunked(lo, hi, size, step):
    whole = (hi - lo) // size
    if whole == 1:
        step(lo, size)
    elif whole:
        pl.loop(0, whole)(lambda n: step(lo + n * size, size))
    rest = (hi - lo) % size
    if rest:
        step(hi - rest, rest)


def split_matrix():
    row = lax.broadcasted_iota(jnp.int32, (256, 256), 0)
    col = lax.broadcasted_iota(jnp.int32, (256, 256), 1)
    want = (col // 64 % 2) * 128 + (col % 64) * 2 + col // 128
    return jnp.where(row == want, 1.0, 0.0).astype(BF16)


def merge_matrix():
    row = lax.broadcasted_iota(jnp.int32, (256, 256), 0)
    col = lax.broadcasted_iota(jnp.int32, (256, 256), 1)
    want = (row // 64 % 2) * 128 + (row % 64) * 2 + row // 128
    return jnp.where(col == want, 1.0, 0.0).astype(BF16)


def column_before(v):
    return shifted(v, 1, 0)


def column_after(v):
    return shifted(v, 127, 63)


def shifted(v, by, edge):
    parts = []
    for h in range(v.shape[1] // 128):
        part = v[:, h * 128 : (h + 1) * 128]
        lane = lax.broadcasted_iota(jnp.int32, part.shape, 1) % 64
        parts.append(jnp.where(lane == edge, jnp.zeros_like(part), pltpu.roll(part, by, axis=1)))
    return parts[0] if len(parts) == 1 else jnp.concatenate(parts, axis=1)


def split_rows(rows, split):
    pieces = [jnp.concatenate([row(2 * h), row(2 * h + 1)], axis=1) for row in rows for h in range(2)]
    y = dot(jnp.concatenate(pieces, axis=0), split)
    out = []
    for n in range(len(rows)):
        a, b = y[n * 128 : n * 128 + 64], y[n * 128 + 64 : n * 128 + 128]
        out.append([jnp.concatenate([a[:, p * 128 : p * 128 + 128], b[:, p * 128 : p * 128 + 128]], axis=1) for p in range(2)])
    return out


def merge_rows(v, merge):
    pieces = [
        jnp.concatenate([v[rho * 128 : rho * 128 + 64, h * 128 : h * 128 + 128], v[rho * 128 + 64 : rho * 128 + 128, h * 128 : h * 128 + 128]], axis=1)
        for rho in range(2)
        for h in range(2)
    ]
    y = dot(jnp.concatenate(pieces, axis=0), merge).astype(BF16)
    return [
        [y[(rho * 2 + n // 2) * 64 : (rho * 2 + n // 2) * 64 + 64, (n % 2) * 128 : (n % 2) * 128 + 128] for n in range(4)]
        for rho in range(2)
    ]


def up_weights(dest, taps, sign):
    for rho in range(2):
        for pi in range(2):
            for di in range(-1, 2):
                for dj in range(-1, 2):
                    a, b = 2 + sign * (2 * di - rho), 2 + sign * (2 * dj - pi)
                    inside = 0 <= a <= 4 and 0 <= b <= 4
                    block = taps[a, b].astype(BF16) if inside else jnp.zeros((64, 128), BF16)
                    r, c = (rho * 2 + pi) * 64, ((di + 1) * 3 + dj + 1) * 128
                    dest[r : r + 64, c : c + 128] = block


def lane_sums(v):
    ones = jnp.ones((8, v.shape[1]), F32)
    return lax.dot_general(ones, v, NT, precision=lax.Precision.HIGHEST, preferred_element_type=F32)[:1]


def store_columns(xb, at, halves):
    even, odd = [v.astype(BF16) for v in halves]
    for b, v in enumerate([column_before(even), column_before(odd), even, odd, column_after(even)]):
        xb[at, b * 64 : b * 64 + 64] = v


def store_split(seeds, at, pair, live_lane):
    for rho, halves in enumerate(pair):
        for pi, v in enumerate(halves):
            row = (rho * 2 + pi) * 64
            seeds[at, row : row + 64] = (v * live_lane).astype(BF16)


def up(weights, rows, at):
    even = dot(weights[:128], rows[pl.ds(at, 3)].reshape(9 * 128, 256))
    odd = dot(weights[128:, 384:], rows[pl.ds(at + 1, 2)].reshape(6 * 128, 256))
    return jnp.concatenate([even, odd], axis=0)


def encode_row(u, I, ends, we2, bias, xb, l3, slope):
    pre = dot(we2[...], xb[pl.ds(2 * u, 5)].reshape(KERNEL_ROWS, 256)) + bias
    grow = jnp.exp(jnp.minimum(pre, 0.0))
    lat = jnp.maximum(pre, grow - 1.0)
    if ends is not None:
        if u < 3:
            lat = jnp.where(ends[0], 0.0, lat)
        if u >= I + 3:
            lat = jnp.where(ends[1], 0.0, lat)
    if ends is None or 2 <= u < I + 4:
        slope[u - 2] = grow
    lat = lat.astype(BF16)
    l3[u, :128] = column_before(lat)
    l3[u, 128:256] = lat
    l3[u, 256:] = column_after(lat)


def decode_row(w, own, wd2, bias, seeds, l3, d5, value, dsum):
    pre = up(wd2, l3, w) + bias
    grow = jnp.exp(jnp.minimum(pre, 0.0))
    if own:
        value[w - 2] = jnp.maximum(pre, grow - 1.0).astype(BF16)
    full = seeds[w].astype(F32) * grow
    if own:
        dsum[...] += (full[:64] + full[64:128]) + (full[128:192] + full[192:])
    back = full.astype(BF16)
    for rho in range(2):
        even, odd = [back[(rho * 2 + pi) * 64 : (rho * 2 + pi) * 64 + 64] for pi in range(2)]
        for b, v in enumerate([column_after(even), odd, even, column_before(odd), column_before(even)]):
            d5[2 * w + rho, b * 64 : b * 64 + 64] = v


def back_row(e, own, wb, d5, slope, e_rows, esum, outside=None):
    v = dot(wb[...], d5[pl.ds(2 * e, 5)].reshape(KERNEL_ROWS, 256)) * slope[e]
    if own:
        esum[...] += v
    else:
        v = jnp.where(outside, 0.0, v)
    e_rows[e] = v.astype(BF16)


def live_lanes(lens, mask):
    lane = lax.broadcasted_iota(jnp.int32, (1, 256), 1)
    length, valid = jnp.broadcast_to(lens, (1, 256)), jnp.zeros((1, 256), jnp.int32)
    for n in range(4):
        valid = jnp.where(lane // 64 == n, jnp.broadcast_to(mask[:, n : n + 1], (1, 256)), valid)
    return jnp.where((lane // 64 < length) & (valid > 0), 1.0, 0.0)


def bias_tiles(bias):
    def column(row):
        count = row.shape[1]
        at = lax.broadcasted_iota(jnp.int32, (count, count), 0)
        to = lax.broadcasted_iota(jnp.int32, (count, count), 1)
        return jnp.sum(jnp.where(at == to, jnp.broadcast_to(row, (count, count)), 0.0), axis=1, keepdims=True)

    enc = column(bias[:, :128])
    dec = column(bias[:, 128:])
    return jnp.broadcast_to(enc, (128, 256)), jnp.broadcast_to(jnp.concatenate([dec] * 4, axis=0), (256, 256))


def far_pairs(groups, nx):
    pairs = []
    for g in range(groups):
        base = g * 2 * nx
        for n in range(nx - 1):
            a, b = base + 2 * n + 1, base + 2 * n + 2
            pairs += [(a, b), (b, a)]
        other = g ^ 1
        if other < groups:
            pairs += [(base, other * 2 * nx), (base + 2 * nx - 1, (other + 1) * 2 * nx - 1)]
    return pairs


def halo_kernel(R, x_hbm, c_hbm, near, far, sems):
    core = lax.axis_index("core")
    copies = []
    for n, (dest, low) in enumerate(((near, core == 0), (far, core == 1))):
        for m, (src, rows, at) in enumerate(((x_hbm, XH, 0), (c_hbm, CH, XH))):
            start = jnp.where(low, R - rows, 0)
            copies.append(pltpu.make_async_copy(src.at[:, pl.ds(start, rows)], dest.at[:, at : at + rows], sems.at[2 * n + m]))
    for c in copies:
        c.start()
    for c in copies:
        c.wait()


def kernel_grad(rows, cols, cols_at, latent, latent_at):
    rhs = jnp.concatenate(
        [jnp.concatenate([latent(latent_at + s + d) for d in range(3)], axis=0) for s in rows], axis=1
    )
    even, odd = [jnp.concatenate([cols[cols_at + 2 * s + rho] for s in rows], axis=1) for rho in range(2)]
    return (
        lax.dot_general(even, rhs, NT, preferred_element_type=F32),
        lax.dot_general(odd, rhs[128:], NT, preferred_element_type=F32),
    )


def inner_kernel(
    R, U, xv, cv, we_hbm, wdt_hbm, bias, lens, mask,
    xb, l3, slope, d5, value, seeds, dsum, acc0, acc1, e_rows, esum, we2, wd2, wb, bias_enc, bias_dec, split_ref, live, we, wdt, sems,
):
    I = R // 2
    copies = [pltpu.make_async_copy(a, b, sems.at[n]) for n, (a, b) in enumerate(((we_hbm, we), (wdt_hbm, wdt)))]
    for c in copies:
        c.start()
    split_ref[...] = split_matrix()
    dsum[...] = jnp.zeros_like(dsum)
    live_lane = live_lanes(lens[...], mask[...])
    live[...] = jnp.broadcast_to(live_lane, live.shape)
    bias_enc[...], bias_dec[...] = bias_tiles(bias[...])
    esum[...] = jnp.zeros_like(esum)

    def columns(t, count):
        rows = [lambda s, r=t + m: xv[s, r] for m in range(count)]
        for n, halves in enumerate(split_rows(rows, split_ref[...])):
            store_columns(xb, XU + t + n, halves)

    def cotangent(s, count):
        rows = [lambda k, r=2 * s + m: cv[k, r] for m in range(2 * count)]
        halves = split_rows(rows, split_ref[...])
        for n in range(count):
            store_split(seeds, s + n + 2, halves[2 * n : 2 * n + 2], live_lane)

    def encode(u, count):
        for n in range(count):
            encode_row(u + n, I, None, we2, bias_enc[...], xb, l3, slope)

    def decode(w, count):
        for n in range(count):
            decode_row(w + n, True, wd2, bias_dec[...], seeds, l3, d5, value, dsum)

    columns(0, R)
    copies[0].wait()
    we2[...] = we[...].reshape(KERNEL_ROWS, 128).T.astype(BF16)
    chunked(4, I + 2, U, encode)
    copies[1].wait()
    up_weights(wd2, wdt, 1)
    chunked(0, I, U, cotangent)
    chunked(4, I, U, decode)
    wb[...] = jnp.concatenate([wdt[4 - q].reshape(320, 128) for q in range(5)], axis=0).T.astype(BF16)
    acc0[...], acc1[...] = kernel_grad(range(2, I - 2), d5, CH, lambda u: l3[u, 128:256], 2)
    for e in range(4, I - 2):
        back_row(e, True, wb, d5, slope, e_rows, esum)


def outer_kernel(
    R, far, near, we2, wd2, wb, bias_enc, bias_dec, split_ref, live,
    xb_in, l3_in, slope_in, d5_in, value_in, seeds_in, dsum_in, dec0_in, dec1_in, e_rows_in, esum_in,
    keep, send, xb, l3, slope, d5, value, seeds, dsum, dec0, dec1, e_rows, esum, enc0, enc1,
):
    I = R // 2
    core = lax.axis_index("core")
    row_at = lax.axis_index("x") * 2 + core
    ends = row_at == 0, row_at == lax.axis_size("x") * 2 - 1
    live_lane = live[:1]
    count = sum(live_lane[:, n * 64 : n * 64 + 1] for n in range(4))
    upper = core == 0

    def above(r):
        return lambda s: jnp.where(ends[0], jnp.zeros((64, 128), BF16), jnp.where(upper, far[s, r], near[s, r]))

    def below(r):
        return lambda s: jnp.where(ends[1], jnp.zeros((64, 128), BF16), jnp.where(upper, near[s, r], far[s, r]))

    def encoder_grad(rows):
        return kernel_grad(rows, xb, XU, lambda e: e_rows[e], 0)

    rows = [above(r) for r in range(XU)] + [below(r) for r in range(XD)]
    for n, halves in enumerate(split_rows(rows, split_ref[...])):
        store_columns(xb, n if n < XU else R + n, halves)
    halves = split_rows([above(XH + r) for r in range(CH)] + [below(XH + r) for r in range(CH)], split_ref[...])
    for n, w in enumerate((0, 1, I + 2, I + 3)):
        store_split(seeds, w, halves[2 * n : 2 * n + 2], live_lane)
    for u in list(range(4)) + list(range(I + 2, I + 6)):
        encode_row(u, I, ends, we2, bias_enc[...], xb, l3, slope)
    ready = range(4, I - 4)
    if ready:
        enc0[...], enc1[...] = encoder_grad(ready)
    for w in list(range(4)) + list(range(I, I + 4)):
        decode_row(w, 2 <= w < I + 2, wd2, bias_dec[...], seeds, l3, d5, value, dsum)
    even, odd = kernel_grad([0, 1, I - 2, I - 1], d5, CH, lambda u: l3[u, 128:256], 2)
    dec0[...] += even
    dec1[...] += odd
    for e in list(range(4)) + list(range(I - 2, I + 2)):
        back_row(e, 1 <= e < I + 1, wb, d5, slope, e_rows, esum, ends[0] if e == 0 else ends[1])
    even, odd = encoder_grad([s for s in range(I) if s not in ready])
    if ready:
        enc0[...] += even
        enc1[...] += odd
    else:
        enc0[...], enc1[...] = even, odd

    count_row = jnp.broadcast_to(jnp.where(row_at == 0, count, 0.0), (1, 128))
    dec_row = jnp.concatenate([lane_sums(dsum[...]), jnp.zeros((1, 64), F32)], axis=1)
    head = jnp.concatenate([count_row, lane_sums(esum[...]), dec_row, jnp.zeros((HEAD - 3, 128), F32)], axis=0).astype(BF16)
    other_head = jnp.concatenate([count_row, jnp.zeros((HEAD - 1, 128), F32)], axis=0).astype(BF16)
    chunks, chunk_rows = keep.shape[:2]

    def fill(dest, even_acc, odd_acc, even_taps, odd_taps):
        blocks = [(a, even_acc, d) for d, a in enumerate(even_taps)] + [(a, odd_acc, d) for d, a in enumerate(odd_taps)]
        runs = chunk_runs(chunks)
        for a, acc, d in blocks:
            block = acc[:, d * 128 : d * 128 + 128]
            for p, (start, end) in enumerate(runs):
                lo, hi = max(start, a * 320), min(end, a * 320 + 320)
                if lo < hi:
                    dest[p, HEAD + lo - start : HEAD + hi - start] = block[lo - a * 320 : hi - a * 320].astype(BF16)
        for p, (start, end) in enumerate(runs):
            dest[p, :HEAD] = other_head if p else head
            if HEAD + end - start < chunk_rows:
                dest[p, HEAD + end - start :] = jnp.zeros((chunk_rows - HEAD - end + start, 128), BF16)

    def fill_both(enc_dest, dec_dest):
        fill(enc_dest, enc0, enc1, (4, 2, 0), (3, 1))
        fill(dec_dest, dec0, dec1, (0, 2, 4), (1, 3))

    pl.when(core == 0)(lambda: fill_both(keep, send))
    pl.when(core != 0)(lambda: fill_both(send, keep))


def field_copies(R, field, out, sems):
    step = R // 4
    return [pltpu.make_async_copy(field.at[:, n * step : n * step + step], out.at[:, n * step : n * step + step], sems.at[n]) for n in range(4)]


def merge_field(R, value, merge, field, out, sems):
    I = R // 2
    copies = field_copies(R, field, out, sems)
    for n, c in enumerate(copies):
        for s in range(n * I // 4, (n + 1) * I // 4):
            for rho, slots in enumerate(merge_rows(value(s), merge)):
                for k, piece in enumerate(slots):
                    field[k, 2 * s + rho] = piece
        c.start()
    return copies


def output_kernel(R, value, out, field, merge_ref, sems):
    merge_ref[...] = merge_matrix()
    for c in merge_field(R, lambda s: value[s], merge_ref[...], field, out, sems):
        c.wait()


def scatter_kernel(R, U, e_rows, we_hbm, *refs):
    sources, grads, targets, (we, e3, we3, sems) = refs[:6], refs[6], refs[7:13], refs[13:]
    I = R // 2
    fetch = [pltpu.make_async_copy(we_hbm, we, sems.at[6])]
    fetch += [pltpu.make_async_copy(a, b, sems.at[n]) for n, (a, b) in enumerate(zip(sources, targets, strict=True))]
    for c in fetch:
        c.start()

    def widen(e, count):
        for n in range(count):
            v = e_rows[e + n]
            e3[e + n, :128] = column_before(v)
            e3[e + n, 128:256] = v
            e3[e + n, 256:] = column_after(v)

    def scatter(s, count):
        for n in range(count):
            grads[s + n] = up(we3, e3, s + n)

    chunked(0, I + 2, I + 2, widen)
    fetch[0].wait()
    up_weights(we3, we, -1)
    chunked(0, I, U, scatter)
    for c in fetch[1:]:
        c.wait()


def partial_kernel(parts, partial):
    partial[...] = sum(parts[p].astype(F32) for p in range(parts.shape[0])).astype(BF16)


def total_kernel(own, other, wide):
    both = own[...].astype(F32) + other[...].astype(F32)
    for p in range(wide.shape[0]):
        wide[p] = both.astype(BF16)


PARTS = 2


def update_kernel(owner, totals, *refs):
    params, results, staged, sems = refs[:6], refs[-16:-6], refs[-6:-1], refs[-1]
    head = totals[0, :16].astype(F32)
    scale = 1.0 / head[:1]

    def half(n):
        copies, sent = [], 0
        for p, (lo, hi) in enumerate(chunk_runs(totals.shape[0])):
            if lo == hi:
                break
            grad = totals[p, HEAD : HEAD + hi - lo].astype(F32) * scale
            mom, ema, new = advance(grad, *[r[lo:hi] for r in params[3 * n : 3 * n + 3]])
            for ref, v in zip(staged, (grad, mom, ema, new, new.astype(BF16)), strict=True):
                ref[lo:hi] = v
            if hi == KERNEL_ROWS or (hi - sent >= KERNEL_ROWS // PARTS and hi % 16 == 0):
                for m in range(5):
                    c = pltpu.make_async_copy(staged[m].at[sent:hi], results[5 * n + m].at[sent:hi], sems.at[len(copies)])
                    c.start()
                    copies.append(c)
                sent = hi
        for c in copies:
            c.wait()

    core = lax.axis_index("core")
    pl.when(core == owner)(lambda: half(0))
    pl.when(core != owner)(lambda: half(1))


def own_update_kernel(R, totals, *refs):
    params, small, grads, bias_out, ig, rest, (field, merge_ref, sems), bias_ref, bias_sems = (
        refs[:6], refs[6:9], refs[9], refs[10:15], refs[15], refs[16:32], refs[32:35], refs[35:40], refs[40],
    )
    head = totals[0, :16].astype(F32)
    scale = 1.0 / head[:1]
    wide_scale = jnp.concatenate([scale] * 2, axis=1)
    merge_ref[...] = merge_matrix()
    grad = jnp.concatenate([head[1:2], head[2:3, :64]], axis=1) * scale[:, :1]
    mom, ema, new = advance(grad, *[r[...] for r in small])
    copies = []
    for n, v in enumerate((grad, mom, ema, new, new.astype(BF16).reshape(-1))):
        bias_ref[n][...] = v
        copies.append(pltpu.make_async_copy(bias_ref[n], bias_out[n], bias_sems.at[n]))
        copies[-1].start()
    copies += merge_field(R, lambda s: (grads[s] * wide_scale).astype(BF16), merge_ref[...], field, ig, sems)
    update_kernel(0, totals, *params, *rest)
    for c in copies:
        c.wait()


def advance(grad, weight, moment, average):
    moment_new = MOMENTUM * moment + grad
    weight_new = weight - LEARN_RATE * (grad + MOMENTUM * moment_new)
    average_new = EMA_DECAY * average + (1.0 - EMA_DECAY) * weight_new
    return (moment_new, average_new, weight_new)


def on_device(
    snapshots, cotangent, lengths, slot_mask, encoder_kernel, decoder_kernel, biases,
    encoder_mom, decoder_mom, bias_mom, encoder_ema, decoder_ema, bias_ema,
):
    slots, R, C, W = snapshots.shape
    latent_ch = encoder_kernel.shape[3]
    I, U = R // 2, 16
    nx = lax.axis_size("x")
    peers = lax.axis_size("snap") * nx
    swap = [(0, 1), (1, 0)]
    decoder_t = jnp.swapaxes(decoder_kernel, 2, 3)
    vmem, hbm = (pl.BlockSpec(memory_space=m) for m in (pltpu.VMEM, pltpu.HBM))

    def call(kernel, name, megabytes, flops, **kw):
        return pl.pallas_call(
            kernel,
            name=name,
            compiler_params=pltpu.CompilerParams(vmem_limit_bytes=megabytes * 2**20),
            cost_estimate=pl.CostEstimate(flops=flops, bytes_accessed=4 << 20, transcendentals=0),
            **kw,
        )

    def sds(*shape, dtype=BF16):
        return jax.ShapeDtypeStruct(shape, dtype)

    def in_vmem(v):
        return pltpu.with_memory_space_constraint(v, pltpu.VMEM)

    def in_hbm(v):
        return pltpu.with_memory_space_constraint(v, pltpu.HBM)

    conv = 2 * 4096 * 204800
    halo = sds(slots, XH + CH, C, W)
    near, far = call(
        functools.partial(halo_kernel, R), "halo", 4, 0,
        out_shape=[halo, halo],
        in_specs=[hbm] * 2,
        out_specs=[vmem] * 2,
        scratch_shapes=[pltpu.SemaphoreType.DMA((4,))],
    )(in_hbm(snapshots), in_hbm(cotangent))
    far = lax.ppermute(far, ("snap", "x", "core"), far_pairs(lax.axis_size("snap"), nx))
    near = lax.ppermute(near, "core", swap)
    bias_row = biases.reshape(1, -1)

    field = pltpu.HBM(snapshots.shape, BF16)
    state = [
        sds(XU + R + 8, 320, 256), sds(I + 6, 384, 256), sds(I + 2, 128, 256, dtype=F32), sds(R + 8, 320, 256),
        sds(I, 256, 256), sds(I + 4, 256, 256), sds(64, 256, dtype=F32), sds(320, 384, dtype=F32), sds(320, 256, dtype=F32),
        sds(I + 2, 128, 256), sds(128, 256, dtype=F32),
    ]
    shared = [
        sds(128, KERNEL_ROWS), sds(256, 1152), sds(128, KERNEL_ROWS), sds(128, 256, dtype=F32), sds(256, 256, dtype=F32), sds(256, 256),
        sds(8, 256, dtype=F32),
    ]
    parts = call(
        functools.partial(inner_kernel, R, U), "inner", INNER_MB, 2 * conv,
        out_shape=state + shared,
        in_specs=[vmem] * 2 + [hbm] * 2 + [vmem] * 3,
        out_specs=[vmem] * 18,
        scratch_shapes=[
            pltpu.VMEM(encoder_kernel.shape, F32),
            pltpu.VMEM(encoder_kernel.shape, F32),
            pltpu.SemaphoreType.DMA((2,)),
        ],
    )(in_vmem(snapshots), in_vmem(cotangent), in_hbm(encoder_kernel), in_hbm(decoder_t), bias_row, lengths.reshape(1, 1), slot_mask.reshape(1, slots))
    chunk = sds(peers, HEAD + chunk_span(peers), 128)
    keep, send, _, _, _, _, value, _, _, _, _, e_rows, _ = call(
        functools.partial(outer_kernel, R), "outer", OUTER_MB, 4 * conv,
        out_shape=[chunk, chunk] + state,
        in_specs=[vmem] * 20,
        out_specs=[vmem] * 13,
        input_output_aliases={9 + n: 2 + n for n in range(11)},
        scratch_shapes=[pltpu.VMEM((320, 384), F32), pltpu.VMEM((320, 256), F32)],
    )(far, near, *parts[11:], *parts[:11])

    recv = lax.ppermute(send, "core", swap)
    output = call(
        functools.partial(output_kernel, R), "output", FIELD_MB, conv // 4,
        out_shape=field,
        in_specs=[vmem],
        out_specs=hbm,
        scratch_shapes=[pltpu.VMEM(snapshots.shape, BF16), pltpu.VMEM((256, 256), BF16), pltpu.SemaphoreType.DMA((4,))],
    )(value)
    part = (keep.astype(F32) + recv.astype(F32)).astype(BF16)
    part, output = lax.optimization_barrier((part, output))
    parts = lax.all_to_all(part, ("snap", "x"), 0, 0, tiled=True)
    parts, e_rows = lax.optimization_barrier((parts, e_rows))
    own_side = call(partial_kernel, "partial", 4, 0, out_shape=sds(*part.shape[1:]), in_specs=[vmem], out_specs=vmem)(parts)
    other_side = lax.ppermute(own_side, "side", swap)

    def rows(v):
        return v.reshape(KERNEL_ROWS, 128)

    def trows(v):
        return jnp.swapaxes(v, 2, 3).reshape(KERNEL_ROWS, 128)

    params = [
        rows(encoder_kernel), rows(encoder_mom), rows(encoder_ema),
        trows(decoder_kernel), trows(decoder_mom), trows(decoder_ema),
    ]
    shape = (KERNEL_ROWS, 128)
    grads, *params = call(
        functools.partial(scatter_kernel, R, U), "scatter", FIELD_MB, conv,
        out_shape=[sds(I, 256, 256, dtype=F32)] + [sds(*shape, dtype=F32)] * 6,
        in_specs=[vmem] + [hbm] * 7,
        out_specs=[vmem] * 7,
        scratch_shapes=[
            pltpu.VMEM(encoder_kernel.shape, F32),
            pltpu.VMEM((I + 2, 384, 256), BF16),
            pltpu.VMEM((256, 1152), BF16),
            pltpu.SemaphoreType.DMA((7,)),
        ],
    )(e_rows, in_hbm(encoder_kernel), *[in_hbm(v) for v in params])
    other_side, grads, params = lax.optimization_barrier((other_side, grads, params))
    wide = call(total_kernel, "total", 4, 0, out_shape=sds(*part.shape), in_specs=[vmem] * 2, out_specs=vmem)(own_side, other_side)
    mine = lax.all_to_all(wide, ("snap", "x"), 0, 0, tiled=True)
    mine, grads, params = lax.optimization_barrier((mine, grads, params))
    other = lax.ppermute(mine, "core", swap)
    five = [pltpu.HBM(shape, F32)] * 4 + [pltpu.HBM(shape, BF16)]
    staged = [pltpu.VMEM(v.shape, v.dtype) for v in five] + [pltpu.SemaphoreType.DMA((5 * PARTS,))]
    bias_shape = [pltpu.HBM((1, latent_ch + C), F32)] * 4 + [pltpu.HBM((latent_ch + C,), BF16)]
    own = call(
        functools.partial(own_update_kernel, R), "update_own", UPDATE_MB, 1 << 20,
        out_shape=bias_shape + [field] + five * 2,
        in_specs=[vmem] * 11,
        out_specs=[hbm] * 16,
        scratch_shapes=staged
        + [pltpu.VMEM(snapshots.shape, BF16), pltpu.VMEM((256, 256), BF16), pltpu.SemaphoreType.DMA((4,))]
        + [pltpu.VMEM(v.shape, v.dtype) for v in bias_shape]
        + [pltpu.SemaphoreType.DMA((5,))],
    )(mine, *params, bias_row, bias_mom.reshape(1, -1), bias_ema.reshape(1, -1), grads)
    bias_results, input_grad, begun = own[:5], own[5], own[6:]
    bias_grad, bia_mom, bia_ema, bia_new, bia_copy = [v.reshape(biases.shape) for v in bias_results]
    results = call(
        functools.partial(update_kernel, 1), "update_other", UPDATE_MB, 1 << 20,
        out_shape=five * 2,
        in_specs=[vmem] * 7 + [hbm] * 10,
        out_specs=[hbm] * 10,
        input_output_aliases={7 + n: n for n in range(10)},
        scratch_shapes=staged,
    )(other, *params, *[in_hbm(v) for v in begun])
    enc_grad, enc_mom, enc_ema, enc_new, enc_copy = [v.reshape(encoder_kernel.shape) for v in results[:5]]
    dec_grad, dec_mom, dec_ema, dec_new, dec_copy = [jnp.swapaxes(v.reshape(decoder_t.shape), 2, 3) for v in results[5:]]
    return (
        output, input_grad, enc_grad, dec_grad, bias_grad, enc_mom, dec_mom, bia_mom,
        enc_ema, dec_ema, bia_ema, enc_new, dec_new, bia_new, enc_copy, dec_copy, bia_copy,
    )


def solution(mesh):
    snap, rows = mesh.devices.shape
    split = Mesh(mesh.devices.reshape(2, snap // 2, rows // 2, 2), ("side", "snap", "x", "core"))
    slots = ("side", "snap")
    field = P(slots, ("x", "core"), None, None)
    return jax.shard_map(
        on_device,
        mesh=split,
        in_specs=(field, field, P(slots), P(slots)) + (P(),) * 9,
        out_specs=(field, field) + (P(),) * 15,
        check_vma=False,
    )
```
